128 devices in a mesh: gx: 8 (over x, core), gy: 16 (over z, y).
Axes of the slice: x: 4, y: 4, z: 4, core: 2. Of those that a mesh axis runs over, the one named last changes fastest.
Arguments:
- thermal_departure: float32 [40, 512, 4096], P(None, 'gx', 'gy'), may hold values from -6 to 6
- current_speeds: float32 [2, 40, 512, 4096], P(None, None, 'gx', 'gy'), may hold values from -3 to 3
- mixing_coefficient: float32 [40, 512, 4096], P(None, 'gx', 'gy'), may hold values from 0.1 to 10
- seawater_indicator: int32 [512, 4096], P('gx', 'gy'), may hold values 0 or 1
- submerged_layer_tally: int32 [512, 4096], P('gx', 'gy'), may hold values from 1 to 40
- rainfall_runoff_input: float32 [512, 4096], P('gx', 'gy'), may hold values from -6 to 6
Outputs:
- temperature_next: float32 [40, 512, 4096], P(None, 'gx', 'gy')
- velocity_next: float32 [2, 40, 512, 4096], P(None, None, 'gx', 'gy')
- surface_pressure: float32 [512, 4096], P('gx', 'gy')
The draws below stay inside these ranges and needn't reach their ends.
All inputs are finite; a program needn't handle non-finite values. No bound on the sum of `seawater_indicator` on one device may be relied on, other than what follows from the above.
Results may differ from the reference program's by a relative error of at most 0.0003.
Values sent between devices are 32-bit elements; how exact they have to be, the bound alone decides.
No kernel may reach another device: no remote copies, remote signals or barrier semaphores. Data moves between devices by JAX's collectives and lax.ppermute only.
A program may use at most 128 MiB of HBM per device.

```python
import math
import jax
import jax.numpy as jnp
from jax import lax

DEPTH_LAYERS = 40
ITERS = 6
PARALLEL_POINTS = 512
MERIDIAN_POINTS = 4096


def with_ends(array, rng, smallest, largest):
    extent = array.shape
    index_at = [jax.random.randint(jax.random.fold_in(rng, axis), (), 0, extent[axis]) for axis in range(len(extent))]
    array = array.at[tuple(index_at)].set(smallest)
    longest = extent.index(max(extent))
    index_at[longest] = (index_at[longest] + 1) % extent[longest]
    return array.at[tuple(index_at)].set(largest)


def shard_levels(key, shape, pieces, smallest, top_value):
    def one(axis_at, shards_of):
        steps = jax.random.uniform(jax.random.fold_in(jax.random.fold_in(key, 6), axis_at), (shards_of,), jnp.float32, smallest / len(pieces), top_value / len(pieces))
        return jnp.repeat(jnp.exp(steps), shape[axis_at] // shards_of).reshape((-1,) + (1,) * (len(shape) - axis_at - 1))

    factor_of = one(*pieces[0])
    for cut in pieces[1:]:
        factor_of = factor_of * one(*cut)
    return factor_of


def bell_draw(key, extent, width, bound, shards=(), kind=jnp.bfloat16):
    values = width * jax.random.normal(key, extent, jnp.float32)
    if shards:
        values = values * shard_levels(key, extent, shards, -0.22, 0.18)
    return jnp.clip(values, -bound, bound).astype(kind)


def setup_inputs(seed: int = 0) -> dict:
    arg_keys = jax.random.split(jax.random.key(seed), 7)
    thermal_departure = bell_draw(arg_keys[0], (DEPTH_LAYERS, PARALLEL_POINTS, MERIDIAN_POINTS), 1.0, 6.0, ((1, 8), (2, 16)), jnp.float32)
    current_speeds = bell_draw(arg_keys[1], (2, DEPTH_LAYERS, PARALLEL_POINTS, MERIDIAN_POINTS), 0.5, 3.0, ((2, 8), (3, 16)), jnp.float32)
    mixing_coefficient = jnp.clip(jnp.exp(math.log(10.0) - 4.6051702 * jax.random.uniform(arg_keys[2], (DEPTH_LAYERS, PARALLEL_POINTS, MERIDIAN_POINTS), jnp.float32) ** shard_levels(arg_keys[2], (DEPTH_LAYERS, PARALLEL_POINTS, MERIDIAN_POINTS), ((1, 8), (2, 16)), -0.2, 0.2)), 0.1, 10.0)
    seawater_indicator = with_ends((jax.random.randint(arg_keys[3], (PARALLEL_POINTS, MERIDIAN_POINTS), 0, 4) < 3).astype(jnp.int32), jax.random.fold_in(arg_keys[3], 1), 0, 1)
    submerged_layer_tally = with_ends(jax.random.randint(arg_keys[4], (PARALLEL_POINTS, MERIDIAN_POINTS), 1, DEPTH_LAYERS + 1), jax.random.fold_in(arg_keys[4], 1), 1, DEPTH_LAYERS).astype(jnp.int32)
    rainfall_runoff_input = bell_draw(arg_keys[5], (PARALLEL_POINTS, MERIDIAN_POINTS), 1.0, 6.0, ((0, 8), (1, 16)), jnp.float32)
    return {"thermal_departure": thermal_departure, "current_speeds": current_speeds, "mixing_coefficient": mixing_coefficient, "seawater_indicator": seawater_indicator, "submerged_layer_tally": submerged_layer_tally, "rainfall_runoff_input": rainfall_runoff_input}


damping = 0.05
lower_bound = 0.02
upper_bound = 2.0
cheb_alpha = 2.0 / (upper_bound - lower_bound)
cheb_gamma = (upper_bound + lower_bound) / 2.0
advect_scale = 0.4
force_scale = 4.0
source_scale = 0.5
divergence_scale = 4.0

def neighbor_total(padded):
    edges = padded[..., 2:, 1:-1] + padded[..., :-2, 1:-1] + padded[..., 1:-1, 2:] + padded[..., 1:-1, :-2]
    corners = padded[..., 2:, 2:] + padded[..., 2:, :-2] + padded[..., :-2, 2:] + padded[..., :-2, :-2]
    return edges + 0.5 * corners

def vertical_mix(source, coupling):
    count = source.shape[0]
    zeros = jnp.zeros_like(source[0])
    above = [zeros] + [coupling[level] for level in range(1, count)]
    below = above[1:] + [zeros]
    factors = []
    values = []
    for level in range(count):
        denominator = 1.0 + above[level] + below[level]
        numerator = source[level]
        if level > 0:
            denominator = denominator - above[level] * factors[-1]
            numerator = numerator + above[level] * values[-1]
        values.append(numerator / denominator)
        factors.append(below[level] / denominator)
    result = [values[-1]]
    for level in range(count - 2, -1, -1):
        result.append(values[level] + factors[level] * result[-1])
    return jnp.stack(result[::-1])

def tracer_update(extended):
    temp_ext = extended[0]
    east_vel = extended[1]
    north_vel = extended[2]
    wet_ext = (extended[3] > 0).astype(jnp.float32)
    east_open = wet_ext[:, :-1, 1:-1] * wet_ext[:, 1:, 1:-1] * east_vel[:, :-1, 1:-1]
    north_open = wet_ext[:, 1:-1, :-1] * wet_ext[:, 1:-1, 1:] * north_vel[:, 1:-1, :-1]
    flux_east = jnp.maximum(east_open, 0.0) * temp_ext[:, :-1, 1:-1] + jnp.minimum(east_open, 0.0) * temp_ext[:, 1:, 1:-1]
    flux_north = jnp.maximum(north_open, 0.0) * temp_ext[:, 1:-1, :-1] + jnp.minimum(north_open, 0.0) * temp_ext[:, 1:-1, 1:]
    convergence = flux_east[:, 1:] - flux_east[:, :-1] + flux_north[:, :, 1:] - flux_north[:, :, :-1]
    provisional = temp_ext[:, 1:-1, 1:-1] - advect_scale * wet_ext[:, 1:-1, 1:-1] * convergence
    temp_next = vertical_mix(provisional, extended[3][:, 1:-1, 1:-1])
    buoyancy = -temp_next
    pressure = (jnp.cumsum(buoyancy, axis=0) - 0.5 * buoyancy) / temp_next.shape[0]
    return (temp_next, pressure)

def momentum_update(extended, press_ext, ocean, rainfall_runoff_input):
    east_vel = extended[1]
    north_vel = extended[2]
    wet_ext = (extended[3] > 0).astype(jnp.float32)
    east_full = wet_ext[:, :-1, 1:-1] * wet_ext[:, 1:, 1:-1] * (east_vel[:, :-1, 1:-1] + force_scale * (press_ext[:, :-1, 1:-1] - press_ext[:, 1:, 1:-1]))
    north_full = wet_ext[:, 1:-1, :-1] * wet_ext[:, 1:-1, 1:] * (north_vel[:, 1:-1, :-1] + force_scale * (press_ext[:, 1:-1, :-1] - press_ext[:, 1:-1, 1:]))
    velocity_next = jnp.stack([east_full[:, 1:], north_full[:, :, 1:]])
    east_total = lax.optimization_barrier(jnp.sum(east_full, axis=0)) / east_full.shape[0]
    north_total = lax.optimization_barrier(jnp.sum(north_full, axis=0)) / north_full.shape[0]
    divergence = east_total[1:] - east_total[:-1] + north_total[:, 1:] - north_total[:, :-1]
    forcing = ocean * (source_scale * rainfall_runoff_input - divergence_scale * divergence)
    return (velocity_next, forcing)

def chebyshev(forcing, depth_root, total_fn):
    diag = damping + depth_root * total_fn(depth_root)
    inverse = 1.0 / diag
    update = inverse * forcing / cheb_gamma
    iterate = update
    omega = 2.0 / cheb_gamma
    for step in range(1, ITERS):
        residual = forcing - (diag * iterate - depth_root * total_fn(depth_root * iterate))
        omega = 1.0 / (cheb_gamma - omega / (4.0 * cheb_alpha * cheb_alpha))
        update = omega * inverse * residual + (cheb_gamma * omega - 1.0) * update
        iterate = iterate + update
    return iterate

def wrap_pad(field):
    widths = [(0, 0)] * (field.ndim - 2) + [(1, 1), (1, 1)]
    return jnp.pad(field, widths, mode='wrap')

def reference(thermal_departure, current_speeds, mixing_coefficient, seawater_indicator, submerged_layer_tally, rainfall_runoff_input):
    latitude = jnp.arange(MERIDIAN_POINTS)
    inner = (latitude > 0) & (latitude < MERIDIAN_POINTS - 1)
    ocean_int = jnp.where(inner[None, :], seawater_indicator, 0)
    ocean = ocean_int.astype(jnp.float32)
    levels = jnp.arange(DEPTH_LAYERS)[:, None, None]
    submerged_indicator = ((levels < submerged_layer_tally[None]) & (ocean_int[None] == 1)).astype(jnp.float32)
    joined_quantities = jnp.stack([thermal_departure, current_speeds[0], current_speeds[1], mixing_coefficient * submerged_indicator])
    extended = wrap_pad(joined_quantities)
    temp_next, pressure = tracer_update(extended)
    velocity_next, forcing = momentum_update(extended, wrap_pad(pressure), ocean, rainfall_runoff_input)
    depth_root = jnp.sqrt((submerged_layer_tally * ocean_int).astype(jnp.float32) / DEPTH_LAYERS)

    def total_fn(field):
        return neighbor_total(wrap_pad(field))
    surface = chebyshev(forcing, depth_root, total_fn)
    return (temp_next, velocity_next, surface)
```

```python
import jax
import jax.numpy as jnp
from jax import lax
from jax.experimental import pallas as pl
from jax.experimental.pallas import tpu as pltpu
from jax.sharding import PartitionSpec as P

ITERS = 6
LEVELS = 40
ROWS = 64
COLS = 256
BLOCKS = ROWS // 8
CHUNK = 8
CHUNKS = LEVELS // CHUNK

damping = 0.05
lower_bound = 0.02
upper_bound = 2.0
cheb_alpha = 2.0 / (upper_bound - lower_bound)
cheb_gamma = (upper_bound + lower_bound) / 2.0
advect_scale = 0.4
force_scale = 4.0
source_scale = 0.5
divergence_scale = 4.0
PRESS = force_scale / LEVELS
DIVERGE = divergence_scale / LEVELS

VMEM = pl.BlockSpec(memory_space=pltpu.VMEM)
ANY = pl.BlockSpec(memory_space=pl.ANY)
SMEM = pl.BlockSpec(memory_space=pltpu.SMEM)
F32 = jnp.float32
TILES = [(b, h) for b in range(BLOCKS) for h in range(2)]


def shape(*dims):
    return jax.ShapeDtypeStruct(dims, F32)


def params():
    return pltpu.CompilerParams(vmem_limit_bytes=40 * 1024 * 1024)


def lane_id(rows=8):
    return lax.broadcasted_iota(jnp.int32, (rows, 128), 1)


def row_id():
    return lax.broadcasted_iota(jnp.int32, (8, 128), 0)


def rows_of(b):
    return slice(8 * b, 8 * b + 8)


def lanes_of(h):
    return slice(128 * h, 128 * h + 128)


def tiles_of(ref, *lead):
    return {(b, h): ref[(*lead, rows_of(b), lanes_of(h))] for b, h in TILES}


def next_row(x, after, last):
    turned = {t: pltpu.roll(x[t], 7, 0) for t in TILES}
    return {
        (b, h): jnp.where(last, after[h] if b == BLOCKS - 1 else turned[b + 1, h], turned[b, h])
        for b, h in TILES
    }


def prev_row(x, before, first):
    turned = {t: pltpu.roll(x[t], 1, 0) for t in TILES}
    return {
        (b, h): jnp.where(first, before[h] if b == 0 else turned[b - 1, h], turned[b, h])
        for b, h in TILES
    }


def next_col(x, after, last):
    turned = {t: pltpu.roll(x[t], 127, 1) for t in TILES}
    return {
        (b, h): jnp.where(last, after[b] if h == 1 else turned[b, 1], turned[b, h])
        for b, h in TILES
    }


def prev_col(x, before, first):
    turned = {t: pltpu.roll(x[t], 1, 1) for t in TILES}
    return {
        (b, h): jnp.where(first, before[b] if h == 0 else turned[b, 0], turned[b, h])
        for b, h in TILES
    }


def spread(ref, k, h):
    return jnp.broadcast_to(ref[h, pl.ds(k, 1), :], (8, 128))


def pack_kernel(
    tile_y, temp, speeds, sea, tally,
    count_out, to_east, to_west, to_north, to_south,
    t_low, t_high, v_high, t_top, t_end, u_end, sems,
):
    copies = [
        pltpu.make_async_copy(temp.at[:, :, pl.ds(0, 128)], t_low, sems.at[0]),
        pltpu.make_async_copy(temp.at[:, :, pl.ds(128, 128)], t_high, sems.at[1]),
        pltpu.make_async_copy(speeds.at[1, :, :, pl.ds(128, 128)], v_high, sems.at[2]),
        pltpu.make_async_copy(temp.at[:, pl.ds(0, 8), :], t_top, sems.at[3]),
        pltpu.make_async_copy(temp.at[:, pl.ds(ROWS - 8, 8), :], t_end, sems.at[4]),
        pltpu.make_async_copy(speeds.at[0, :, pl.ds(ROWS - 8, 8), :], u_end, sems.at[5]),
    ]
    for copy in copies:
        copy.start()
    latitude = tile_y[0] * COLS + lax.broadcasted_iota(jnp.int32, (ROWS, COLS), 1)
    inner = (latitude > 0) & (latitude < tile_y[1] - 1)
    count = jnp.where(inner & (sea[...] == 1), tally[...], 0).astype(F32)
    count_out[...] = count
    for h in range(2):
        to_east[h, 80:86, :] = count[ROWS - 6 :, lanes_of(h)]
        to_east[h, 86:88, :] = jnp.zeros((2, 128), F32)
        to_west[h, 40:46, :] = count[:6, lanes_of(h)]
        to_west[h, 46:48, :] = jnp.zeros((2, 128), F32)
    lane = lane_id(ROWS)

    def gather(ref, column, start, total):
        for k in range(LEVELS):
            total = jnp.where(
                lane == start + k, pltpu.roll(ref[k], (start + k - column) % 128, 1), total
            )
        return total

    copies[0].wait()
    to_south[...] = gather(
        t_low, 0, 0, pltpu.roll(count[:, :128], 40, 1)
    )
    copies[1].wait()
    total = gather(t_high, 127, 0, pltpu.roll(count[:, 128:], (80 - 127) % 128, 1))
    copies[2].wait()
    to_north[...] = gather(v_high, 127, 40, total)
    copies[3].wait()
    copies[4].wait()
    copies[5].wait()
    for h in range(2):
        to_west[h, 0:40, :] = t_top[:, 0, lanes_of(h)]
        to_east[h, 0:40, :] = t_end[:, 7, lanes_of(h)]
        to_east[h, 40:80, :] = u_end[:, 7, lanes_of(h)]


def pack(tile_y, temp, speeds, sea, tally):
    return pl.pallas_call(
        pack_kernel,
        out_shape=(
            shape(ROWS, COLS), shape(2, 88, 128), shape(2, 48, 128), shape(ROWS, 128), shape(ROWS, 128)
        ),
        in_specs=[SMEM, ANY, ANY, VMEM, VMEM],
        out_specs=(VMEM,) * 5,
        scratch_shapes=[
            pltpu.VMEM((LEVELS, ROWS, 128), F32),
            pltpu.VMEM((LEVELS, ROWS, 128), F32),
            pltpu.VMEM((LEVELS, ROWS, 128), F32),
            pltpu.VMEM((LEVELS, 8, COLS), F32),
            pltpu.VMEM((LEVELS, 8, COLS), F32),
            pltpu.VMEM((LEVELS, 8, COLS), F32),
            pltpu.SemaphoreType.DMA((6,)),
        ],
        compiler_params=params(),
        name="pack",
    )(tile_y, temp, speeds, sea, tally)


def column_kernel(
    temp, speeds, mix, count, rain, west, east_in, south, north_in,
    temp_out, speeds_out, force_out, to_east, to_west, q_row, q_col, sides,
    tb, ub, vb, mb, east_lim, north_lim, south_lim, west_lim, run, in_sems, out_sems,
):
    def load(which, c):
        part = pl.ds(c * CHUNK, CHUNK)
        source, target = (
            (mix, mb), (temp, tb), (speeds.at[0], ub), (speeds.at[1], vb)
        )[which]
        return pltpu.make_async_copy(source.at[part], target.at[part], in_sems.at[which, c])

    def store(which, c):
        part = pl.ds(c * CHUNK, CHUNK)
        source, target = (
            (tb, temp_out), (ub, speeds_out.at[0]), (vb, speeds_out.at[1])
        )[which]
        return pltpu.make_async_copy(source.at[part], target.at[part], out_sems.at[which, c])

    for c in range(CHUNKS):
        for which in range(4):
            load(which, c).start()

    lane = lane_id()
    row = row_id()
    first_row, last_row = row == 0, row == 7
    first_lane, last_lane = lane == 0, lane == 127

    counts = tiles_of(count)
    after = {h: jnp.broadcast_to(east_in[h, 40:41, :], (8, 128)) for h in range(2)}
    before = {h: jnp.broadcast_to(west[h, 85:86, :], (8, 128)) for h in range(2)}
    ahead = next_row(counts, after, last_row)
    for b, h in TILES:
        east_lim[rows_of(b), lanes_of(h)] = jnp.minimum(counts[b, h], ahead[b, h])
    for h in range(2):
        west_lim[:, lanes_of(h)] = jnp.minimum(counts[0, h], before[h])
    after = {b: pltpu.roll(north_in[rows_of(b), :], 127 - 40, 1) for b in range(BLOCKS)}
    ahead = next_col(counts, after, last_lane)
    for b, h in TILES:
        north_lim[rows_of(b), lanes_of(h)] = jnp.minimum(counts[b, h], ahead[b, h])
    for b in range(BLOCKS):
        south_lim[rows_of(b), :] = jnp.minimum(
            counts[b, 0], pltpu.roll(south[rows_of(b), :], 128 - 80, 1)
        )

    zero = jnp.zeros((8, 128), F32)

    def forward(k):
        level = k.astype(F32)
        masked = jnp.where(k == 0, F32(1e9), level)
        t = tiles_of(tb, k)
        u = tiles_of(ub, k)
        v = tiles_of(vb, k)
        wet = tiles_of(count)
        t_after = {h: spread(east_in, k, h) for h in range(2)}
        ahead = next_row(t, t_after, last_row)
        flux = {
            i: jnp.where(level < east_lim[rows_of(i[0]), lanes_of(i[1])], u[i], 0.0)
            * jnp.where(u[i] > 0.0, t[i], ahead[i])
            for i in TILES
        }
        edge = {}
        for h in range(2):
            speed = spread(west, k + 40, h)
            edge[h] = jnp.where(level < west_lim[:, lanes_of(h)], speed, 0.0) * jnp.where(
                speed > 0.0, spread(west, k, h), t[0, h]
            )
        behind = prev_row(flux, edge, first_row)
        change = {i: flux[i] - behind[i] for i in TILES}
        t_after = {b: pltpu.roll(north_in[rows_of(b), :], 127 - k, 1) for b in range(BLOCKS)}
        ahead = next_col(t, t_after, last_lane)
        flux = {
            i: jnp.where(level < north_lim[rows_of(i[0]), lanes_of(i[1])], v[i], 0.0)
            * jnp.where(v[i] > 0.0, t[i], ahead[i])
            for i in TILES
        }
        edge = {}
        for b in range(BLOCKS):
            held = south[rows_of(b), :]
            speed = pltpu.roll(held, 88 - k, 1)
            edge[b] = jnp.where(level < south_lim[rows_of(b), :], speed, 0.0) * jnp.where(
                speed > 0.0, pltpu.roll(held, 128 - k, 1), t[b, 0]
            )
        behind = prev_col(flux, edge, first_lane)
        below_at = jnp.minimum(k + 1, LEVELS - 1)
        above_at = jnp.maximum(k - 1, 0)
        for i in TILES:
            at = (rows_of(i[0]), lanes_of(i[1]))
            total = change[i] + (flux[i] - behind[i])
            source = t[i] - jnp.where(level < wet[i], advect_scale * total, 0.0)
            a = jnp.where(masked < wet[i], mb[(k, *at)], 0.0)
            below = jnp.where(level + 1.0 < wet[i], mb[(below_at, *at)], 0.0)
            factor = mb[(above_at, *at)]
            value = tb[(above_at, *at)]
            pivot = (1.0 + below) + (a - a * factor)
            inverse = pl.reciprocal(pivot, approx=True)
            inverse = inverse * (2.0 - pivot * inverse)
            tb[(k, *at)] = (source + a * value) * inverse
            mb[(k, *at)] = below * inverse

    load(0, 0).wait()

    def forward_chunk(c, _):
        @pl.when(c < CHUNKS - 1)
        def _():
            load(0, c + 1).wait()

        for which in range(1, 4):
            load(which, c).wait()

        def step(k, _):
            forward(k)
            return 0

        return lax.fori_loop(c * CHUNK, (c + 1) * CHUNK, step, 0)

    lax.fori_loop(0, CHUNKS, forward_chunk, 0)

    def back_chunk(c_up, x):
        c = CHUNKS - 1 - c_up

        def step(n, x):
            k = c * CHUNK + (CHUNK - 1 - n)
            out = []
            for i, below in zip(TILES, x):
                at = (k, rows_of(i[0]), lanes_of(i[1]))
                value = tb[at] + mb[at] * below
                tb[at] = value
                out.append(value)
            return tuple(out)

        x = lax.fori_loop(0, CHUNK, step, x)
        store(0, c).start()
        return x

    lax.fori_loop(0, CHUNKS, back_chunk, tuple(zero for _ in TILES))

    run[...] = jnp.zeros_like(run)
    q_col[...] = jnp.zeros_like(q_col)

    def momentum(k, carry):
        level = k.astype(F32)
        east_sum, north_sum, row_sum, col_sum = carry
        q = {}
        for i in TILES:
            at = (rows_of(i[0]), lanes_of(i[1]))
            half = 0.5 * tb[(k, *at)]
            q[i] = run[at] + half
            run[at] = q[i] + half
        for h in range(2):
            q_row[h, pl.ds(k, 1), :] = q[0, h][0:1]
        ahead = next_row(q, {h: zero for h in range(2)}, last_row)
        east_new = []
        for i, total in zip(TILES, east_sum):
            at = (rows_of(i[0]), lanes_of(i[1]))
            speed = jnp.where(
                level < east_lim[at], ub[(k, *at)] - PRESS * (q[i] - ahead[i]), 0.0
            )
            ub[(k, *at)] = speed
            east_new.append(total + speed)
        ahead = next_col(q, {b: zero for b in range(BLOCKS)}, last_lane)
        north_new = []
        for i, total in zip(TILES, north_sum):
            at = (rows_of(i[0]), lanes_of(i[1]))
            speed = jnp.where(
                level < north_lim[at], vb[(k, *at)] - PRESS * (q[i] - ahead[i]), 0.0
            )
            vb[(k, *at)] = speed
            north_new.append(total + speed)
        row_new = tuple(
            row_sum[h] + jnp.where(level < west_lim[:, lanes_of(h)], PRESS * q[0, h], 0.0)
            for h in range(2)
        )
        col_new = []
        for b in range(BLOCKS):
            col_new.append(
                col_sum[b] + jnp.where(level < south_lim[rows_of(b), :], PRESS * q[b, 0], 0.0)
            )
            q_col[rows_of(b), :] = jnp.where(
                lane == k, pltpu.roll(q[b, 0], k, 1), q_col[rows_of(b), :]
            )
        return tuple(east_new), tuple(north_new), row_new, tuple(col_new)

    def momentum_chunk(c, carry):
        carry = lax.fori_loop(c * CHUNK, (c + 1) * CHUNK, momentum, carry)
        store(1, c).start()
        store(2, c).start()
        return carry

    blank = tuple(zero for _ in TILES)
    east_sum, north_sum, row_sum, col_sum = lax.fori_loop(
        0, CHUNKS, momentum_chunk, (blank, blank, (zero, zero), (zero,) * BLOCKS)
    )

    east_sum = dict(zip(TILES, east_sum))
    north_sum = dict(zip(TILES, north_sum))
    east_before = prev_row(east_sum, row_sum, first_row)
    north_before = prev_col(north_sum, col_sum, first_lane)
    for i in TILES:
        at = (rows_of(i[0]), lanes_of(i[1]))
        divergence = (east_sum[i] - east_before[i]) + (north_sum[i] - north_before[i])
        force_out[at] = jnp.where(
            count[at] > 0.0, source_scale * rain[at] - DIVERGE * divergence, 0.0
        )
    for b in range(BLOCKS):
        sides[rows_of(b), :] = jnp.where(
            first_lane,
            pltpu.roll(north_sum[b, 1], 1, 1),
            jnp.where(last_lane, pltpu.roll(col_sum[b], 127, 1), 0.0),
        )
    to_east[0:8, 0:COLS] = pltpu.roll(force_out[ROWS - 8 : ROWS, :], 5, 0)
    to_east[0:8, COLS:] = pltpu.roll(sides[ROWS - 8 : ROWS, :], 5, 0)
    to_west[0:8, 0:COLS] = force_out[0:8, :]
    to_west[0:8, COLS:] = sides[0:8, :]
    for h in range(2):
        to_east[5:6, lanes_of(h)] = east_sum[BLOCKS - 1, h][7:8]
        to_west[5:6, lanes_of(h)] = row_sum[h][0:1]

    for c in range(CHUNKS):
        for which in range(3):
            store(which, c).wait()


def columns(temp, speeds, mix, count, rain, west, east_in, south, north_in):
    block = pltpu.VMEM((LEVELS, ROWS, COLS), F32)
    return pl.pallas_call(
        column_kernel,
        out_shape=(
            shape(LEVELS, ROWS, COLS), shape(2, LEVELS, ROWS, COLS), shape(ROWS, COLS),
            shape(8, COLS + 128), shape(8, COLS + 128), shape(2, LEVELS, 128),
            shape(ROWS, 128), shape(ROWS, 128),
        ),
        in_specs=[ANY, ANY, ANY] + [VMEM] * 6,
        out_specs=(ANY, ANY) + (VMEM,) * 6,
        scratch_shapes=[
            block, block, block, block,
            pltpu.VMEM((ROWS, COLS), F32), pltpu.VMEM((ROWS, COLS), F32),
            pltpu.VMEM((ROWS, 128), F32), pltpu.VMEM((8, COLS), F32),
            pltpu.VMEM((ROWS, COLS), F32),
            pltpu.SemaphoreType.DMA((4, CHUNKS)), pltpu.SemaphoreType.DMA((3, CHUNKS)),
        ],
        compiler_params=params(),
        name="columns",
    )(temp, speeds, mix, count, rain, west, east_in, south, north_in)


def mend_kernel(
    speeds, q_row, q_col, count, east_in, north_in, speeds_out, rows, cols, sems
):
    row_part = (0, slice(None), pl.ds(ROWS - 8, 8), slice(None))
    col_part = (1, slice(None), slice(None), pl.ds(128, 128))
    load_rows = pltpu.make_async_copy(speeds.at[row_part], rows, sems.at[0])
    load_cols = pltpu.make_async_copy(speeds.at[col_part], cols, sems.at[1])
    load_rows.start()
    load_cols.start()
    last_row = row_id() == 7
    load_rows.wait()
    for h in range(2):
        limit = jnp.minimum(
            count[ROWS - 8 :, lanes_of(h)], jnp.broadcast_to(east_in[h, 40:41, :], (8, 128))
        )
        limit = jnp.where(last_row, limit, 0.0)
        for k in range(LEVELS):
            rows[k, :, lanes_of(h)] = rows[k, :, lanes_of(h)] + jnp.where(
                float(k) < limit, PRESS * spread(q_row, k, h), 0.0
            )
    save_rows = pltpu.make_async_copy(rows, speeds_out.at[row_part], sems.at[2])
    save_rows.start()
    last_lane = lane_id(ROWS) == 127
    limit = jnp.minimum(count[:, 128:], pltpu.roll(north_in[...], 127 - 40, 1))
    limit = jnp.where(last_lane, limit, 0.0)
    load_cols.wait()
    for k in range(LEVELS):
        cols[k] = cols[k] + jnp.where(
            float(k) < limit, PRESS * pltpu.roll(q_col[...], 127 - k, 1), 0.0
        )
    save_cols = pltpu.make_async_copy(cols, speeds_out.at[col_part], sems.at[3])
    save_cols.start()
    save_rows.wait()
    save_cols.wait()


def mend(speeds, q_row, q_col, count, east_in, north_in):
    return pl.pallas_call(
        mend_kernel,
        out_shape=shape(2, LEVELS, ROWS, COLS),
        in_specs=[ANY] + [VMEM] * 5,
        out_specs=ANY,
        scratch_shapes=[
            pltpu.VMEM((LEVELS, 8, COLS), F32),
            pltpu.VMEM((LEVELS, ROWS, 128), F32),
            pltpu.SemaphoreType.DMA((4,)),
        ],
        input_output_aliases={0: 0},
        compiler_params=params(),
        name="mend",
    )(speeds, q_row, q_col, count, east_in, north_in)


EXT = ROWS + 16


def edges_kernel(
    force, sides, count, west, east_in, own_east, own_west, from_west, from_east,
    force_ext, count_ext, sides_ext, to_north, to_south,
):
    zeros8 = jnp.zeros((8, COLS), F32)
    count_ext[0:8, :] = zeros8
    for h in range(2):
        count_ext[2:8, lanes_of(h)] = west[h, 80:86, :]
    count_ext[8 : 8 + ROWS, :] = count[...]
    count_ext[8 + ROWS :, :] = zeros8
    for h in range(2):
        count_ext[8 + ROWS : 14 + ROWS, lanes_of(h)] = east_in[h, 40:46, :]
    sides_ext[0:8, :] = jnp.zeros((8, 128), F32)
    sides_ext[3:8, :] = from_west[0:5, COLS:]
    sides_ext[8 : 8 + ROWS, :] = sides[...]
    sides_ext[8 + ROWS :, :] = jnp.zeros((8, 128), F32)
    sides_ext[8 + ROWS : 13 + ROWS, :] = from_east[0:5, COLS:]
    force_ext[0:8, :] = zeros8
    force_ext[3:8, :] = from_west[0:5, 0:COLS]
    force_ext[8 : 8 + ROWS, :] = force[...]
    force_ext[8 + ROWS :, :] = zeros8
    force_ext[8 + ROWS : 13 + ROWS, :] = from_east[0:5, 0:COLS]

    def add(at, amount):
        force_ext[at : at + 1, :] = force_ext[at : at + 1, :] + jnp.where(
            count_ext[at : at + 1, :] > 0.0, DIVERGE * amount, 0.0
        )

    add(7, -own_west[5:6, 0:COLS])
    add(8, from_west[5:6, 0:COLS])
    add(7 + ROWS, -from_east[5:6, 0:COLS])
    add(8 + ROWS, own_east[5:6, 0:COLS])
    lane = lane_id(EXT)
    side = sides_ext[...]
    to_north[...] = jnp.where(
        lane >= 123,
        force_ext[:, 128:],
        jnp.where(lane == 0, side, pltpu.roll(count_ext[:, 128:], 122, 1)),
    )
    to_south[...] = jnp.where(
        lane < 5,
        force_ext[:, :128],
        jnp.where(lane == 127, side, pltpu.roll(count_ext[:, :128], 8, 1)),
    )


def edges(*args):
    return pl.pallas_call(
        edges_kernel,
        out_shape=(
            shape(EXT, COLS), shape(EXT, COLS), shape(EXT, 128), shape(EXT, 128), shape(EXT, 128)
        ),
        in_specs=[VMEM] * 9,
        out_specs=(VMEM,) * 5,
        compiler_params=params(),
        name="edges",
    )(*args)


def chebyshev_kernel(force_ext, count_ext, sides_ext, south, north, out):
    lane = lane_id(EXT)
    count_side = jnp.where(
        lane >= 122,
        pltpu.roll(south[...], 6, 1),
        jnp.where(lane < 6, pltpu.roll(north[...], 120, 1), 0.0),
    )
    force_side = jnp.where(
        lane >= 123, south[...], jnp.where(lane < 5, north[...], 0.0)
    )
    side = sides_ext[...]
    low, high = force_ext[:, :128], force_ext[:, 128:]
    low = low + jnp.where(
        (lane == 0) & (count_ext[:, :128] > 0.0), DIVERGE * south[...], 0.0
    )
    high = high - jnp.where(
        (lane == 127) & (count_ext[:, 128:] > 0.0), DIVERGE * north[...], 0.0
    )
    force_side = force_side + jnp.where(
        (lane == 0) & (count_side > 0.0), DIVERGE * side, 0.0
    )
    force_side = force_side - jnp.where(
        (lane == 127) & (count_side > 0.0), DIVERGE * side, 0.0
    )
    force = jnp.concatenate([low, high, force_side], axis=1)
    count = jnp.concatenate([count_ext[...], count_side], axis=1)
    root = jnp.sqrt(count * (1.0 / LEVELS))
    wide = COLS + 128

    def total(field):
        sideways = pltpu.roll(field, 1, 1) + pltpu.roll(field, wide - 1, 1)
        mixed = field + 0.5 * sideways
        return sideways + (pltpu.roll(mixed, 1, 0) + pltpu.roll(mixed, EXT - 1, 0))

    diag = damping + root * total(root)
    inverse = 1.0 / diag
    update = inverse * force * (1.0 / cheb_gamma)
    iterate = update
    omega = 2.0 / cheb_gamma
    for step in range(1, ITERS):
        residual = force - (diag * iterate - root * total(root * iterate))
        omega = 1.0 / (cheb_gamma - omega / (4.0 * cheb_alpha * cheb_alpha))
        update = omega * inverse * residual + (cheb_gamma * omega - 1.0) * update
        iterate = iterate + update
    out[...] = iterate[8 : 8 + ROWS, 0:COLS]


def chebyshev(*args):
    return pl.pallas_call(
        chebyshev_kernel,
        out_shape=shape(ROWS, COLS),
        in_specs=[VMEM] * 5,
        out_specs=VMEM,
        compiler_params=params(),
        name="chebyshev",
    )(*args)


def shift(array, axis, step):
    count = lax.axis_size(axis)
    return lax.ppermute(array, axis, [(i, (i + step) % count) for i in range(count)])


def local(
    thermal_departure,
    current_speeds,
    mixing_coefficient,
    seawater_indicator,
    submerged_layer_tally,
    rainfall_runoff_input,
):
    tile_y = jnp.stack(
        [lax.axis_index("gy"), jnp.int32(lax.axis_size("gy") * COLS)]
    ).astype(jnp.int32)
    count, to_east, to_west, to_north, to_south = pack(
        tile_y, thermal_departure, current_speeds,
        seawater_indicator, submerged_layer_tally,
    )
    south = shift(to_north, "gy", 1)
    north = shift(to_south, "gy", -1)
    west = shift(to_east, "gx", 1)
    east = shift(to_west, "gx", -1)
    temp_next, speeds, force, own_east, own_west, q_row, q_col, sides = columns(
        thermal_departure, current_speeds, mixing_coefficient, count,
        rainfall_runoff_input, west, east, south, north,
    )
    from_west = shift(own_east, "gx", 1)
    from_east = shift(own_west, "gx", -1)
    q_north = shift(q_col, "gy", -1)
    q_east = shift(q_row, "gx", -1)
    force_ext, count_ext, sides_ext, to_north, to_south = edges(
        force, sides, count, west, east, own_east, own_west, from_west, from_east
    )
    from_south = shift(to_north, "gy", 1)
    from_north = shift(to_south, "gy", -1)
    velocity_next = mend(speeds, q_east, q_north, count, east, north)
    surface = chebyshev(force_ext, count_ext, sides_ext, from_south, from_north)
    return (temp_next, velocity_next, surface)


def solution(mesh):
    placed = (
        P(None, "gx", "gy"),
        P(None, None, "gx", "gy"),
        P(None, "gx", "gy"),
        P("gx", "gy"),
        P("gx", "gy"),
        P("gx", "gy"),
    )
    return jax.shard_map(
        local,
        mesh=mesh,
        in_specs=placed,
        out_specs=(P(None, "gx", "gy"), P(None, None, "gx", "gy"), P("gx", "gy")),
        check_vma=False,
    )
```

```python
import jax
import jax.numpy as jnp
from jax import lax
from jax.experimental import pallas as pl
from jax.experimental.pallas import tpu as pltpu
from jax.sharding import PartitionSpec as P

ITERS = 6
LIMIT_PACK = 40
LIMIT_INTERIOR = 40
LIMIT_COLUMNS = 24
LEVELS = 40
ROWS = 64
COLS = 256
BLOCKS = ROWS // 8
CHUNK = 8
CHUNKS = LEVELS // CHUNK

damping = 0.05
lower_bound = 0.02
upper_bound = 2.0
cheb_alpha = 2.0 / (upper_bound - lower_bound)
cheb_gamma = (upper_bound + lower_bound) / 2.0
advect_scale = 0.4
force_scale = 4.0
source_scale = 0.5
divergence_scale = 4.0
PRESS = force_scale / LEVELS
DIVERGE = divergence_scale / LEVELS

VMEM = pl.BlockSpec(memory_space=pltpu.VMEM)
ANY = pl.BlockSpec(memory_space=pl.ANY)
HBM = pl.BlockSpec(memory_space=pltpu.HBM)
F32 = jnp.float32
TILES = [(b, h) for b in range(BLOCKS) for h in range(2)]


def shape(*dims):
    return jax.ShapeDtypeStruct(dims, F32)


def params(mebibytes=40):
    return pltpu.CompilerParams(vmem_limit_bytes=int(mebibytes * 1024 * 1024))


def lane_id(rows=8):
    return lax.broadcasted_iota(jnp.int32, (rows, 128), 1)


def row_id():
    return lax.broadcasted_iota(jnp.int32, (8, 128), 0)


def rows_of(b):
    return slice(8 * b, 8 * b + 8)


def lanes_of(h):
    return slice(128 * h, 128 * h + 128)


def tiles_of(ref, *lead):
    return {(b, h): ref[(*lead, rows_of(b), lanes_of(h))] for b, h in TILES}


def next_row(x, after, last):
    turned = {t: pltpu.roll(x[t], 7, 0) for t in TILES}
    return {
        (b, h): jnp.where(last, after[h] if b == BLOCKS - 1 else turned[b + 1, h], turned[b, h])
        for b, h in TILES
    }


def prev_row(x, before, first):
    turned = {t: pltpu.roll(x[t], 1, 0) for t in TILES}
    return {
        (b, h): jnp.where(first, before[h] if b == 0 else turned[b - 1, h], turned[b, h])
        for b, h in TILES
    }


def next_col(x, after, last):
    turned = {t: pltpu.roll(x[t], 127, 1) for t in TILES}
    return {
        (b, h): jnp.where(last, after[b] if h == 1 else turned[b, 1], turned[b, h])
        for b, h in TILES
    }


def prev_col(x, before, first):
    turned = {t: pltpu.roll(x[t], 1, 1) for t in TILES}
    return {
        (b, h): jnp.where(first, before[b] if h == 0 else turned[b, 0], turned[b, h])
        for b, h in TILES
    }


def spread(ref, k, h):
    return jnp.broadcast_to(ref[h, pl.ds(k, 1), :], (8, 128))


def pack_kernel(
    temp, speeds, sea_in, tally_in,
    count_out, to_east, to_west, to_north, to_south,
    t_low, t_high, v_high, t_top, t_end, u_end, sea, tally, sems,
):
    copies = [
        pltpu.make_async_copy(sea_in, sea, sems.at[6]),
        pltpu.make_async_copy(tally_in, tally, sems.at[7]),
        pltpu.make_async_copy(temp.at[:, :, pl.ds(0, 128)], t_low, sems.at[0]),
        pltpu.make_async_copy(temp.at[:, :, pl.ds(128, 128)], t_high, sems.at[1]),
        pltpu.make_async_copy(speeds.at[1, :, :, pl.ds(128, 128)], v_high, sems.at[2]),
        pltpu.make_async_copy(temp.at[:, pl.ds(0, 8), :], t_top, sems.at[3]),
        pltpu.make_async_copy(temp.at[:, pl.ds(ROWS - 8, 8), :], t_end, sems.at[4]),
        pltpu.make_async_copy(speeds.at[0, :, pl.ds(ROWS - 8, 8), :], u_end, sems.at[5]),
    ]
    for copy in copies:
        copy.start()
    copies[0].wait()
    copies[1].wait()
    copies = copies[2:]
    latitude = lax.axis_index("gy") * COLS + lax.broadcasted_iota(jnp.int32, (ROWS, COLS), 1)
    inner = (latitude > 0) & (latitude < lax.axis_size("gy") * COLS - 1)
    count = jnp.where(inner & (sea[...] == 1), tally[...], 0).astype(F32)
    count_out[...] = count
    for h in range(2):
        to_east[h, 80:86, :] = count[ROWS - 6 :, lanes_of(h)]
        to_east[h, 86:88, :] = jnp.zeros((2, 128), F32)
        to_west[h, 40:46, :] = count[:6, lanes_of(h)]
        to_west[h, 46:48, :] = jnp.zeros((2, 128), F32)
    lane = lane_id(ROWS)

    def gather(ref, column, start, total):
        for k in range(LEVELS):
            total = jnp.where(
                lane == start + k, pltpu.roll(ref[k], (start + k - column) % 128, 1), total
            )
        return total

    copies[0].wait()
    to_south[...] = gather(
        t_low, 0, 0, pltpu.roll(count[:, :128], 40, 1)
    )
    copies[1].wait()
    total = gather(t_high, 127, 0, pltpu.roll(count[:, 128:], (80 - 127) % 128, 1))
    copies[2].wait()
    to_north[...] = gather(v_high, 127, 40, total)
    copies[3].wait()
    copies[4].wait()
    copies[5].wait()
    for h in range(2):
        to_west[h, 0:40, :] = t_top[:, 0, lanes_of(h)]
        to_east[h, 0:40, :] = t_end[:, 7, lanes_of(h)]
        to_east[h, 40:80, :] = u_end[:, 7, lanes_of(h)]


def pack(temp, speeds, sea, tally):
    return pl.pallas_call(
        pack_kernel,
        out_shape=(
            shape(ROWS, COLS), shape(2, 88, 128), shape(2, 48, 128), shape(ROWS, 128), shape(ROWS, 128)
        ),
        in_specs=[HBM, HBM, HBM, HBM],
        out_specs=(VMEM,) * 5,
        scratch_shapes=[
            pltpu.VMEM((LEVELS, ROWS, 128), F32),
            pltpu.VMEM((LEVELS, ROWS, 128), F32),
            pltpu.VMEM((LEVELS, ROWS, 128), F32),
            pltpu.VMEM((LEVELS, 8, COLS), F32),
            pltpu.VMEM((LEVELS, 8, COLS), F32),
            pltpu.VMEM((LEVELS, 8, COLS), F32),
            pltpu.VMEM((ROWS, COLS), jnp.int32),
            pltpu.VMEM((ROWS, COLS), jnp.int32),
            pltpu.SemaphoreType.DMA((8,)),
        ],
        compiler_params=params(LIMIT_PACK),
        name="pack",
    )(temp, speeds, sea, tally)


UNROLL_IN = 2
UNROLL_FWD = 2
UNROLL_BACK = 4
UNROLL_MOM = 4


def interior_kernel(
    temp, speeds, mix, count,
    source_out, inverse_out, link_out, u_out, v_out,
    tb, mb, east_lim, north_lim, sems,
):
    def load(which, c):
        part = pl.ds(c * CHUNK, CHUNK)
        origin, target = (
            (mix, mb), (temp, tb), (speeds.at[0], u_out), (speeds.at[1], v_out)
        )[which]
        return pltpu.make_async_copy(origin.at[part], target.at[part], sems.at[which, c])

    for c in range(CHUNKS):
        for which in range(4):
            load(which, c).start()

    lane, row = lane_id(), row_id()
    first_row, last_row = row == 0, row == 7
    first_lane, last_lane = lane == 0, lane == 127
    zero = jnp.zeros((8, 128), F32)
    pair = range(2)

    counts = tiles_of(count)
    ahead = next_row(counts, [zero, zero], last_row)
    for b, h in TILES:
        east_lim[rows_of(b), lanes_of(h)] = jnp.minimum(counts[b, h], ahead[b, h])
    ahead = next_col(counts, [zero] * BLOCKS, last_lane)
    for b, h in TILES:
        north_lim[rows_of(b), lanes_of(h)] = jnp.minimum(counts[b, h], ahead[b, h])

    def level_step(k, factors, links):
        level = k.astype(F32)
        below_at = jnp.minimum(k + 1, LEVELS - 1)
        t_next = [tb[k, rows_of(0), lanes_of(h)] for h in pair]
        turned_next = [pltpu.roll(t_next[h], 7, 0) for h in pair]
        flux_turned = [zero, zero]
        new_factors, new_links = [], []
        for b in range(BLOCKS):
            rows = rows_of(b)
            t, turned = t_next, turned_next
            if b < BLOCKS - 1:
                t_next = [tb[k, rows_of(b + 1), lanes_of(h)] for h in pair]
                turned_next = [pltpu.roll(t_next[h], 7, 0) for h in pair]
            u = [u_out[k, rows, lanes_of(h)] for h in pair]
            v = [v_out[k, rows, lanes_of(h)] for h in pair]
            change = []
            for h in pair:
                ahead = jnp.where(last_row, turned_next[h], turned[h])
                flux = jnp.where(level < east_lim[rows, lanes_of(h)], u[h], 0.0) * jnp.where(
                    u[h] > 0.0, t[h], ahead
                )
                flux_before, flux_turned[h] = flux_turned[h], pltpu.roll(flux, 1, 0)
                change.append(flux - jnp.where(first_row, flux_before, flux_turned[h]))
            left = [pltpu.roll(t[h], 127, 1) for h in pair]
            ahead = [jnp.where(last_lane, left[1], left[0]), left[1]]
            flux = [
                jnp.where(level < north_lim[rows, lanes_of(h)], v[h], 0.0)
                * jnp.where(v[h] > 0.0, t[h], ahead[h])
                for h in pair
            ]
            right = [pltpu.roll(flux[h], 1, 1) for h in pair]
            behind = [jnp.where(first_lane, 0.0, right[0]), jnp.where(first_lane, right[0], right[1])]
            for h in pair:
                n = 2 * b + h
                at = (k, rows, lanes_of(h))
                wet = count[rows, lanes_of(h)]
                total = change[h] + (flux[h] - behind[h])
                source_out[at] = t[h] - jnp.where(level < wet, advect_scale * total, 0.0)
                a = links[n]
                below = jnp.where(
                    level + 1.0 < wet, mb[below_at, rows, lanes_of(h)], 0.0
                )
                pivot = (1.0 + below) + (a - a * factors[n])
                inverse = pl.reciprocal(pivot, approx=True)
                inverse = inverse * (2.0 - pivot * inverse)
                inverse_out[at] = inverse
                link_out[at] = a
                new_factors.append(below * inverse)
                new_links.append(below)
        return tuple(new_factors), tuple(new_links)

    load(0, 0).wait()

    def chunk_step(c, carry):
        @pl.when(c < CHUNKS - 1)
        def _():
            load(0, c + 1).wait()

        for which in range(1, 4):
            load(which, c).wait()

        def step(m, carry):
            for n in range(UNROLL_IN):
                carry = level_step(c * CHUNK + m * UNROLL_IN + n, *carry)
            return carry

        return lax.fori_loop(0, CHUNK // UNROLL_IN, step, carry)

    blank = tuple(zero for _ in TILES)
    lax.fori_loop(0, CHUNKS, chunk_step, (blank, blank))


def interior(temp, speeds, mix, count):
    block = shape(LEVELS, ROWS, COLS)
    scratch = pltpu.VMEM((LEVELS, ROWS, COLS), F32)
    return pl.pallas_call(
        interior_kernel,
        out_shape=(block,) * 5,
        in_specs=[ANY, ANY, ANY, VMEM],
        out_specs=(VMEM,) * 5,
        scratch_shapes=[
            scratch, scratch,
            pltpu.VMEM((ROWS, COLS), F32), pltpu.VMEM((ROWS, COLS), F32),
            pltpu.SemaphoreType.DMA((4, CHUNKS)),
        ],
        cost_estimate=pl.CostEstimate(
            flops=30 * LEVELS * ROWS * COLS, bytes_accessed=16 * LEVELS * ROWS * COLS,
            transcendentals=0,
        ),
        compiler_params=params(LIMIT_INTERIOR),
        name="interior",
    )(temp, speeds, mix, count)


def column_kernel(
    source, inverse, link, u_in, v_in, count, rain, own_east, own_west, own_north, own_south,
    west, east, south, north,
    temp_out, speeds_out, force_out, to_east, to_west, q_col, sides, u_end, v_high,
    solved, u_new, v_low, row_low, row_high, col_low, col_high,
    east_lim, north_lim, south_lim, west_lim, run, u_sum, v_sum, out_sems,
):
    def store(which, c):
        part = pl.ds(c * CHUNK, CHUNK)
        origin, target = (
            (solved.at[part], temp_out.at[part]),
            (u_new.at[part], speeds_out.at[0, part, pl.ds(0, ROWS - 8), :]),
            (v_low.at[part], speeds_out.at[1, part, :, pl.ds(0, 128)]),
        )[which]
        return pltpu.make_async_copy(origin, target, out_sems.at[which, c])

    lane, row = lane_id(), row_id()
    first_row, last_row = row == 0, row == 7
    first_lane, last_lane = lane == 0, lane == 127
    zero = jnp.zeros((8, 128), F32)
    pair = range(2)

    counts = tiles_of(count)
    after = [jnp.broadcast_to(east[h, 40:41, :], (8, 128)) for h in pair]
    before = [jnp.broadcast_to(west[h, 85:86, :], (8, 128)) for h in pair]
    ahead = next_row(counts, after, last_row)
    for b, h in TILES:
        east_lim[rows_of(b), lanes_of(h)] = jnp.minimum(counts[b, h], ahead[b, h])
    for h in pair:
        west_lim[:, lanes_of(h)] = jnp.minimum(counts[0, h], before[h])
    after = [pltpu.roll(north[rows_of(b), :], 127 - 40, 1) for b in range(BLOCKS)]
    ahead = next_col(counts, after, last_lane)
    for b, h in TILES:
        north_lim[rows_of(b), lanes_of(h)] = jnp.minimum(counts[b, h], ahead[b, h])
    for b in range(BLOCKS):
        south_lim[rows_of(b), :] = jnp.minimum(
            counts[b, 0], pltpu.roll(south[rows_of(b), :], 128 - 80, 1)
        )

    depth = lax.broadcasted_iota(jnp.int32, (LEVELS, 128), 0).astype(F32)
    for h in pair:
        speed = west[h, 40:80, :]
        row_low[h] = (
            advect_scale
            * jnp.where(depth < west_lim[0:1, lanes_of(h)], speed, 0.0)
            * jnp.where(speed > 0.0, west[h, 0:40, :], own_west[h, 0:40, :])
        )
        speed = own_east[h, 40:80, :]
        row_high[h] = (
            -advect_scale
            * jnp.where(depth < east_lim[ROWS - 1 : ROWS, lanes_of(h)], speed, 0.0)
            * jnp.where(speed > 0.0, own_east[h, 0:40, :], east[h, 0:40, :])
        )
    depth = lane.astype(F32)
    for b in range(BLOCKS):
        rows = rows_of(b)
        limit = jnp.broadcast_to(south_lim[rows, 0:1], (8, 128))
        speed = pltpu.roll(south[rows, :], 128 - 40, 1)
        col_low[rows, :] = (
            advect_scale
            * jnp.where(depth < limit, speed, 0.0)
            * jnp.where(speed > 0.0, south[rows, :], own_south[rows, :])
        )
        limit = jnp.broadcast_to(north_lim[rows, COLS - 1 : COLS], (8, 128))
        speed = pltpu.roll(own_north[rows, :], 128 - 40, 1)
        col_high[rows, :] = (
            -advect_scale
            * jnp.where(depth < limit, speed, 0.0)
            * jnp.where(speed > 0.0, own_north[rows, :], north[rows, :])
        )

    def forward(k, values):
        out = []
        low = [jnp.where(first_row, spread(row_low, k, h), 0.0) for h in pair]
        high = [jnp.where(last_row, spread(row_high, k, h), 0.0) for h in pair]
        for b in range(BLOCKS):
            rows = rows_of(b)
            add = [
                jnp.where(first_lane, pltpu.roll(col_low[rows, :], 128 - k, 1), 0.0),
                jnp.where(last_lane, pltpu.roll(col_high[rows, :], 127 - k, 1), 0.0),
            ]
            for h in pair:
                at = (k, rows, lanes_of(h))
                total = source[at] + add[h]
                if b == 0:
                    total = total + low[h]
                if b == BLOCKS - 1:
                    total = total + high[h]
                value = (total + link[at] * values[2 * b + h]) * inverse[at]
                solved[at] = value
                out.append(value)
        return tuple(out)

    blank = tuple(zero for _ in TILES)

    def forward_step(m, values):
        for n in range(UNROLL_FWD):
            values = forward(m * UNROLL_FWD + n, values)
        return values

    lax.fori_loop(0, LEVELS // UNROLL_FWD, forward_step, blank)

    def back_chunk(c_up, linked):
        c = CHUNKS - 1 - c_up

        def step(m, linked):
            for n in range(UNROLL_BACK):
                k = c * CHUNK + (CHUNK - 1 - m * UNROLL_BACK - n)
                out = []
                for i, below in zip(TILES, linked):
                    at = (k, rows_of(i[0]), lanes_of(i[1]))
                    value = solved[at] + inverse[at] * below
                    solved[at] = value
                    out.append(link[at] * value)
                linked = tuple(out)
            return linked

        linked = lax.fori_loop(0, CHUNK // UNROLL_BACK, step, linked)
        store(0, c).start()
        return linked

    lax.fori_loop(0, CHUNKS, back_chunk, blank)

    run[...] = jnp.zeros_like(run)
    u_sum[...] = jnp.zeros_like(u_sum)
    v_sum[...] = jnp.zeros_like(v_sum)
    q_col[...] = jnp.zeros_like(q_col)
    many = range(UNROLL_MOM)

    def momentum(m, _):
        first = m * UNROLL_MOM
        levels = [first + n for n in many]
        depths = [k.astype(F32) for k in levels]

        def running(b):
            out = []
            for h in pair:
                at = (rows_of(b), lanes_of(h))
                total = run[at]
                qs = []
                for k in levels:
                    half = 0.5 * solved[(k, *at)]
                    qs.append(total + half)
                    total = qs[-1] + half
                run[at] = total
                out.append(qs)
            return out

        q_next = running(0)
        turned_next = [[pltpu.roll(q, 7, 0) for q in q_next[h]] for h in pair]
        for h in pair:
            for n in many:
                to_west[pl.ds(24 + 40 * h + levels[n], 1), :] = q_next[h][n][0:1]
        for b in range(BLOCKS):
            rows = rows_of(b)
            q, turned = q_next, turned_next
            if b < BLOCKS - 1:
                q_next = running(b + 1)
                turned_next = [[pltpu.roll(x, 7, 0) for x in q_next[h]] for h in pair]
            else:
                turned_next = [[zero] * UNROLL_MOM] * 2
            left = [[pltpu.roll(x, 127, 1) for x in q[h]] for h in pair]
            column = q_col[rows, :]
            for n in many:
                column = jnp.where(lane == levels[n], pltpu.roll(q[0][n], levels[n], 1), column)
            q_col[rows, :] = column
            for h in pair:
                at = (rows, lanes_of(h))
                limit = east_lim[at]
                total = u_sum[at]
                for n in many:
                    ahead = jnp.where(last_row, turned_next[h][n], turned[h][n])
                    speed = jnp.where(
                        depths[n] < limit, u_in[(levels[n], *at)] - PRESS * (q[h][n] - ahead), 0.0
                    )
                    if b < BLOCKS - 1:
                        u_new[(levels[n], *at)] = speed
                    else:
                        u_end[levels[n], :, lanes_of(h)] = speed
                    total = total + speed
                u_sum[at] = total
                limit = north_lim[at]
                total = v_sum[at]
                for n in many:
                    ahead = jnp.where(last_lane, left[1][n] if h == 0 else 0.0, left[h][n])
                    speed = jnp.where(
                        depths[n] < limit, v_in[(levels[n], *at)] - PRESS * (q[h][n] - ahead), 0.0
                    )
                    if h == 0:
                        v_low[levels[n], rows, :] = speed
                    else:
                        v_high[levels[n], rows, :] = speed
                    total = total + speed
                v_sum[at] = total
        return 0

    def momentum_chunk(c, _):
        per = CHUNK // UNROLL_MOM
        lax.fori_loop(c * per, (c + 1) * per, momentum, 0)
        store(1, c).start()
        store(2, c).start()
        return 0

    lax.fori_loop(0, CHUNKS, momentum_chunk, 0)

    depth = lax.broadcasted_iota(jnp.int32, (LEVELS, 128), 0).astype(F32)
    row_sum = []
    for h in pair:
        part = jnp.where(
            depth < west_lim[0:1, lanes_of(h)], PRESS * to_west[24 + 40 * h : 64 + 40 * h, :], 0.0
        )
        row_sum.append(
            jnp.broadcast_to(jnp.sum(part, axis=0, keepdims=True), (8, 128))
        )
    depth = lane.astype(F32)
    col_sum = []
    for b in range(BLOCKS):
        rows = rows_of(b)
        limit = jnp.broadcast_to(south_lim[rows, 0:1], (8, 128))
        part = jnp.where(depth < limit, PRESS * q_col[rows, :], 0.0)
        col_sum.append(jnp.broadcast_to(jnp.sum(part, axis=1, keepdims=True), (8, 128)))

    east_sum, north_sum = tiles_of(u_sum), tiles_of(v_sum)
    east_before = prev_row(east_sum, row_sum, first_row)
    north_before = prev_col(north_sum, col_sum, first_lane)
    for i in TILES:
        at = (rows_of(i[0]), lanes_of(i[1]))
        divergence = (east_sum[i] - east_before[i]) + (north_sum[i] - north_before[i])
        force_out[at] = jnp.where(
            count[at] > 0.0, source_scale * rain[at] - DIVERGE * divergence, 0.0
        )
    for b in range(BLOCKS):
        sides[rows_of(b), :] = jnp.where(
            first_lane,
            pltpu.roll(north_sum[b, 1], 1, 1),
            jnp.where(last_lane, col_sum[b], 0.0),
        )
    for h in pair:
        to_east[rows_of(h), :] = pltpu.roll(force_out[ROWS - 8 : ROWS, lanes_of(h)], 5, 0)
        to_east[8 * h + 5 : 8 * h + 6, :] = east_sum[BLOCKS - 1, h][7:8]
        to_west[rows_of(h), :] = force_out[0:8, lanes_of(h)]
        to_west[8 * h + 5 : 8 * h + 6, :] = row_sum[h][0:1]
    to_east[16:24, :] = pltpu.roll(sides[ROWS - 8 : ROWS, :], 5, 0)
    to_west[16:24, :] = sides[0:8, :]

    for c in range(CHUNKS):
        for which in range(3):
            store(which, c).wait()


def columns(*args):
    return pl.pallas_call(
        column_kernel,
        out_shape=(
            shape(LEVELS, ROWS, COLS), shape(2, LEVELS, ROWS, COLS), shape(ROWS, COLS),
            shape(24, 128), shape(104, 128), shape(ROWS, 128), shape(ROWS, 128),
            shape(LEVELS, 8, COLS), shape(LEVELS, ROWS, 128),
        ),
        in_specs=[VMEM] * 15,
        out_specs=(ANY, ANY) + (VMEM,) * 7,
        scratch_shapes=[
            pltpu.VMEM((LEVELS, ROWS, COLS), F32),
            pltpu.VMEM((LEVELS, ROWS - 8, COLS), F32),
            pltpu.VMEM((LEVELS, ROWS, 128), F32),
            pltpu.VMEM((2, LEVELS, 128), F32), pltpu.VMEM((2, LEVELS, 128), F32),
            pltpu.VMEM((ROWS, 128), F32), pltpu.VMEM((ROWS, 128), F32),
            pltpu.VMEM((ROWS, COLS), F32), pltpu.VMEM((ROWS, COLS), F32),
            pltpu.VMEM((ROWS, 128), F32), pltpu.VMEM((8, COLS), F32),
            pltpu.VMEM((ROWS, COLS), F32), pltpu.VMEM((ROWS, COLS), F32),
            pltpu.VMEM((ROWS, COLS), F32),
            pltpu.SemaphoreType.DMA((3, CHUNKS)),
        ],
        compiler_params=params(LIMIT_COLUMNS),
        name="columns",
    )(*args)


EXT = ROWS + 16


def edges_kernel(
    force, sides, q_col, count, west, east_in, own_east, own_west, from_west, from_east,
    force_ext, count_ext, sides_ext, to_north, to_south,
):
    zeros8 = jnp.zeros((8, COLS), F32)
    count_ext[0:8, :] = zeros8
    for h in range(2):
        count_ext[2:8, lanes_of(h)] = west[h, 80:86, :]
    count_ext[8 : 8 + ROWS, :] = count[...]
    count_ext[8 + ROWS :, :] = zeros8
    for h in range(2):
        count_ext[8 + ROWS : 14 + ROWS, lanes_of(h)] = east_in[h, 40:46, :]
    sides_ext[0:8, :] = jnp.zeros((8, 128), F32)
    sides_ext[3:8, :] = from_west[16:21, :]
    sides_ext[8 : 8 + ROWS, :] = sides[...]
    sides_ext[8 + ROWS :, :] = jnp.zeros((8, 128), F32)
    sides_ext[8 + ROWS : 13 + ROWS, :] = from_east[16:21, :]
    force_ext[0:8, :] = zeros8
    for h in range(2):
        force_ext[3:8, lanes_of(h)] = from_west[8 * h : 8 * h + 5, :]
    force_ext[8 : 8 + ROWS, :] = force[...]
    force_ext[8 + ROWS :, :] = zeros8
    for h in range(2):
        force_ext[8 + ROWS : 13 + ROWS, lanes_of(h)] = from_east[8 * h : 8 * h + 5, :]

    def add(at, sign, ref):
        for h in range(2):
            place = (slice(at, at + 1), lanes_of(h))
            force_ext[place] = force_ext[place] + jnp.where(
                count_ext[place] > 0.0, sign * DIVERGE * ref[8 * h + 5 : 8 * h + 6, :], 0.0
            )

    add(7, -1.0, own_west)
    add(8, 1.0, from_west)
    add(7 + ROWS, -1.0, from_east)
    add(8 + ROWS, 1.0, own_east)
    lane = lane_id(EXT)
    side = sides_ext[...]
    to_north[...] = jnp.where(
        lane >= 123,
        force_ext[:, 128:],
        jnp.where(lane == 0, side, pltpu.roll(count_ext[:, 128:], 122, 1)),
    )
    to_south[...] = jnp.where(
        lane < 5,
        force_ext[:, :128],
        jnp.where(lane == 127, side, pltpu.roll(count_ext[:, :128], 8, 1)),
    )
    lane = lane_id(ROWS)
    to_south[8 : 8 + ROWS, :] = jnp.where(
        (lane >= 64) & (lane < 64 + LEVELS),
        pltpu.roll(q_col[...], 64, 1),
        to_south[8 : 8 + ROWS, :],
    )


def edges(*args):
    return pl.pallas_call(
        edges_kernel,
        out_shape=(
            shape(EXT, COLS), shape(EXT, COLS), shape(EXT, 128), shape(EXT, 128), shape(EXT, 128)
        ),
        in_specs=[VMEM] * 10,
        out_specs=(VMEM,) * 5,
        compiler_params=params(LIMIT_COLUMNS),
        name="edges",
    )(*args)


def final_kernel(
    speeds, u_end, v_high, from_east, count, east,
    force_ext, count_ext, sides_ext, south, north,
    speeds_out, out, u_fix, v_fix, sems,
):
    last_row = row_id() == 7
    for h in range(2):
        limit = jnp.minimum(
            count[ROWS - 8 :, lanes_of(h)], jnp.broadcast_to(east[h, 40:41, :], (8, 128))
        )
        limit = jnp.where(last_row, limit, 0.0)
        for k in range(LEVELS):
            at = 24 + 40 * h + k
            u_fix[k, :, lanes_of(h)] = u_end[k, :, lanes_of(h)] + jnp.where(
                float(k) < limit,
                PRESS * jnp.broadcast_to(from_east[at : at + 1, :], (8, 128)),
                0.0,
            )
    save_rows = pltpu.make_async_copy(
        u_fix, speeds_out.at[0, :, pl.ds(ROWS - 8, 8), :], sems.at[0]
    )
    save_rows.start()
    last_lane = lane_id(8) == 127
    for b in range(BLOCKS):
        rows = rows_of(b)
        held = north[8 * b + 8 : 8 * b + 16, :]
        limit = jnp.minimum(count[rows, 128:], pltpu.roll(held, 127 - 8, 1))
        limit = jnp.where(last_lane, limit, 0.0)
        for k in range(LEVELS):
            v_fix[k, rows, :] = v_high[k, rows, :] + jnp.where(
                float(k) < limit, PRESS * pltpu.roll(held, 63 - k, 1), 0.0
            )
    save_cols = pltpu.make_async_copy(
        v_fix, speeds_out.at[1, :, :, pl.ds(128, 128)], sems.at[1]
    )
    save_cols.start()
    lane = lane_id(EXT)
    count_side = jnp.where(
        lane >= 122,
        pltpu.roll(south[...], 6, 1),
        jnp.where(lane < 6, pltpu.roll(north[...], 120, 1), 0.0),
    )
    force_side = jnp.where(
        lane >= 123, south[...], jnp.where(lane < 5, north[...], 0.0)
    )
    side = sides_ext[...]
    low, high = force_ext[:, :128], force_ext[:, 128:]
    low = low + jnp.where(
        (lane == 0) & (count_ext[:, :128] > 0.0), DIVERGE * south[...], 0.0
    )
    high = high - jnp.where(
        (lane == 127) & (count_ext[:, 128:] > 0.0), DIVERGE * north[...], 0.0
    )
    force_side = force_side + jnp.where(
        (lane == 0) & (count_side > 0.0), DIVERGE * side, 0.0
    )
    force_side = force_side - jnp.where(
        (lane == 127) & (count_side > 0.0), DIVERGE * side, 0.0
    )
    force = jnp.concatenate([low, high, force_side], axis=1)
    count = jnp.concatenate([count_ext[...], count_side], axis=1)
    root = jnp.sqrt(count * (1.0 / LEVELS))
    wide = COLS + 128

    def total(field):
        sideways = pltpu.roll(field, 1, 1) + pltpu.roll(field, wide - 1, 1)
        mixed = field + 0.5 * sideways
        return sideways + (pltpu.roll(mixed, 1, 0) + pltpu.roll(mixed, EXT - 1, 0))

    diag = damping + root * total(root)
    inverse = 1.0 / diag
    update = inverse * force * (1.0 / cheb_gamma)
    iterate = update
    omega = 2.0 / cheb_gamma
    for step in range(1, ITERS):
        residual = force - (diag * iterate - root * total(root * iterate))
        omega = 1.0 / (cheb_gamma - omega / (4.0 * cheb_alpha * cheb_alpha))
        update = omega * inverse * residual + (cheb_gamma * omega - 1.0) * update
        iterate = iterate + update
    out[...] = iterate[8 : 8 + ROWS, 0:COLS]
    save_rows.wait()
    save_cols.wait()


def final(*args):
    return pl.pallas_call(
        final_kernel,
        out_shape=(shape(2, LEVELS, ROWS, COLS), shape(ROWS, COLS)),
        in_specs=[ANY] + [VMEM] * 10,
        out_specs=(ANY, VMEM),
        scratch_shapes=[
            pltpu.VMEM((LEVELS, 8, COLS), F32),
            pltpu.VMEM((LEVELS, ROWS, 128), F32),
            pltpu.SemaphoreType.DMA((2,)),
        ],
        input_output_aliases={0: 0},
        compiler_params=params(LIMIT_COLUMNS),
        name="final",
    )(*args)


def shift(array, axis, step):
    count = lax.axis_size(axis)
    return lax.ppermute(array, axis, [(i, (i + step) % count) for i in range(count)])


def local(
    thermal_departure,
    current_speeds,
    mixing_coefficient,
    seawater_indicator,
    submerged_layer_tally,
    rainfall_runoff_input,
):
    count, to_east, to_west, to_north, to_south = pack(
        *(
            pltpu.with_memory_space_constraint(x, pltpu.HBM)
            for x in (
                thermal_departure, current_speeds, seawater_indicator, submerged_layer_tally
            )
        )
    )
    south = shift(to_north, "gy", 1)
    north = shift(to_south, "gy", -1)
    west = shift(to_east, "gx", 1)
    east = shift(to_west, "gx", -1)
    inside = interior(thermal_departure, current_speeds, mixing_coefficient, count)
    temp_next, speeds, force, own_east, own_west, q_col, sides, u_end, v_high = columns(
        *inside, count, rainfall_runoff_input, to_east, to_west, to_north, to_south,
        west, east, south, north,
    )
    from_west = shift(own_east, "gx", 1)
    from_east = shift(own_west, "gx", -1)
    force_ext, count_ext, sides_ext, north_edge, south_edge = edges(
        force, sides, q_col, count, west, east, own_east, own_west, from_west, from_east
    )
    from_south = shift(north_edge, "gy", 1)
    from_north = shift(south_edge, "gy", -1)
    velocity_next, surface = final(
        speeds, u_end, v_high, from_east, count, east,
        force_ext, count_ext, sides_ext, from_south, from_north,
    )
    return (temp_next, velocity_next, surface)


def solution(mesh):
    placed = (
        P(None, "gx", "gy"),
        P(None, None, "gx", "gy"),
        P(None, "gx", "gy"),
        P("gx", "gy"),
        P("gx", "gy"),
        P("gx", "gy"),
    )
    return jax.shard_map(
        local,
        mesh=mesh,
        in_specs=placed,
        out_specs=(P(None, "gx", "gy"), P(None, None, "gx", "gy"), P("gx", "gy")),
        check_vma=False,
    )
```

```python
import jax
import jax.numpy as jnp
from jax import lax
from jax.experimental import pallas as pl
from jax.experimental.pallas import tpu as pltpu
from jax.sharding import PartitionSpec as P

ITERS = 6
LIMIT_PACK = 40
LIMIT_INTERIOR = 40
LIMIT_COLUMNS = 24
LEVELS = 40
ROWS = 64
COLS = 256
BLOCKS = ROWS // 8
CHUNK = 8
CHUNKS = LEVELS // CHUNK

damping = 0.05
lower_bound = 0.02
upper_bound = 2.0
cheb_alpha = 2.0 / (upper_bound - lower_bound)
cheb_gamma = (upper_bound + lower_bound) / 2.0
advect_scale = 0.4
force_scale = 4.0
source_scale = 0.5
divergence_scale = 4.0
PRESS = force_scale / LEVELS
DIVERGE = divergence_scale / LEVELS

VMEM = pl.BlockSpec(memory_space=pltpu.VMEM)
ANY = pl.BlockSpec(memory_space=pl.ANY)
HBM = pl.BlockSpec(memory_space=pltpu.HBM)
F32 = jnp.float32
TILES = [(b, h) for b in range(BLOCKS) for h in range(2)]


def shape(*dims):
    return jax.ShapeDtypeStruct(dims, F32)


def params(mebibytes=40):
    return pltpu.CompilerParams(vmem_limit_bytes=int(mebibytes * 1024 * 1024))


def lane_id(rows=8):
    return lax.broadcasted_iota(jnp.int32, (rows, 128), 1)


def row_id():
    return lax.broadcasted_iota(jnp.int32, (8, 128), 0)


def rows_of(b):
    return slice(8 * b, 8 * b + 8)


def lanes_of(h):
    return slice(128 * h, 128 * h + 128)


def tiles_of(ref, *lead):
    return {(b, h): ref[(*lead, rows_of(b), lanes_of(h))] for b, h in TILES}


def next_row(x, after, last):
    turned = {t: pltpu.roll(x[t], 7, 0) for t in TILES}
    return {
        (b, h): jnp.where(last, after[h] if b == BLOCKS - 1 else turned[b + 1, h], turned[b, h])
        for b, h in TILES
    }


def prev_row(x, before, first):
    turned = {t: pltpu.roll(x[t], 1, 0) for t in TILES}
    return {
        (b, h): jnp.where(first, before[h] if b == 0 else turned[b - 1, h], turned[b, h])
        for b, h in TILES
    }


def next_col(x, after, last):
    turned = {t: pltpu.roll(x[t], 127, 1) for t in TILES}
    return {
        (b, h): jnp.where(last, after[b] if h == 1 else turned[b, 1], turned[b, h])
        for b, h in TILES
    }


def prev_col(x, before, first):
    turned = {t: pltpu.roll(x[t], 1, 1) for t in TILES}
    return {
        (b, h): jnp.where(first, before[b] if h == 0 else turned[b, 0], turned[b, h])
        for b, h in TILES
    }


def spread(ref, k, h):
    return jnp.broadcast_to(ref[h, pl.ds(k, 1), :], (8, 128))


def pack_kernel(
    temp, speeds, sea_in, tally_in,
    count_out, to_east, to_west, to_north, to_south,
    t_low, t_high, v_high, t_top, t_end, u_end, sea, tally, sems,
):
    copies = [
        pltpu.make_async_copy(sea_in, sea, sems.at[6]),
        pltpu.make_async_copy(tally_in, tally, sems.at[7]),
        pltpu.make_async_copy(temp.at[:, :, pl.ds(0, 128)], t_low, sems.at[0]),
        pltpu.make_async_copy(temp.at[:, :, pl.ds(128, 128)], t_high, sems.at[1]),
        pltpu.make_async_copy(speeds.at[1, :, :, pl.ds(128, 128)], v_high, sems.at[2]),
        pltpu.make_async_copy(temp.at[:, pl.ds(0, 8), :], t_top, sems.at[3]),
        pltpu.make_async_copy(temp.at[:, pl.ds(ROWS - 8, 8), :], t_end, sems.at[4]),
        pltpu.make_async_copy(speeds.at[0, :, pl.ds(ROWS - 8, 8), :], u_end, sems.at[5]),
    ]
    for copy in copies:
        copy.start()
    copies[0].wait()
    copies[1].wait()
    copies = copies[2:]
    latitude = lax.axis_index("gy") * COLS + lax.broadcasted_iota(jnp.int32, (ROWS, COLS), 1)
    inner = (latitude > 0) & (latitude < lax.axis_size("gy") * COLS - 1)
    count = jnp.where(inner & (sea[...] == 1), tally[...], 0).astype(F32)
    count_out[...] = count
    for h in range(2):
        to_east[h, 80:86, :] = count[ROWS - 6 :, lanes_of(h)]
        to_east[h, 86:88, :] = jnp.zeros((2, 128), F32)
        to_west[h, 40:46, :] = count[:6, lanes_of(h)]
        to_west[h, 46:48, :] = jnp.zeros((2, 128), F32)
    lane = lane_id(ROWS)

    def gather(ref, column, start, total):
        for k in range(LEVELS):
            total = jnp.where(
                lane == start + k, pltpu.roll(ref[k], (start + k - column) % 128, 1), total
            )
        return total

    copies[0].wait()
    to_south[...] = gather(
        t_low, 0, 0, pltpu.roll(count[:, :128], 40, 1)
    )
    copies[1].wait()
    total = gather(t_high, 127, 0, pltpu.roll(count[:, 128:], (80 - 127) % 128, 1))
    copies[2].wait()
    to_north[...] = gather(v_high, 127, 40, total)
    copies[3].wait()
    copies[4].wait()
    copies[5].wait()
    for h in range(2):
        to_west[h, 0:40, :] = t_top[:, 0, lanes_of(h)]
        to_east[h, 0:40, :] = t_end[:, 7, lanes_of(h)]
        to_east[h, 40:80, :] = u_end[:, 7, lanes_of(h)]


def pack(temp, speeds, sea, tally):
    return pl.pallas_call(
        pack_kernel,
        out_shape=(
            shape(ROWS, COLS), shape(2, 88, 128), shape(2, 48, 128), shape(ROWS, 128), shape(ROWS, 128)
        ),
        in_specs=[HBM, HBM, HBM, HBM],
        out_specs=(VMEM,) * 5,
        scratch_shapes=[
            pltpu.VMEM((LEVELS, ROWS, 128), F32),
            pltpu.VMEM((LEVELS, ROWS, 128), F32),
            pltpu.VMEM((LEVELS, ROWS, 128), F32),
            pltpu.VMEM((LEVELS, 8, COLS), F32),
            pltpu.VMEM((LEVELS, 8, COLS), F32),
            pltpu.VMEM((LEVELS, 8, COLS), F32),
            pltpu.VMEM((ROWS, COLS), jnp.int32),
            pltpu.VMEM((ROWS, COLS), jnp.int32),
            pltpu.SemaphoreType.DMA((8,)),
        ],
        compiler_params=params(LIMIT_PACK),
        name="pack",
    )(temp, speeds, sea, tally)


UNROLL_IN = 4
UNROLL_FWD = 20
UNROLL_BACK = 20
UNROLL_MOM = 5


def interior_kernel(
    temp, speeds, mix, count,
    source_out, inverse_out, link_out, u_out, v_out,
    tb, mb, east_lim, north_lim, sems,
):
    def load(which, c):
        part = pl.ds(c * CHUNK, CHUNK)
        origin, target = (
            (mix, mb), (temp, tb), (speeds.at[0], u_out), (speeds.at[1], v_out)
        )[which]
        return pltpu.make_async_copy(origin.at[part], target.at[part], sems.at[which, c])

    for c in range(CHUNKS):
        for which in range(4):
            load(which, c).start()

    lane, row = lane_id(), row_id()
    first_row, last_row = row == 0, row == 7
    first_lane, last_lane = lane == 0, lane == 127
    zero = jnp.zeros((8, 128), F32)
    pair = range(2)

    counts = tiles_of(count)
    ahead = next_row(counts, [zero, zero], last_row)
    for b, h in TILES:
        east_lim[rows_of(b), lanes_of(h)] = jnp.minimum(counts[b, h], ahead[b, h])
    ahead = next_col(counts, [zero] * BLOCKS, last_lane)
    for b, h in TILES:
        north_lim[rows_of(b), lanes_of(h)] = jnp.minimum(counts[b, h], ahead[b, h])

    def level_step(k, factors, links):
        level = k.astype(F32)
        below_at = jnp.minimum(k + 1, LEVELS - 1)
        t_next = [tb[k, rows_of(0), lanes_of(h)] for h in pair]
        turned_next = [pltpu.roll(t_next[h], 7, 0) for h in pair]
        flux_turned = [zero, zero]
        new_factors, new_links = [], []
        for b in range(BLOCKS):
            rows = rows_of(b)
            t, turned = t_next, turned_next
            if b < BLOCKS - 1:
                t_next = [tb[k, rows_of(b + 1), lanes_of(h)] for h in pair]
                turned_next = [pltpu.roll(t_next[h], 7, 0) for h in pair]
            u = [u_out[k, rows, lanes_of(h)] for h in pair]
            v = [v_out[k, rows, lanes_of(h)] for h in pair]
            change = []
            for h in pair:
                ahead = jnp.where(last_row, turned_next[h], turned[h])
                flux = jnp.where(level < east_lim[rows, lanes_of(h)], u[h], 0.0) * jnp.where(
                    u[h] > 0.0, t[h], ahead
                )
                flux_before, flux_turned[h] = flux_turned[h], pltpu.roll(flux, 1, 0)
                change.append(flux - jnp.where(first_row, flux_before, flux_turned[h]))
            left = [pltpu.roll(t[h], 127, 1) for h in pair]
            ahead = [jnp.where(last_lane, left[1], left[0]), left[1]]
            flux = [
                jnp.where(level < north_lim[rows, lanes_of(h)], v[h], 0.0)
                * jnp.where(v[h] > 0.0, t[h], ahead[h])
                for h in pair
            ]
            right = [pltpu.roll(flux[h], 1, 1) for h in pair]
            behind = [jnp.where(first_lane, 0.0, right[0]), jnp.where(first_lane, right[0], right[1])]
            for h in pair:
                n = 2 * b + h
                at = (k, rows, lanes_of(h))
                wet = count[rows, lanes_of(h)]
                total = change[h] + (flux[h] - behind[h])
                source_out[at] = t[h] - jnp.where(level < wet, advect_scale * total, 0.0)
                a = links[n]
                below = jnp.where(
                    level + 1.0 < wet, mb[below_at, rows, lanes_of(h)], 0.0
                )
                pivot = (1.0 + below) + (a - a * factors[n])
                inverse = pl.reciprocal(pivot, approx=True)
                inverse = inverse * (2.0 - pivot * inverse)
                inverse_out[at] = inverse
                link_out[at] = a
                new_factors.append(below * inverse)
                new_links.append(below)
        return tuple(new_factors), tuple(new_links)

    load(0, 0).wait()

    def chunk_step(c, carry):
        @pl.when(c < CHUNKS - 1)
        def _():
            load(0, c + 1).wait()

        for which in range(1, 4):
            load(which, c).wait()

        def step(m, carry):
            for n in range(UNROLL_IN):
                carry = level_step(c * CHUNK + m * UNROLL_IN + n, *carry)
            return carry

        return lax.fori_loop(0, CHUNK // UNROLL_IN, step, carry)

    blank = tuple(zero for _ in TILES)
    lax.fori_loop(0, CHUNKS, chunk_step, (blank, blank))


def interior(temp, speeds, mix, count):
    block = shape(LEVELS, ROWS, COLS)
    scratch = pltpu.VMEM((LEVELS, ROWS, COLS), F32)
    return pl.pallas_call(
        interior_kernel,
        out_shape=(block,) * 5,
        in_specs=[ANY, ANY, ANY, VMEM],
        out_specs=(VMEM,) * 5,
        scratch_shapes=[
            scratch, scratch,
            pltpu.VMEM((ROWS, COLS), F32), pltpu.VMEM((ROWS, COLS), F32),
            pltpu.SemaphoreType.DMA((4, CHUNKS)),
        ],
        cost_estimate=pl.CostEstimate(
            flops=30 * LEVELS * ROWS * COLS, bytes_accessed=16 * LEVELS * ROWS * COLS,
            transcendentals=0,
        ),
        compiler_params=params(LIMIT_INTERIOR),
        name="interior",
    )(temp, speeds, mix, count)


OUTER = (0, BLOCKS - 1)
MIDDLE = tuple(range(1, BLOCKS - 1))


def face_limits(
    blocks, count, west, east, south, north, east_lim, north_lim, south_lim, west_lim
):
    lane, row = lane_id(), row_id()
    last_row, last_lane = row == 7, lane == 127
    counts = tiles_of(count)
    pair = range(2)
    for h in pair:
        before = jnp.broadcast_to(west[h, 85:86, :], (8, 128))
        west_lim[:, lanes_of(h)] = jnp.minimum(counts[0, h], before)
        for b in blocks:
            if b == BLOCKS - 1:
                after = jnp.broadcast_to(east[h, 40:41, :], (8, 128))
            else:
                after = pltpu.roll(counts[b + 1, h], 7, 0)
            ahead = jnp.where(last_row, after, pltpu.roll(counts[b, h], 7, 0))
            east_lim[rows_of(b), lanes_of(h)] = jnp.minimum(counts[b, h], ahead)
    for b in blocks:
        rows = rows_of(b)
        left = [pltpu.roll(counts[b, h], 127, 1) for h in pair]
        left.append(pltpu.roll(north[rows, :], 127 - 40, 1))
        for h in pair:
            ahead = jnp.where(last_lane, left[h + 1], left[h])
            north_lim[rows, lanes_of(h)] = jnp.minimum(counts[b, h], ahead)
        south_lim[rows, :] = jnp.minimum(counts[b, 0], pltpu.roll(south[rows, :], 128 - 80, 1))


def column_fluxes(
    blocks, own_north, own_south, south, north, south_lim, north_lim, col_low, col_high
):
    depth = lane_id().astype(F32)
    for b in blocks:
        rows = rows_of(b)
        limit = jnp.broadcast_to(south_lim[rows, 0:1], (8, 128))
        speed = pltpu.roll(south[rows, :], 128 - 40, 1)
        col_low[rows, :] = (
            advect_scale
            * jnp.where(depth < limit, speed, 0.0)
            * jnp.where(speed > 0.0, south[rows, :], own_south[rows, :])
        )
        limit = jnp.broadcast_to(north_lim[rows, COLS - 1 : COLS], (8, 128))
        speed = pltpu.roll(own_north[rows, :], 128 - 40, 1)
        col_high[rows, :] = (
            -advect_scale
            * jnp.where(depth < limit, speed, 0.0)
            * jnp.where(speed > 0.0, own_north[rows, :], north[rows, :])
        )


def row_fluxes(own_east, own_west, west, east, west_lim, east_lim, row_low, row_high):
    depth = lax.broadcasted_iota(jnp.int32, (LEVELS, 128), 0).astype(F32)
    for h in range(2):
        speed = west[h, 40:80, :]
        row_low[h] = (
            advect_scale
            * jnp.where(depth < west_lim[0:1, lanes_of(h)], speed, 0.0)
            * jnp.where(speed > 0.0, west[h, 0:40, :], own_west[h, 0:40, :])
        )
        speed = own_east[h, 40:80, :]
        row_high[h] = (
            -advect_scale
            * jnp.where(depth < east_lim[ROWS - 1 : ROWS, lanes_of(h)], speed, 0.0)
            * jnp.where(speed > 0.0, own_east[h, 0:40, :], east[h, 0:40, :])
        )


def solve(blocks, place, source, inverse, link, col_low, col_high, row_low, row_high, solved):
    lane, row = lane_id(), row_id()
    first_row, last_row = row == 0, row == 7
    first_lane, last_lane = lane == 0, lane == 127
    zero = jnp.zeros((8, 128), F32)
    pair = range(2)

    def forward(k, values):
        out = []
        for n, b in enumerate(blocks):
            rows = rows_of(b)
            add = [
                jnp.where(first_lane, pltpu.roll(col_low[rows, :], 128 - k, 1), 0.0),
                jnp.where(last_lane, pltpu.roll(col_high[rows, :], 127 - k, 1), 0.0),
            ]
            for h in pair:
                at = (k, rows, lanes_of(h))
                total = source[at] + add[h]
                if b == 0:
                    total = total + jnp.where(first_row, spread(row_low, k, h), 0.0)
                if b == BLOCKS - 1:
                    total = total + jnp.where(last_row, spread(row_high, k, h), 0.0)
                value = (total + link[at] * values[2 * n + h]) * inverse[at]
                solved[k, place(b), lanes_of(h)] = value
                out.append(value)
        return tuple(out)

    blank = (zero,) * (2 * len(blocks))

    def forward_step(m, values):
        for n in range(UNROLL_FWD):
            values = forward(m * UNROLL_FWD + n, values)
        return values

    lax.fori_loop(0, LEVELS // UNROLL_FWD, forward_step, blank)

    def back_step(m, linked):
        for n in range(UNROLL_BACK):
            k = LEVELS - 1 - m * UNROLL_BACK - n
            out = []
            for i, below in zip([(b, h) for b in blocks for h in pair], linked):
                at = (k, rows_of(i[0]), lanes_of(i[1]))
                to = (k, place(i[0]), lanes_of(i[1]))
                value = solved[to] + inverse[at] * below
                solved[to] = value
                out.append(link[at] * value)
            linked = tuple(out)
        return linked

    lax.fori_loop(0, LEVELS // UNROLL_BACK, back_step, blank)


def row_face_sum(west_lim, q_rows):
    depth = lax.broadcasted_iota(jnp.int32, (LEVELS, 128), 0).astype(F32)
    out = []
    for h in range(2):
        part = jnp.where(depth < west_lim[0:1, lanes_of(h)], PRESS * q_rows(h), 0.0)
        out.append(jnp.broadcast_to(jnp.sum(part, axis=0, keepdims=True), (8, 128)))
    return out


def col_face_sum(rows, south_lim, q_col):
    limit = jnp.broadcast_to(south_lim[rows, 0:1], (8, 128))
    part = jnp.where(lane_id().astype(F32) < limit, PRESS * q_col[rows, :], 0.0)
    return jnp.broadcast_to(jnp.sum(part, axis=1, keepdims=True), (8, 128))


def momentum(
    blocks, values, following, u_in, v_in, east_lim, north_lim, run, u_sum, v_sum, q_col,
    keep_u, keep_v, keep_row,
):
    lane, row = lane_id(), row_id()
    last_row, last_lane = row == 7, lane == 127
    zero = jnp.zeros((8, 128), F32)
    pair = range(2)
    many = range(UNROLL_MOM)
    for b in blocks:
        run[rows_of(b), :] = jnp.zeros((8, COLS), F32)
        u_sum[rows_of(b), :] = jnp.zeros((8, COLS), F32)
        v_sum[rows_of(b), :] = jnp.zeros((8, COLS), F32)
        q_col[rows_of(b), :] = zero

    def step(m, _):
        first = m * UNROLL_MOM
        levels = [first + n for n in many]
        depths = [k.astype(F32) for k in levels]

        def running(b):
            out = []
            for h in pair:
                at = (rows_of(b), lanes_of(h))
                total = run[at]
                qs = []
                for k in levels:
                    half = 0.5 * values(k, b, h)
                    qs.append(total + half)
                    total = qs[-1] + half
                run[at] = total
                out.append(qs)
            return out

        q_next = None
        for b in blocks:
            rows = rows_of(b)
            if q_next is None:
                q = running(b)
                turned = [[pltpu.roll(x, 7, 0) for x in q[h]] for h in pair]
            else:
                q, turned = q_next, turned_next
            if b == 0:
                for h in pair:
                    for n in many:
                        keep_row(levels[n], h, q[h][n][0:1])
            if following(b):
                q_next = running(b + 1)
                turned_next = [[pltpu.roll(x, 7, 0) for x in q_next[h]] for h in pair]
            else:
                q_next, turned_next = None, [[zero] * UNROLL_MOM] * 2
            left = [[pltpu.roll(x, 127, 1) for x in q[h]] for h in pair]
            column = q_col[rows, :]
            for n in many:
                column = jnp.where(lane == levels[n], pltpu.roll(q[0][n], levels[n], 1), column)
            q_col[rows, :] = column
            for h in pair:
                at = (rows, lanes_of(h))
                limit = east_lim[at]
                total = u_sum[at]
                for n in many:
                    ahead = jnp.where(last_row, turned_next[h][n], turned[h][n])
                    speed = jnp.where(
                        depths[n] < limit, u_in[(levels[n], *at)] - PRESS * (q[h][n] - ahead), 0.0
                    )
                    keep_u(levels[n], b, h, speed)
                    total = total + speed
                u_sum[at] = total
                limit = north_lim[at]
                total = v_sum[at]
                for n in many:
                    ahead = jnp.where(last_lane, left[1][n] if h == 0 else 0.0, left[h][n])
                    speed = jnp.where(
                        depths[n] < limit, v_in[(levels[n], *at)] - PRESS * (q[h][n] - ahead), 0.0
                    )
                    keep_v(levels[n], b, h, speed)
                    total = total + speed
                v_sum[at] = total
        return 0

    lax.fori_loop(0, LEVELS // UNROLL_MOM, step, 0)


def forcing(blocks, u_sum, v_sum, row_sum, south_lim, q_col, count, rain, keep):
    lane, row = lane_id(), row_id()
    first_row, first_lane, last_lane = row == 0, lane == 0, lane == 127
    pair = range(2)
    for b in blocks:
        rows = rows_of(b)
        col_sum = col_face_sum(rows, south_lim, q_col)
        u = [u_sum[rows, lanes_of(h)] for h in pair]
        v = [v_sum[rows, lanes_of(h)] for h in pair]
        right = [pltpu.roll(v[h], 1, 1) for h in pair]
        v_before = [
            jnp.where(first_lane, col_sum, right[0]), jnp.where(first_lane, right[0], right[1])
        ]
        tiles = []
        for h in pair:
            at = (rows, lanes_of(h))
            if b == 0:
                before = row_sum[h]
            else:
                before = pltpu.roll(u_sum[rows_of(b - 1), lanes_of(h)], 1, 0)
            u_before = jnp.where(first_row, before, pltpu.roll(u[h], 1, 0))
            divergence = (u[h] - u_before) + (v[h] - v_before[h])
            tiles.append(
                jnp.where(count[at] > 0.0, source_scale * rain[at] - DIVERGE * divergence, 0.0)
            )
        side = jnp.where(first_lane, right[1], jnp.where(last_lane, col_sum, 0.0))
        keep(b, tiles, side)


def outer_kernel(
    source, inverse, link, u_in, v_in, count, rain, own_east, own_west, own_north, own_south,
    west, east, south, north,
    solved, to_east, to_west,
    row_low, row_high, col_low, col_high, east_lim, north_lim, south_lim, west_lim,
    run, u_sum, v_sum, q_col,
):
    face_limits(
        OUTER, count, west, east, south, north, east_lim, north_lim, south_lim, west_lim
    )
    row_fluxes(own_east, own_west, west, east, west_lim, east_lim, row_low, row_high)
    column_fluxes(
        OUTER, own_north, own_south, south, north, south_lim, north_lim, col_low, col_high
    )

    def place(b):
        return slice(0, 8) if b == 0 else slice(8, 16)

    solve(OUTER, place, source, inverse, link, col_low, col_high, row_low, row_high, solved)

    def keep_row(k, h, value):
        to_west[pl.ds(24 + 40 * h + k, 1), :] = value

    def drop(*args):
        pass

    momentum(
        OUTER, lambda k, b, h: solved[k, place(b), lanes_of(h)], lambda b: False,
        u_in, v_in, east_lim, north_lim, run, u_sum, v_sum, q_col, drop, drop, keep_row,
    )
    row_sum = row_face_sum(west_lim, lambda h: to_west[24 + 40 * h : 64 + 40 * h, :])
    u_sum[rows_of(BLOCKS - 2), :] = jnp.zeros((8, COLS), F32)

    def keep(b, tiles, side):
        for h in range(2):
            if b == 0:
                to_west[rows_of(h), :] = tiles[h]
                to_west[8 * h + 5 : 8 * h + 6, :] = row_sum[h][0:1]
            else:
                to_east[rows_of(h), :] = pltpu.roll(tiles[h], 5, 0)
                to_east[8 * h + 5 : 8 * h + 6, :] = u_sum[ROWS - 1 : ROWS, lanes_of(h)]
        if b == 0:
            to_west[16:24, :] = side
        else:
            to_east[16:24, :] = pltpu.roll(side, 5, 0)

    forcing(OUTER, u_sum, v_sum, row_sum, south_lim, q_col, count, rain, keep)


def outer(*args):
    plane = pltpu.VMEM((ROWS, COLS), F32)
    strip = pltpu.VMEM((ROWS, 128), F32)
    levels = pltpu.VMEM((2, LEVELS, 128), F32)
    return pl.pallas_call(
        outer_kernel,
        out_shape=(shape(LEVELS, 16, COLS), shape(24, 128), shape(104, 128)),
        in_specs=[VMEM] * 15,
        out_specs=(VMEM,) * 3,
        scratch_shapes=[
            levels, levels, strip, strip, plane, plane, strip, pltpu.VMEM((8, COLS), F32),
            plane, plane, plane, strip,
        ],
        compiler_params=params(LIMIT_COLUMNS),
        name="outer",
    )(*args)


def middle_kernel(
    source, inverse, link, u_in, v_in, count, rain, own_north, own_south,
    west, east, south, north, outside, own_west,
    solved, u_new, v_low, v_high, force_out, q_col, sides,
    col_low, col_high, east_lim, north_lim, south_lim, west_lim, run, u_sum, v_sum,
):
    every = tuple(range(BLOCKS))
    face_limits(
        every, count, west, east, south, north, east_lim, north_lim, south_lim, west_lim
    )
    column_fluxes(
        MIDDLE, own_north, own_south, south, north, south_lim, north_lim, col_low, col_high
    )

    def place(b):
        return rows_of(b - 1)

    solve(MIDDLE, place, source, inverse, link, col_low, col_high, None, None, solved)

    def values(k, b, h):
        if b == 0:
            return outside[k, 0:8, lanes_of(h)]
        if b == BLOCKS - 1:
            return outside[k, 8:16, lanes_of(h)]
        return solved[k, place(b), lanes_of(h)]

    def keep_u(k, b, h, speed):
        u_new[k, rows_of(b), lanes_of(h)] = speed

    def keep_v(k, b, h, speed):
        if h == 0:
            v_low[k, rows_of(b), :] = speed
        else:
            v_high[k, rows_of(b), :] = speed

    momentum(
        every, values, lambda b: b < BLOCKS - 1, u_in, v_in, east_lim, north_lim,
        run, u_sum, v_sum, q_col, keep_u, keep_v, lambda k, h, value: None,
    )
    row_sum = [
        jnp.broadcast_to(own_west[8 * h + 5 : 8 * h + 6, :], (8, 128)) for h in range(2)
    ]

    def keep(b, tiles, side):
        for h in range(2):
            force_out[rows_of(b), lanes_of(h)] = tiles[h]
        sides[rows_of(b), :] = side

    forcing(every, u_sum, v_sum, row_sum, south_lim, q_col, count, rain, keep)


def middle(*args):
    plane = pltpu.VMEM((ROWS, COLS), F32)
    strip = pltpu.VMEM((ROWS, 128), F32)
    half = shape(LEVELS, ROWS, 128)
    return pl.pallas_call(
        middle_kernel,
        out_shape=(
            shape(LEVELS, ROWS - 16, COLS), shape(LEVELS, ROWS, COLS), half, half,
            shape(ROWS, COLS), shape(ROWS, 128), shape(ROWS, 128),
        ),
        in_specs=[VMEM] * 15,
        out_specs=(VMEM,) * 7,
        scratch_shapes=[
            strip, strip, plane, plane, strip, pltpu.VMEM((8, COLS), F32), plane, plane, plane,
        ],
        cost_estimate=pl.CostEstimate(
            flops=30 * LEVELS * ROWS * COLS, bytes_accessed=16 * LEVELS * ROWS * COLS,
            transcendentals=0,
        ),
        compiler_params=params(LIMIT_COLUMNS),
        name="middle",
    )(*args)


def writer_kernel(
    outside, solved, u_new, v_low, from_east, count, east, temp_out, speeds_out, u_fix, sems
):
    copies = [
        (outside.at[:, pl.ds(0, 8), :], temp_out.at[:, pl.ds(0, 8), :]),
        (outside.at[:, pl.ds(8, 8), :], temp_out.at[:, pl.ds(ROWS - 8, 8), :]),
        (solved, temp_out.at[:, pl.ds(8, ROWS - 16), :]),
        (u_new.at[:, pl.ds(0, ROWS - 8), :], speeds_out.at[0, :, pl.ds(0, ROWS - 8), :]),
        (v_low, speeds_out.at[1, :, :, pl.ds(0, 128)]),
        (u_fix, speeds_out.at[0, :, pl.ds(ROWS - 8, 8), :]),
    ]
    copies = [
        pltpu.make_async_copy(origin, target, sems.at[n])
        for n, (origin, target) in enumerate(copies)
    ]
    for copy in copies[:-1]:
        copy.start()
    last_row = row_id() == 7
    for h in range(2):
        limit = jnp.minimum(
            count[ROWS - 8 :, lanes_of(h)], jnp.broadcast_to(east[h, 40:41, :], (8, 128))
        )
        limit = jnp.where(last_row, limit, 0.0)
        for k in range(LEVELS):
            at = 24 + 40 * h + k
            u_fix[k, :, lanes_of(h)] = u_new[k, ROWS - 8 :, lanes_of(h)] + jnp.where(
                float(k) < limit,
                PRESS * jnp.broadcast_to(from_east[at : at + 1, :], (8, 128)),
                0.0,
            )
    copies[-1].start()
    for copy in copies:
        copy.wait()


def writer(*args):
    return pl.pallas_call(
        writer_kernel,
        out_shape=(shape(LEVELS, ROWS, COLS), shape(2, LEVELS, ROWS, COLS)),
        in_specs=[VMEM] * 7,
        out_specs=(ANY, ANY),
        scratch_shapes=[
            pltpu.VMEM((LEVELS, 8, COLS), F32),
            pltpu.SemaphoreType.DMA((6,)),
        ],
        cost_estimate=pl.CostEstimate(
            flops=LEVELS * ROWS * COLS, bytes_accessed=12 * LEVELS * ROWS * COLS,
            transcendentals=0,
        ),
        compiler_params=params(LIMIT_COLUMNS),
        name="writer",
    )(*args)


EXT = ROWS + 16


def edges_kernel(
    force, sides, q_col, count, west, east_in, own_east, own_west, from_west, from_east,
    force_ext, count_ext, sides_ext, to_north, to_south,
):
    zeros8 = jnp.zeros((8, COLS), F32)
    count_ext[0:8, :] = zeros8
    for h in range(2):
        count_ext[2:8, lanes_of(h)] = west[h, 80:86, :]
    count_ext[8 : 8 + ROWS, :] = count[...]
    count_ext[8 + ROWS :, :] = zeros8
    for h in range(2):
        count_ext[8 + ROWS : 14 + ROWS, lanes_of(h)] = east_in[h, 40:46, :]
    sides_ext[0:8, :] = jnp.zeros((8, 128), F32)
    sides_ext[3:8, :] = from_west[16:21, :]
    sides_ext[8 : 8 + ROWS, :] = sides[...]
    sides_ext[8 + ROWS :, :] = jnp.zeros((8, 128), F32)
    sides_ext[8 + ROWS : 13 + ROWS, :] = from_east[16:21, :]
    force_ext[0:8, :] = zeros8
    for h in range(2):
        force_ext[3:8, lanes_of(h)] = from_west[8 * h : 8 * h + 5, :]
    force_ext[8 : 8 + ROWS, :] = force[...]
    force_ext[8 + ROWS :, :] = zeros8
    for h in range(2):
        force_ext[8 + ROWS : 13 + ROWS, lanes_of(h)] = from_east[8 * h : 8 * h + 5, :]

    def add(at, sign, ref):
        for h in range(2):
            place = (slice(at, at + 1), lanes_of(h))
            force_ext[place] = force_ext[place] + jnp.where(
                count_ext[place] > 0.0, sign * DIVERGE * ref[8 * h + 5 : 8 * h + 6, :], 0.0
            )

    add(7, -1.0, own_west)
    add(8, 1.0, from_west)
    add(7 + ROWS, -1.0, from_east)
    add(8 + ROWS, 1.0, own_east)
    lane = lane_id(EXT)
    side = sides_ext[...]
    to_north[...] = jnp.where(
        lane >= 123,
        force_ext[:, 128:],
        jnp.where(lane == 0, side, pltpu.roll(count_ext[:, 128:], 122, 1)),
    )
    to_south[...] = jnp.where(
        lane < 5,
        force_ext[:, :128],
        jnp.where(lane == 127, side, pltpu.roll(count_ext[:, :128], 8, 1)),
    )
    lane = lane_id(ROWS)
    to_south[8 : 8 + ROWS, :] = jnp.where(
        (lane >= 64) & (lane < 64 + LEVELS),
        pltpu.roll(q_col[...], 64, 1),
        to_south[8 : 8 + ROWS, :],
    )


def edges(*args):
    return pl.pallas_call(
        edges_kernel,
        out_shape=(
            shape(EXT, COLS), shape(EXT, COLS), shape(EXT, 128), shape(EXT, 128), shape(EXT, 128)
        ),
        in_specs=[VMEM] * 10,
        out_specs=(VMEM,) * 5,
        compiler_params=params(LIMIT_COLUMNS),
        name="edges",
    )(*args)


def final_kernel(
    speeds, v_high, count,
    force_ext, count_ext, sides_ext, south, north,
    speeds_out, out, v_fix, sem,
):
    last_lane = lane_id(8) == 127
    for b in range(BLOCKS):
        rows = rows_of(b)
        held = north[8 * b + 8 : 8 * b + 16, :]
        limit = jnp.minimum(count[rows, 128:], pltpu.roll(held, 127 - 8, 1))
        limit = jnp.where(last_lane, limit, 0.0)
        for k in range(LEVELS):
            v_fix[k, rows, :] = v_high[k, rows, :] + jnp.where(
                float(k) < limit, PRESS * pltpu.roll(held, 63 - k, 1), 0.0
            )
    save_cols = pltpu.make_async_copy(
        v_fix, speeds_out.at[1, :, :, pl.ds(128, 128)], sem
    )
    save_cols.start()
    lane = lane_id(EXT)
    count_side = jnp.where(
        lane >= 122,
        pltpu.roll(south[...], 6, 1),
        jnp.where(lane < 6, pltpu.roll(north[...], 120, 1), 0.0),
    )
    force_side = jnp.where(
        lane >= 123, south[...], jnp.where(lane < 5, north[...], 0.0)
    )
    side = sides_ext[...]
    low, high = force_ext[:, :128], force_ext[:, 128:]
    low = low + jnp.where(
        (lane == 0) & (count_ext[:, :128] > 0.0), DIVERGE * south[...], 0.0
    )
    high = high - jnp.where(
        (lane == 127) & (count_ext[:, 128:] > 0.0), DIVERGE * north[...], 0.0
    )
    force_side = force_side + jnp.where(
        (lane == 0) & (count_side > 0.0), DIVERGE * side, 0.0
    )
    force_side = force_side - jnp.where(
        (lane == 127) & (count_side > 0.0), DIVERGE * side, 0.0
    )
    force = jnp.concatenate([low, high, force_side], axis=1)
    count = jnp.concatenate([count_ext[...], count_side], axis=1)
    root = jnp.sqrt(count * (1.0 / LEVELS))
    wide = COLS + 128

    def total(field):
        sideways = pltpu.roll(field, 1, 1) + pltpu.roll(field, wide - 1, 1)
        mixed = field + 0.5 * sideways
        return sideways + (pltpu.roll(mixed, 1, 0) + pltpu.roll(mixed, EXT - 1, 0))

    diag = damping + root * total(root)
    inverse = 1.0 / diag
    update = inverse * force * (1.0 / cheb_gamma)
    iterate = update
    omega = 2.0 / cheb_gamma
    for step in range(1, ITERS):
        residual = force - (diag * iterate - root * total(root * iterate))
        omega = 1.0 / (cheb_gamma - omega / (4.0 * cheb_alpha * cheb_alpha))
        update = omega * inverse * residual + (cheb_gamma * omega - 1.0) * update
        iterate = iterate + update
    out[...] = iterate[8 : 8 + ROWS, 0:COLS]
    save_cols.wait()


def final(*args):
    return pl.pallas_call(
        final_kernel,
        out_shape=(shape(2, LEVELS, ROWS, COLS), shape(ROWS, COLS)),
        in_specs=[ANY] + [VMEM] * 7,
        out_specs=(ANY, VMEM),
        scratch_shapes=[
            pltpu.VMEM((LEVELS, ROWS, 128), F32),
            pltpu.SemaphoreType.DMA,
        ],
        input_output_aliases={0: 0},
        compiler_params=params(LIMIT_COLUMNS),
        name="final",
    )(*args)


def shift(array, axis, step):
    count = lax.axis_size(axis)
    return lax.ppermute(array, axis, [(i, (i + step) % count) for i in range(count)])


def local(
    thermal_departure,
    current_speeds,
    mixing_coefficient,
    seawater_indicator,
    submerged_layer_tally,
    rainfall_runoff_input,
):
    count, to_east, to_west, to_north, to_south = pack(
        *(
            pltpu.with_memory_space_constraint(x, pltpu.HBM)
            for x in (
                thermal_departure, current_speeds, seawater_indicator, submerged_layer_tally
            )
        )
    )
    south = shift(to_north, "gy", 1)
    north = shift(to_south, "gy", -1)
    west = shift(to_east, "gx", 1)
    east = shift(to_west, "gx", -1)
    inside = interior(thermal_departure, current_speeds, mixing_coefficient, count)
    outside, own_east, own_west = outer(
        *inside, count, rainfall_runoff_input, to_east, to_west, to_north, to_south,
        west, east, south, north,
    )
    from_west = shift(own_east, "gx", 1)
    from_east = shift(own_west, "gx", -1)
    solved, u_new, v_low, v_high, force, q_col, sides = middle(
        *inside, count, rainfall_runoff_input, to_north, to_south,
        west, east, south, north, outside, own_west,
    )
    force_ext, count_ext, sides_ext, north_edge, south_edge = edges(
        force, sides, q_col, count, west, east, own_east, own_west, from_west, from_east
    )
    from_south = shift(north_edge, "gy", 1)
    from_north = shift(south_edge, "gy", -1)
    temp_next, speeds = writer(
        outside, solved, u_new, v_low, from_east, count, east
    )
    velocity_next, surface = final(
        speeds, v_high, count, force_ext, count_ext, sides_ext, from_south, from_north,
    )
    return (temp_next, velocity_next, surface)


def solution(mesh):
    placed = (
        P(None, "gx", "gy"),
        P(None, None, "gx", "gy"),
        P(None, "gx", "gy"),
        P("gx", "gy"),
        P("gx", "gy"),
        P("gx", "gy"),
    )
    return jax.shard_map(
        local,
        mesh=mesh,
        in_specs=placed,
        out_specs=(P(None, "gx", "gy"), P(None, None, "gx", "gy"), P("gx", "gy")),
        check_vma=False,
    )
```

```python
import jax
import jax.numpy as jnp
from jax import lax
from jax.experimental import pallas as pl
from jax.experimental.pallas import tpu as pltpu
from jax.sharding import PartitionSpec as P

ITERS = 6
Y_ROWS = 184
LIMIT_PACK = 12
LIMIT_INTERIOR = 8
LIMIT_COLUMNS = 12
LEVELS = 40
ROWS = 64
COLS = 256
BLOCKS = ROWS // 8
CHUNK = 20
CHUNKS = LEVELS // CHUNK

damping = 0.05
lower_bound = 0.02
upper_bound = 2.0
cheb_alpha = 2.0 / (upper_bound - lower_bound)
cheb_gamma = (upper_bound + lower_bound) / 2.0
advect_scale = 0.4
force_scale = 4.0
source_scale = 0.5
divergence_scale = 4.0
PRESS = force_scale / LEVELS
DIVERGE = divergence_scale / LEVELS

VMEM = pl.BlockSpec(memory_space=pltpu.VMEM)
ANY = pl.BlockSpec(memory_space=pl.ANY)
HBM = pl.BlockSpec(memory_space=pltpu.HBM)
F32 = jnp.float32
TILES = [(b, h) for b in range(BLOCKS) for h in range(2)]


def shape(*dims):
    return jax.ShapeDtypeStruct(dims, F32)


def params(mebibytes=40):
    return pltpu.CompilerParams(vmem_limit_bytes=int(mebibytes * 1024 * 1024))


def lane_id(rows=8):
    return lax.broadcasted_iota(jnp.int32, (rows, 128), 1)


def row_id():
    return lax.broadcasted_iota(jnp.int32, (8, 128), 0)


def rows_of(b):
    return slice(8 * b, 8 * b + 8)


def lanes_of(h):
    return slice(128 * h, 128 * h + 128)


def odd_place(axis):
    return lax.axis_index(axis) % 2 == 1


def sort_out(axis, lower, upper):
    odd = odd_place(axis)
    return jnp.where(odd, lower, upper), jnp.where(odd, upper, lower)


def sort_in(axis, even_pair, odd_pair):
    odd = odd_place(axis)
    return jnp.where(odd, even_pair, odd_pair), jnp.where(odd, odd_pair, even_pair)


def tiles_of(ref, *lead):
    return {(b, h): ref[(*lead, rows_of(b), lanes_of(h))] for b, h in TILES}


def next_row(x, after, last):
    turned = {t: pltpu.roll(x[t], 7, 0) for t in TILES}
    return {
        (b, h): jnp.where(last, after[h] if b == BLOCKS - 1 else turned[b + 1, h], turned[b, h])
        for b, h in TILES
    }


def prev_row(x, before, first):
    turned = {t: pltpu.roll(x[t], 1, 0) for t in TILES}
    return {
        (b, h): jnp.where(first, before[h] if b == 0 else turned[b - 1, h], turned[b, h])
        for b, h in TILES
    }


def next_col(x, after, last):
    turned = {t: pltpu.roll(x[t], 127, 1) for t in TILES}
    return {
        (b, h): jnp.where(last, after[b] if h == 1 else turned[b, 1], turned[b, h])
        for b, h in TILES
    }


def prev_col(x, before, first):
    turned = {t: pltpu.roll(x[t], 1, 1) for t in TILES}
    return {
        (b, h): jnp.where(first, before[b] if h == 0 else turned[b, 0], turned[b, h])
        for b, h in TILES
    }


def spread(ref, k, h):
    return jnp.broadcast_to(ref[h, pl.ds(k, 1), :], (8, 128))


def pack_kernel(
    temp, speeds, sea_in, tally_in,
    near, count_out, to_east, to_west, to_north, to_south, y_odd, y_even, x_odd, x_even,
    v_high, u_end, sea, tally, sems, part_sems,
):
    first = [
        pltpu.make_async_copy(sea_in, sea, sems.at[0]),
        pltpu.make_async_copy(tally_in, tally, sems.at[1]),
    ]
    parts = []
    for c in range(CHUNKS):
        part = pl.ds(c * CHUNK, CHUNK)
        parts.append(
            (
                pltpu.make_async_copy(temp.at[part], near.at[part], part_sems.at[0, c]),
                pltpu.make_async_copy(
                    speeds.at[1, part, :, pl.ds(128, 128)], v_high.at[part], part_sems.at[1, c]
                ),
            )
        )
    last = pltpu.make_async_copy(speeds.at[0, :, pl.ds(ROWS - 8, 8), :], u_end, sems.at[2])
    for copy in first:
        copy.start()
    for pair in parts:
        for copy in pair:
            copy.start()
    last.start()

    for copy in first:
        copy.wait()
    latitude = lax.axis_index("gy") * COLS + lax.broadcasted_iota(jnp.int32, (ROWS, COLS), 1)
    inner = (latitude > 0) & (latitude < lax.axis_size("gy") * COLS - 1)
    count = jnp.where(inner & (sea[...] == 1), tally[...], 0).astype(F32)
    count_out[...] = count
    for h in range(2):
        to_east[h, 80:86, :] = count[ROWS - 6 :, lanes_of(h)]
        to_east[h, 86:88, :] = jnp.zeros((2, 128), F32)
        to_west[h, 40:46, :] = count[:6, lanes_of(h)]
        to_west[h, 46:88, :] = jnp.zeros((42, 128), F32)
    lane = lane_id()
    low, high = [], []
    for b in range(BLOCKS):
        low.append(pltpu.roll(count[rows_of(b), :128], 40, 1))
        high.append(pltpu.roll(count[rows_of(b), 128:], (80 - 127) % 128, 1))

    for c in range(CHUNKS):
        parts[c][0].wait()
        parts[c][1].wait()
        for k in range(c * CHUNK, (c + 1) * CHUNK):
            for b in range(BLOCKS):
                rows = rows_of(b)
                low[b] = jnp.where(lane == k, pltpu.roll(near[k, rows, :128], k, 1), low[b])
                high[b] = jnp.where(lane == k, pltpu.roll(near[k, rows, 128:], k + 1, 1), high[b])
                high[b] = jnp.where(
                    lane == k + 40, pltpu.roll(v_high[k, rows, :], k + 41, 1), high[b]
                )
        levels = slice(c * CHUNK, (c + 1) * CHUNK)
        for h in range(2):
            to_west[h, levels, :] = near[levels, 0, lanes_of(h)]
            to_east[h, levels, :] = near[levels, ROWS - 1, lanes_of(h)]
    for b in range(BLOCKS):
        to_south[rows_of(b), :] = low[b]
        to_north[rows_of(b), :] = high[b]
        y_even[rows_of(b), :], y_odd[rows_of(b), :] = sort_out("gy", low[b], high[b])
    y_even[ROWS:, :] = jnp.zeros((Y_ROWS - ROWS, 128), F32)
    y_odd[ROWS:, :] = jnp.zeros((Y_ROWS - ROWS, 128), F32)
    last.wait()
    for h in range(2):
        to_east[h, 40:80, :] = u_end[:, 7, lanes_of(h)]
    x_even[...], x_odd[...] = sort_out("gx", to_west[...], to_east[...])


def pack(*args):
    return pl.pallas_call(
        pack_kernel,
        out_shape=(
            shape(LEVELS, ROWS, COLS), shape(ROWS, COLS),
            shape(2, 88, 128), shape(2, 88, 128), shape(ROWS, 128), shape(ROWS, 128),
            shape(Y_ROWS, 128), shape(Y_ROWS, 128), shape(2, 88, 128), shape(2, 88, 128),
        ),
        in_specs=[HBM] * 4,
        out_specs=(VMEM,) * 10,
        scratch_shapes=[
            pltpu.VMEM((LEVELS, ROWS, 128), F32),
            pltpu.VMEM((LEVELS, 8, COLS), F32),
            pltpu.VMEM((ROWS, COLS), jnp.int32),
            pltpu.VMEM((ROWS, COLS), jnp.int32),
            pltpu.SemaphoreType.DMA((3,)),
            pltpu.SemaphoreType.DMA((2, CHUNKS)),
        ],
        compiler_params=params(LIMIT_PACK),
        name="pack",
    )(*args)


UNROLL_IN = 4
UNROLL_FWD = 20
UNROLL_BACK = 20
UNROLL_MOM = 5


def interior_kernel(
    tb, speeds, mb, count,
    source_out, inverse_out, link_out,
    east_lim, north_lim,
):
    lane, row = lane_id(), row_id()
    first_row, last_row = row == 0, row == 7
    first_lane, last_lane = lane == 0, lane == 127
    zero = jnp.zeros((8, 128), F32)
    pair = range(2)

    counts = tiles_of(count)
    ahead = next_row(counts, [zero, zero], last_row)
    for b, h in TILES:
        east_lim[rows_of(b), lanes_of(h)] = jnp.minimum(counts[b, h], ahead[b, h])
    ahead = next_col(counts, [zero] * BLOCKS, last_lane)
    for b, h in TILES:
        north_lim[rows_of(b), lanes_of(h)] = jnp.minimum(counts[b, h], ahead[b, h])

    def level_step(k, factors, links):
        level = k.astype(F32)
        below_at = jnp.minimum(k + 1, LEVELS - 1)
        t_next = [tb[k, rows_of(0), lanes_of(h)] for h in pair]
        turned_next = [pltpu.roll(t_next[h], 7, 0) for h in pair]
        flux_turned = [zero, zero]
        new_factors, new_links = [], []
        for b in range(BLOCKS):
            rows = rows_of(b)
            t, turned = t_next, turned_next
            if b < BLOCKS - 1:
                t_next = [tb[k, rows_of(b + 1), lanes_of(h)] for h in pair]
                turned_next = [pltpu.roll(t_next[h], 7, 0) for h in pair]
            u = [speeds[0, k, rows, lanes_of(h)] for h in pair]
            v = [speeds[1, k, rows, lanes_of(h)] for h in pair]
            change = []
            for h in pair:
                ahead = jnp.where(last_row, turned_next[h], turned[h])
                flux = jnp.where(level < east_lim[rows, lanes_of(h)], u[h], 0.0) * jnp.where(
                    u[h] > 0.0, t[h], ahead
                )
                flux_before, flux_turned[h] = flux_turned[h], pltpu.roll(flux, 1, 0)
                change.append(flux - jnp.where(first_row, flux_before, flux_turned[h]))
            left = [pltpu.roll(t[h], 127, 1) for h in pair]
            ahead = [jnp.where(last_lane, left[1], left[0]), left[1]]
            flux = [
                jnp.where(level < north_lim[rows, lanes_of(h)], v[h], 0.0)
                * jnp.where(v[h] > 0.0, t[h], ahead[h])
                for h in pair
            ]
            right = [pltpu.roll(flux[h], 1, 1) for h in pair]
            behind = [jnp.where(first_lane, 0.0, right[0]), jnp.where(first_lane, right[0], right[1])]
            for h in pair:
                n = 2 * b + h
                at = (k, rows, lanes_of(h))
                wet = count[rows, lanes_of(h)]
                total = change[h] + (flux[h] - behind[h])
                source_out[at] = t[h] - jnp.where(level < wet, advect_scale * total, 0.0)
                a = links[n]
                below = jnp.where(
                    level + 1.0 < wet, mb[below_at, rows, lanes_of(h)], 0.0
                )
                pivot = (1.0 + below) + (a - a * factors[n])
                inverse = pl.reciprocal(pivot, approx=True)
                inverse = inverse * (2.0 - pivot * inverse)
                inverse_out[at] = inverse
                link_out[at] = a
                new_factors.append(below * inverse)
                new_links.append(below)
        return tuple(new_factors), tuple(new_links)

    def step(m, carry):
        for n in range(UNROLL_IN):
            carry = level_step(m * UNROLL_IN + n, *carry)
        return carry

    blank = tuple(zero for _ in TILES)
    lax.fori_loop(0, LEVELS // UNROLL_IN, step, (blank, blank))


def interior(temp, speeds, mix, count):
    block = shape(LEVELS, ROWS, COLS)
    return pl.pallas_call(
        interior_kernel,
        out_shape=(block,) * 3,
        in_specs=[VMEM] * 4,
        out_specs=(VMEM,) * 3,
        scratch_shapes=[
            pltpu.VMEM((ROWS, COLS), F32), pltpu.VMEM((ROWS, COLS), F32),
        ],
        cost_estimate=pl.CostEstimate(
            flops=30 * LEVELS * ROWS * COLS, bytes_accessed=16 * LEVELS * ROWS * COLS,
            transcendentals=0,
        ),
        compiler_params=params(LIMIT_INTERIOR),
        name="interior",
    )(temp, speeds, mix, count)


OUTER = (0, BLOCKS - 1)
MIDDLE = tuple(range(1, BLOCKS - 1))


def face_limits(
    blocks, count, west, east, south, north, east_lim, north_lim, south_lim, west_lim
):
    lane, row = lane_id(), row_id()
    last_row, last_lane = row == 7, lane == 127
    counts = tiles_of(count)
    pair = range(2)
    for h in pair:
        before = jnp.broadcast_to(west[h, 85:86, :], (8, 128))
        west_lim[:, lanes_of(h)] = jnp.minimum(counts[0, h], before)
        for b in blocks:
            if b == BLOCKS - 1:
                after = jnp.broadcast_to(east[h, 40:41, :], (8, 128))
            else:
                after = pltpu.roll(counts[b + 1, h], 7, 0)
            ahead = jnp.where(last_row, after, pltpu.roll(counts[b, h], 7, 0))
            east_lim[rows_of(b), lanes_of(h)] = jnp.minimum(counts[b, h], ahead)
    for b in blocks:
        rows = rows_of(b)
        left = [pltpu.roll(counts[b, h], 127, 1) for h in pair]
        left.append(pltpu.roll(north[rows, :], 127 - 40, 1))
        for h in pair:
            ahead = jnp.where(last_lane, left[h + 1], left[h])
            north_lim[rows, lanes_of(h)] = jnp.minimum(counts[b, h], ahead)
        south_lim[rows, :] = jnp.minimum(counts[b, 0], pltpu.roll(south[rows, :], 128 - 80, 1))


def column_fluxes(
    blocks, own_north, own_south, south, north, south_lim, north_lim, col_low, col_high
):
    depth = lane_id().astype(F32)
    for b in blocks:
        rows = rows_of(b)
        limit = jnp.broadcast_to(south_lim[rows, 0:1], (8, 128))
        speed = pltpu.roll(south[rows, :], 128 - 40, 1)
        col_low[rows, :] = (
            advect_scale
            * jnp.where(depth < limit, speed, 0.0)
            * jnp.where(speed > 0.0, south[rows, :], own_south[rows, :])
        )
        limit = jnp.broadcast_to(north_lim[rows, COLS - 1 : COLS], (8, 128))
        speed = pltpu.roll(own_north[rows, :], 128 - 40, 1)
        col_high[rows, :] = (
            -advect_scale
            * jnp.where(depth < limit, speed, 0.0)
            * jnp.where(speed > 0.0, own_north[rows, :], north[rows, :])
        )


def row_fluxes(own_east, own_west, west, east, west_lim, east_lim, row_low, row_high):
    depth = lax.broadcasted_iota(jnp.int32, (LEVELS, 128), 0).astype(F32)
    for h in range(2):
        speed = west[h, 40:80, :]
        row_low[h] = (
            advect_scale
            * jnp.where(depth < west_lim[0:1, lanes_of(h)], speed, 0.0)
            * jnp.where(speed > 0.0, west[h, 0:40, :], own_west[h, 0:40, :])
        )
        speed = own_east[h, 40:80, :]
        row_high[h] = (
            -advect_scale
            * jnp.where(depth < east_lim[ROWS - 1 : ROWS, lanes_of(h)], speed, 0.0)
            * jnp.where(speed > 0.0, own_east[h, 0:40, :], east[h, 0:40, :])
        )


def solve(blocks, place, source, inverse, link, col_low, col_high, row_low, row_high, solved):
    lane, row = lane_id(), row_id()
    first_row, last_row = row == 0, row == 7
    first_lane, last_lane = lane == 0, lane == 127
    zero = jnp.zeros((8, 128), F32)
    pair = range(2)

    def forward(k, values):
        out = []
        for n, b in enumerate(blocks):
            rows = rows_of(b)
            add = [
                jnp.where(first_lane, pltpu.roll(col_low[rows, :], 128 - k, 1), 0.0),
                jnp.where(last_lane, pltpu.roll(col_high[rows, :], 127 - k, 1), 0.0),
            ]
            for h in pair:
                at = (k, rows, lanes_of(h))
                total = source[at] + add[h]
                if b == 0:
                    total = total + jnp.where(first_row, spread(row_low, k, h), 0.0)
                if b == BLOCKS - 1:
                    total = total + jnp.where(last_row, spread(row_high, k, h), 0.0)
                value = (total + link[at] * values[2 * n + h]) * inverse[at]
                solved[k, place(b), lanes_of(h)] = value
                out.append(value)
        return tuple(out)

    blank = (zero,) * (2 * len(blocks))

    def forward_step(m, values):
        for n in range(UNROLL_FWD):
            values = forward(m * UNROLL_FWD + n, values)
        return values

    lax.fori_loop(0, LEVELS // UNROLL_FWD, forward_step, blank)

    def back_step(m, linked):
        for n in range(UNROLL_BACK):
            k = LEVELS - 1 - m * UNROLL_BACK - n
            out = []
            for i, below in zip([(b, h) for b in blocks for h in pair], linked):
                at = (k, rows_of(i[0]), lanes_of(i[1]))
                to = (k, place(i[0]), lanes_of(i[1]))
                value = solved[to] + inverse[at] * below
                solved[to] = value
                out.append(link[at] * value)
            linked = tuple(out)
        return linked

    lax.fori_loop(0, LEVELS // UNROLL_BACK, back_step, blank)


def row_face_sum(west_lim, q_rows):
    depth = lax.broadcasted_iota(jnp.int32, (LEVELS, 128), 0).astype(F32)
    out = []
    for h in range(2):
        part = jnp.where(depth < west_lim[0:1, lanes_of(h)], PRESS * q_rows(h), 0.0)
        out.append(jnp.broadcast_to(jnp.sum(part, axis=0, keepdims=True), (8, 128)))
    return out


def col_face_sum(rows, south_lim, q_col):
    limit = jnp.broadcast_to(south_lim[rows, 0:1], (8, 128))
    part = jnp.where(lane_id().astype(F32) < limit, PRESS * q_col[rows, :], 0.0)
    return jnp.broadcast_to(jnp.sum(part, axis=1, keepdims=True), (8, 128))


def momentum(
    blocks, values, following, speeds, east_lim, north_lim, run, u_sum, v_sum, q_col,
    keep_u, keep_v, keep_row,
):
    lane, row = lane_id(), row_id()
    last_row, last_lane = row == 7, lane == 127
    zero = jnp.zeros((8, 128), F32)
    pair = range(2)
    many = range(UNROLL_MOM)
    for b in blocks:
        run[rows_of(b), :] = jnp.zeros((8, COLS), F32)
        u_sum[rows_of(b), :] = jnp.zeros((8, COLS), F32)
        v_sum[rows_of(b), :] = jnp.zeros((8, COLS), F32)
        q_col[rows_of(b), :] = zero

    def step(m, _):
        first = m * UNROLL_MOM
        levels = [first + n for n in many]
        depths = [k.astype(F32) for k in levels]

        def running(b):
            out = []
            for h in pair:
                at = (rows_of(b), lanes_of(h))
                total = run[at]
                qs = []
                for k in levels:
                    half = 0.5 * values(k, b, h)
                    qs.append(total + half)
                    total = qs[-1] + half
                run[at] = total
                out.append(qs)
            return out

        q_next = None
        for b in blocks:
            rows = rows_of(b)
            if q_next is None:
                q = running(b)
                turned = [[pltpu.roll(x, 7, 0) for x in q[h]] for h in pair]
            else:
                q, turned = q_next, turned_next
            if b == 0:
                for h in pair:
                    for n in many:
                        keep_row(levels[n], h, q[h][n][0:1])
            if following(b):
                q_next = running(b + 1)
                turned_next = [[pltpu.roll(x, 7, 0) for x in q_next[h]] for h in pair]
            else:
                q_next, turned_next = None, [[zero] * UNROLL_MOM] * 2
            left = [[pltpu.roll(x, 127, 1) for x in q[h]] for h in pair]
            column = q_col[rows, :]
            for n in many:
                column = jnp.where(lane == levels[n], pltpu.roll(q[0][n], levels[n], 1), column)
            q_col[rows, :] = column
            for h in pair:
                at = (rows, lanes_of(h))
                limit = east_lim[at]
                total = u_sum[at]
                for n in many:
                    ahead = jnp.where(last_row, turned_next[h][n], turned[h][n])
                    speed = jnp.where(
                        depths[n] < limit, speeds[(0, levels[n], *at)] - PRESS * (q[h][n] - ahead), 0.0
                    )
                    keep_u(levels[n], b, h, speed)
                    total = total + speed
                u_sum[at] = total
                limit = north_lim[at]
                total = v_sum[at]
                for n in many:
                    ahead = jnp.where(last_lane, left[1][n] if h == 0 else 0.0, left[h][n])
                    speed = jnp.where(
                        depths[n] < limit, speeds[(1, levels[n], *at)] - PRESS * (q[h][n] - ahead), 0.0
                    )
                    keep_v(levels[n], b, h, speed)
                    total = total + speed
                v_sum[at] = total
        return 0

    lax.fori_loop(0, LEVELS // UNROLL_MOM, step, 0)


def forcing(blocks, u_sum, v_sum, row_sum, south_lim, q_col, count, rain, keep):
    lane, row = lane_id(), row_id()
    first_row, first_lane, last_lane = row == 0, lane == 0, lane == 127
    pair = range(2)
    for b in blocks:
        rows = rows_of(b)
        col_sum = col_face_sum(rows, south_lim, q_col)
        u = [u_sum[rows, lanes_of(h)] for h in pair]
        v = [v_sum[rows, lanes_of(h)] for h in pair]
        right = [pltpu.roll(v[h], 1, 1) for h in pair]
        v_before = [
            jnp.where(first_lane, col_sum, right[0]), jnp.where(first_lane, right[0], right[1])
        ]
        tiles = []
        for h in pair:
            at = (rows, lanes_of(h))
            if b == 0:
                before = row_sum[h]
            else:
                before = pltpu.roll(u_sum[rows_of(b - 1), lanes_of(h)], 1, 0)
            u_before = jnp.where(first_row, before, pltpu.roll(u[h], 1, 0))
            divergence = (u[h] - u_before) + (v[h] - v_before[h])
            tiles.append(
                jnp.where(count[at] > 0.0, source_scale * rain[at] - DIVERGE * divergence, 0.0)
            )
        side = jnp.where(first_lane, right[1], jnp.where(last_lane, col_sum, 0.0))
        keep(b, tiles, side)


def outer_kernel(
    source, inverse, link, speeds, count, rain, own_east, own_west, own_north, own_south,
    y_odd_in, y_even_in, x_odd_in, x_even_in,
    solved, to_east, to_west, x_odd, x_even, west, east, south, north,
    row_low, row_high, col_low, col_high, east_lim, north_lim, south_lim, west_lim,
    run, u_sum, v_sum, q_col,
):
    west[...], east[...] = sort_in("gx", x_even_in[...], x_odd_in[...])
    south[...], north[...] = sort_in("gy", y_even_in[0:ROWS, :], y_odd_in[0:ROWS, :])
    face_limits(
        OUTER, count, west, east, south, north, east_lim, north_lim, south_lim, west_lim
    )
    row_fluxes(own_east, own_west, west, east, west_lim, east_lim, row_low, row_high)
    column_fluxes(
        OUTER, own_north, own_south, south, north, south_lim, north_lim, col_low, col_high
    )

    def place(b):
        return slice(0, 8) if b == 0 else slice(8, 16)

    solve(OUTER, place, source, inverse, link, col_low, col_high, row_low, row_high, solved)

    def keep_row(k, h, value):
        to_west[pl.ds(24 + 40 * h + k, 1), :] = value

    def drop(*args):
        pass

    momentum(
        OUTER, lambda k, b, h: solved[k, place(b), lanes_of(h)], lambda b: False,
        speeds, east_lim, north_lim, run, u_sum, v_sum, q_col, drop, drop, keep_row,
    )
    row_sum = row_face_sum(west_lim, lambda h: to_west[24 + 40 * h : 64 + 40 * h, :])
    u_sum[rows_of(BLOCKS - 2), :] = jnp.zeros((8, COLS), F32)

    def keep(b, tiles, side):
        for h in range(2):
            if b == 0:
                to_west[rows_of(h), :] = tiles[h]
                to_west[8 * h + 5 : 8 * h + 6, :] = row_sum[h][0:1]
            else:
                to_east[rows_of(h), :] = pltpu.roll(tiles[h], 5, 0)
                to_east[8 * h + 5 : 8 * h + 6, :] = u_sum[ROWS - 1 : ROWS, lanes_of(h)]
        if b == 0:
            to_west[16:24, :] = side
        else:
            to_east[16:24, :] = pltpu.roll(side, 5, 0)

    forcing(OUTER, u_sum, v_sum, row_sum, south_lim, q_col, count, rain, keep)
    to_east[24:104, :] = jnp.zeros((80, 128), F32)
    x_even[...], x_odd[...] = sort_out("gx", to_west[...], to_east[...])


def outer(*args):
    plane = pltpu.VMEM((ROWS, COLS), F32)
    strip = pltpu.VMEM((ROWS, 128), F32)
    levels = pltpu.VMEM((2, LEVELS, 128), F32)
    return pl.pallas_call(
        outer_kernel,
        out_shape=(shape(LEVELS, 16, COLS),)
        + (shape(104, 128),) * 4
        + (shape(2, 88, 128),) * 2
        + (shape(ROWS, 128),) * 2,
        in_specs=[VMEM] * 14,
        out_specs=(VMEM,) * 9,
        scratch_shapes=[
            levels, levels, strip, strip, plane, plane, strip, pltpu.VMEM((8, COLS), F32),
            plane, plane, plane, strip,
        ],
        compiler_params=params(LIMIT_COLUMNS),
        name="outer",
    )(*args)


def middle_kernel(
    source, inverse, link, speeds, count, rain, own_north, own_south,
    west, east, south, north, outside, own_west,
    solved, u_new, v_low, v_high, force_out, q_col, sides,
    col_low, col_high, east_lim, north_lim, south_lim, west_lim, run, u_sum, v_sum,
):
    every = tuple(range(BLOCKS))
    face_limits(
        every, count, west, east, south, north, east_lim, north_lim, south_lim, west_lim
    )
    column_fluxes(
        MIDDLE, own_north, own_south, south, north, south_lim, north_lim, col_low, col_high
    )

    def place(b):
        return rows_of(b - 1)

    solve(MIDDLE, place, source, inverse, link, col_low, col_high, None, None, solved)

    def values(k, b, h):
        if b == 0:
            return outside[k, 0:8, lanes_of(h)]
        if b == BLOCKS - 1:
            return outside[k, 8:16, lanes_of(h)]
        return solved[k, place(b), lanes_of(h)]

    def keep_u(k, b, h, speed):
        u_new[k, rows_of(b), lanes_of(h)] = speed

    def keep_v(k, b, h, speed):
        if h == 0:
            v_low[k, rows_of(b), :] = speed
        else:
            v_high[k, rows_of(b), :] = speed

    momentum(
        every, values, lambda b: b < BLOCKS - 1, speeds, east_lim, north_lim,
        run, u_sum, v_sum, q_col, keep_u, keep_v, lambda k, h, value: None,
    )
    row_sum = [
        jnp.broadcast_to(own_west[8 * h + 5 : 8 * h + 6, :], (8, 128)) for h in range(2)
    ]

    def keep(b, tiles, side):
        for h in range(2):
            force_out[rows_of(b), lanes_of(h)] = tiles[h]
        sides[rows_of(b), :] = side

    forcing(every, u_sum, v_sum, row_sum, south_lim, q_col, count, rain, keep)


def middle(*args):
    plane = pltpu.VMEM((ROWS, COLS), F32)
    strip = pltpu.VMEM((ROWS, 128), F32)
    half = shape(LEVELS, ROWS, 128)
    return pl.pallas_call(
        middle_kernel,
        out_shape=(
            shape(LEVELS, ROWS - 16, COLS), shape(LEVELS, ROWS, COLS), half, half,
            shape(ROWS, COLS), shape(ROWS, 128), shape(ROWS, 128),
        ),
        in_specs=[VMEM] * 14,
        out_specs=(VMEM,) * 7,
        scratch_shapes=[
            strip, strip, plane, plane, strip, pltpu.VMEM((8, COLS), F32), plane, plane, plane,
        ],
        cost_estimate=pl.CostEstimate(
            flops=30 * LEVELS * ROWS * COLS, bytes_accessed=16 * LEVELS * ROWS * COLS,
            transcendentals=0,
        ),
        compiler_params=params(LIMIT_COLUMNS),
        name="middle",
    )(*args)


def writer_kernel(
    outside, solved, u_new, v_low, from_east, count, east, temp_out, speeds_out, u_fix, sems
):
    copies = [
        (outside.at[:, pl.ds(0, 8), :], temp_out.at[:, pl.ds(0, 8), :]),
        (outside.at[:, pl.ds(8, 8), :], temp_out.at[:, pl.ds(ROWS - 8, 8), :]),
        (solved, temp_out.at[:, pl.ds(8, ROWS - 16), :]),
        (u_new.at[:, pl.ds(0, ROWS - 8), :], speeds_out.at[0, :, pl.ds(0, ROWS - 8), :]),
        (v_low, speeds_out.at[1, :, :, pl.ds(0, 128)]),
        (u_fix, speeds_out.at[0, :, pl.ds(ROWS - 8, 8), :]),
    ]
    copies = [
        pltpu.make_async_copy(origin, target, sems.at[n])
        for n, (origin, target) in enumerate(copies)
    ]
    for copy in copies[:-1]:
        copy.start()
    last_row = row_id() == 7
    for h in range(2):
        limit = jnp.minimum(
            count[ROWS - 8 :, lanes_of(h)], jnp.broadcast_to(east[h, 40:41, :], (8, 128))
        )
        limit = jnp.where(last_row, limit, 0.0)
        for k in range(LEVELS):
            at = 24 + 40 * h + k
            u_fix[k, :, lanes_of(h)] = u_new[k, ROWS - 8 :, lanes_of(h)] + jnp.where(
                float(k) < limit,
                PRESS * jnp.broadcast_to(from_east[at : at + 1, :], (8, 128)),
                0.0,
            )
    copies[-1].start()
    for copy in copies:
        copy.wait()


def writer(*args):
    return pl.pallas_call(
        writer_kernel,
        out_shape=(shape(LEVELS, ROWS, COLS), shape(2, LEVELS, ROWS, COLS)),
        in_specs=[VMEM] * 7,
        out_specs=(ANY, ANY),
        scratch_shapes=[
            pltpu.VMEM((LEVELS, 8, COLS), F32),
            pltpu.SemaphoreType.DMA((6,)),
        ],
        cost_estimate=pl.CostEstimate(
            flops=LEVELS * ROWS * COLS, bytes_accessed=12 * LEVELS * ROWS * COLS,
            transcendentals=0,
        ),
        compiler_params=params(LIMIT_COLUMNS),
        name="writer",
    )(*args)


EXT = ROWS + 16


def edges_kernel(
    force, sides, q_col, count, west, east_in, own_east, own_west, x_odd, x_even,
    force_ext, count_ext, sides_ext, y_odd, y_even, from_east, from_west, to_north, to_south,
):
    from_west[...], from_east[...] = sort_in("gx", x_even[...], x_odd[...])
    zeros8 = jnp.zeros((8, COLS), F32)
    count_ext[0:8, :] = zeros8
    for h in range(2):
        count_ext[2:8, lanes_of(h)] = west[h, 80:86, :]
    count_ext[8 : 8 + ROWS, :] = count[...]
    count_ext[8 + ROWS :, :] = zeros8
    for h in range(2):
        count_ext[8 + ROWS : 14 + ROWS, lanes_of(h)] = east_in[h, 40:46, :]
    sides_ext[0:8, :] = jnp.zeros((8, 128), F32)
    sides_ext[3:8, :] = from_west[16:21, :]
    sides_ext[8 : 8 + ROWS, :] = sides[...]
    sides_ext[8 + ROWS :, :] = jnp.zeros((8, 128), F32)
    sides_ext[8 + ROWS : 13 + ROWS, :] = from_east[16:21, :]
    force_ext[0:8, :] = zeros8
    for h in range(2):
        force_ext[3:8, lanes_of(h)] = from_west[8 * h : 8 * h + 5, :]
    force_ext[8 : 8 + ROWS, :] = force[...]
    force_ext[8 + ROWS :, :] = zeros8
    for h in range(2):
        force_ext[8 + ROWS : 13 + ROWS, lanes_of(h)] = from_east[8 * h : 8 * h + 5, :]

    def add(at, sign, ref):
        for h in range(2):
            place = (slice(at, at + 1), lanes_of(h))
            force_ext[place] = force_ext[place] + jnp.where(
                count_ext[place] > 0.0, sign * DIVERGE * ref[8 * h + 5 : 8 * h + 6, :], 0.0
            )

    add(7, -1.0, own_west)
    add(8, 1.0, from_west)
    add(7 + ROWS, -1.0, from_east)
    add(8 + ROWS, 1.0, own_east)
    lane = lane_id(EXT)
    side = sides_ext[...]
    to_north[...] = jnp.where(
        lane >= 123,
        force_ext[:, 128:],
        jnp.where(lane == 0, side, pltpu.roll(count_ext[:, 128:], 122, 1)),
    )
    to_south[...] = jnp.where(
        lane < 5,
        force_ext[:, :128],
        jnp.where(lane == 127, side, pltpu.roll(count_ext[:, :128], 8, 1)),
    )
    lane = lane_id(ROWS)
    to_south[8 : 8 + ROWS, :] = jnp.where(
        (lane >= 64) & (lane < 64 + LEVELS),
        pltpu.roll(q_col[...], 64, 1),
        to_south[8 : 8 + ROWS, :],
    )
    y_even[...], y_odd[...] = sort_out("gy", to_south[...], to_north[...])


def edges(*args):
    return pl.pallas_call(
        edges_kernel,
        out_shape=(
            shape(EXT, COLS), shape(EXT, COLS), shape(EXT, 128), shape(EXT, 128), shape(EXT, 128),
            shape(104, 128),
        ),
        in_specs=[VMEM] * 10,
        out_specs=(VMEM,) * 6,
        scratch_shapes=[
            pltpu.VMEM((104, 128), F32), pltpu.VMEM((EXT, 128), F32), pltpu.VMEM((EXT, 128), F32)
        ],
        compiler_params=params(LIMIT_COLUMNS),
        name="edges",
    )(*args)


def final_kernel(
    speeds, v_high, count,
    force_ext, count_ext, sides_ext, y_odd, y_even,
    speeds_out, out, v_fix, south, north, sem,
):
    south[...], north[...] = sort_in("gy", y_even[...], y_odd[...])
    last_lane = lane_id(8) == 127
    for b in range(BLOCKS):
        rows = rows_of(b)
        held = north[8 * b + 8 : 8 * b + 16, :]
        limit = jnp.minimum(count[rows, 128:], pltpu.roll(held, 127 - 8, 1))
        limit = jnp.where(last_lane, limit, 0.0)
        for k in range(LEVELS):
            v_fix[k, rows, :] = v_high[k, rows, :] + jnp.where(
                float(k) < limit, PRESS * pltpu.roll(held, 63 - k, 1), 0.0
            )
    save_cols = pltpu.make_async_copy(
        v_fix, speeds_out.at[1, :, :, pl.ds(128, 128)], sem
    )
    save_cols.start()
    lane = lane_id(EXT)
    count_side = jnp.where(
        lane >= 122,
        pltpu.roll(south[...], 6, 1),
        jnp.where(lane < 6, pltpu.roll(north[...], 120, 1), 0.0),
    )
    force_side = jnp.where(
        lane >= 123, south[...], jnp.where(lane < 5, north[...], 0.0)
    )
    side = sides_ext[...]
    low, high = force_ext[:, :128], force_ext[:, 128:]
    low = low + jnp.where(
        (lane == 0) & (count_ext[:, :128] > 0.0), DIVERGE * south[...], 0.0
    )
    high = high - jnp.where(
        (lane == 127) & (count_ext[:, 128:] > 0.0), DIVERGE * north[...], 0.0
    )
    force_side = force_side + jnp.where(
        (lane == 0) & (count_side > 0.0), DIVERGE * side, 0.0
    )
    force_side = force_side - jnp.where(
        (lane == 127) & (count_side > 0.0), DIVERGE * side, 0.0
    )
    force = jnp.concatenate([low, high, force_side], axis=1)
    count = jnp.concatenate([count_ext[...], count_side], axis=1)
    root = jnp.sqrt(count * (1.0 / LEVELS))
    wide = COLS + 128

    def total(field):
        sideways = pltpu.roll(field, 1, 1) + pltpu.roll(field, wide - 1, 1)
        mixed = field + 0.5 * sideways
        return sideways + (pltpu.roll(mixed, 1, 0) + pltpu.roll(mixed, EXT - 1, 0))

    diag = damping + root * total(root)
    inverse = 1.0 / diag
    update = inverse * force * (1.0 / cheb_gamma)
    iterate = update
    omega = 2.0 / cheb_gamma
    for step in range(1, ITERS):
        residual = force - (diag * iterate - root * total(root * iterate))
        omega = 1.0 / (cheb_gamma - omega / (4.0 * cheb_alpha * cheb_alpha))
        update = omega * inverse * residual + (cheb_gamma * omega - 1.0) * update
        iterate = iterate + update
    out[...] = iterate[8 : 8 + ROWS, 0:COLS]
    save_cols.wait()


def final(*args):
    return pl.pallas_call(
        final_kernel,
        out_shape=(shape(2, LEVELS, ROWS, COLS), shape(ROWS, COLS)),
        in_specs=[ANY] + [VMEM] * 7,
        out_specs=(ANY, VMEM),
        scratch_shapes=[
            pltpu.VMEM((LEVELS, ROWS, 128), F32),
            pltpu.VMEM((EXT, 128), F32), pltpu.VMEM((EXT, 128), F32),
            pltpu.SemaphoreType.DMA,
        ],
        input_output_aliases={0: 0},
        compiler_params=params(LIMIT_COLUMNS),
        name="final",
    )(*args)


def swap(array, axis, first):
    count = lax.axis_size(axis)
    pairs = []
    for low in range(first, count + first, 2):
        low, high = low % count, (low + 1) % count
        pairs += [(low, high), (high, low)]
    return lax.ppermute(array, axis, pairs)


def local(
    thermal_departure,
    current_speeds,
    mixing_coefficient,
    seawater_indicator,
    submerged_layer_tally,
    rainfall_runoff_input,
):
    near, count, to_east, to_west, to_north, to_south, y_odd, y_even, x_odd, x_even = pack(
        *(
            pltpu.with_memory_space_constraint(x, pltpu.HBM)
            for x in (
                thermal_departure, current_speeds, seawater_indicator, submerged_layer_tally
            )
        )
    )
    y_odd = swap(y_odd, "gy", 1)
    y_even = swap(y_even, "gy", 0)
    x_odd = swap(x_odd, "gx", 1)
    x_even = swap(x_even, "gx", 0)
    speeds, mixing = (
        pltpu.with_memory_space_constraint(x, pltpu.VMEM)
        for x in (current_speeds, mixing_coefficient)
    )
    inside = (*interior(near, speeds, mixing, count), speeds)
    outside, own_east, own_west, x_odd, x_even, west, east, south, north = outer(
        *inside, count, rainfall_runoff_input, to_east, to_west, to_north, to_south,
        y_odd, y_even, x_odd, x_even,
    )
    x_odd = swap(x_odd, "gx", 1)
    x_even = swap(x_even, "gx", 0)
    solved, u_new, v_low, v_high, force, q_col, sides = middle(
        *inside, count, rainfall_runoff_input, to_north, to_south,
        west, east, south, north, outside, own_west,
    )
    force_ext, count_ext, sides_ext, y_odd, y_even, from_east = edges(
        force, sides, q_col, count, west, east, own_east, own_west, x_odd, x_even
    )
    y_odd = swap(y_odd, "gy", 1)
    y_even = swap(y_even, "gy", 0)
    temp_next, stored = writer(
        outside, solved, u_new, v_low, from_east, count, east
    )
    velocity_next, surface = final(
        stored, v_high, count, force_ext, count_ext, sides_ext, y_odd, y_even,
    )
    return (temp_next, velocity_next, surface)


def solution(mesh):
    placed = (
        P(None, "gx", "gy"),
        P(None, None, "gx", "gy"),
        P(None, "gx", "gy"),
        P("gx", "gy"),
        P("gx", "gy"),
        P("gx", "gy"),
    )
    return jax.shard_map(
        local,
        mesh=mesh,
        in_specs=placed,
        out_specs=(P(None, "gx", "gy"), P(None, None, "gx", "gy"), P("gx", "gy")),
        check_vma=False,
    )
```

```python
import jax
import jax.numpy as jnp
from jax import lax
from jax.experimental import pallas as pl
from jax.experimental.pallas import tpu as pltpu
from jax.sharding import PartitionSpec as P

ITERS = 6
FIX_CHUNK = 20
COST = 10000
LIMIT_PACK = 12
LIMIT_INTERIOR = 8
LIMIT_COLUMNS = 12
LEVELS = 40
ROWS = 64
COLS = 256
BLOCKS = ROWS // 8
CHUNK = 20
CHUNKS = LEVELS // CHUNK

damping = 0.05
lower_bound = 0.02
upper_bound = 2.0
cheb_alpha = 2.0 / (upper_bound - lower_bound)
cheb_gamma = (upper_bound + lower_bound) / 2.0
advect_scale = 0.4
force_scale = 4.0
source_scale = 0.5
divergence_scale = 4.0
PRESS = force_scale / LEVELS
DIVERGE = divergence_scale / LEVELS

VMEM = pl.BlockSpec(memory_space=pltpu.VMEM)
ANY = pl.BlockSpec(memory_space=pl.ANY)
HBM = pl.BlockSpec(memory_space=pltpu.HBM)
F32 = jnp.float32
TILES = [(b, h) for b in range(BLOCKS) for h in range(2)]


def shape(*dims):
    return jax.ShapeDtypeStruct(dims, F32)


def params(mebibytes=40):
    return pltpu.CompilerParams(vmem_limit_bytes=int(mebibytes * 1024 * 1024))


def lane_id(rows=8):
    return lax.broadcasted_iota(jnp.int32, (rows, 128), 1)


def row_id():
    return lax.broadcasted_iota(jnp.int32, (8, 128), 0)


def rows_of(b):
    return slice(8 * b, 8 * b + 8)


def lanes_of(h):
    return slice(128 * h, 128 * h + 128)


def odd_place(axis):
    return lax.axis_index(axis) % 2 == 1


def sort_out(axis, lower, upper):
    odd = odd_place(axis)
    return jnp.where(odd, lower, upper), jnp.where(odd, upper, lower)


def sort_in(axis, even_pair, odd_pair):
    odd = odd_place(axis)
    return jnp.where(odd, even_pair, odd_pair), jnp.where(odd, odd_pair, even_pair)


def tiles_of(ref, *lead):
    return {(b, h): ref[(*lead, rows_of(b), lanes_of(h))] for b, h in TILES}


def next_row(x, after, last):
    turned = {t: pltpu.roll(x[t], 7, 0) for t in TILES}
    return {
        (b, h): jnp.where(last, after[h] if b == BLOCKS - 1 else turned[b + 1, h], turned[b, h])
        for b, h in TILES
    }


def prev_row(x, before, first):
    turned = {t: pltpu.roll(x[t], 1, 0) for t in TILES}
    return {
        (b, h): jnp.where(first, before[h] if b == 0 else turned[b - 1, h], turned[b, h])
        for b, h in TILES
    }


def next_col(x, after, last):
    turned = {t: pltpu.roll(x[t], 127, 1) for t in TILES}
    return {
        (b, h): jnp.where(last, after[b] if h == 1 else turned[b, 1], turned[b, h])
        for b, h in TILES
    }


def prev_col(x, before, first):
    turned = {t: pltpu.roll(x[t], 1, 1) for t in TILES}
    return {
        (b, h): jnp.where(first, before[b] if h == 0 else turned[b, 0], turned[b, h])
        for b, h in TILES
    }


def spread(ref, k, h):
    return jnp.broadcast_to(ref[h, pl.ds(k, 1), :], (8, 128))


def pack_kernel(
    temp, speeds, sea_in, tally_in,
    near, count_out, to_east, to_west, to_north, to_south, y_odd, y_even, x_odd, x_even,
    v_high, u_end, sea, tally, sems, part_sems,
):
    first = [
        pltpu.make_async_copy(sea_in, sea, sems.at[0]),
        pltpu.make_async_copy(tally_in, tally, sems.at[1]),
    ]
    parts = []
    for c in range(CHUNKS):
        part = pl.ds(c * CHUNK, CHUNK)
        parts.append(
            (
                pltpu.make_async_copy(temp.at[part], near.at[part], part_sems.at[0, c]),
                pltpu.make_async_copy(
                    speeds.at[1, part, :, pl.ds(128, 128)], v_high.at[part], part_sems.at[1, c]
                ),
            )
        )
    last = pltpu.make_async_copy(speeds.at[0, :, pl.ds(ROWS - 8, 8), :], u_end, sems.at[2])
    for copy in first:
        copy.start()
    for pair in parts:
        for copy in pair:
            copy.start()
    last.start()

    for copy in first:
        copy.wait()
    latitude = lax.axis_index("gy") * COLS + lax.broadcasted_iota(jnp.int32, (ROWS, COLS), 1)
    inner = (latitude > 0) & (latitude < lax.axis_size("gy") * COLS - 1)
    count = jnp.where(inner & (sea[...] == 1), tally[...], 0).astype(F32)
    count_out[...] = count
    for h in range(2):
        to_east[h, 80:86, :] = count[ROWS - 6 :, lanes_of(h)]
        to_east[h, 86:88, :] = jnp.zeros((2, 128), F32)
        to_west[h, 40:46, :] = count[:6, lanes_of(h)]
        to_west[h, 46:88, :] = jnp.zeros((42, 128), F32)
    lane = lane_id()
    low, high = [], []
    for b in range(BLOCKS):
        low.append(pltpu.roll(count[rows_of(b), :128], 40, 1))
        high.append(pltpu.roll(count[rows_of(b), 128:], (80 - 127) % 128, 1))

    for c in range(CHUNKS):
        parts[c][0].wait()
        parts[c][1].wait()
        for k in range(c * CHUNK, (c + 1) * CHUNK):
            for b in range(BLOCKS):
                rows = rows_of(b)
                low[b] = jnp.where(lane == k, pltpu.roll(near[k, rows, :128], k, 1), low[b])
                high[b] = jnp.where(lane == k, pltpu.roll(near[k, rows, 128:], k + 1, 1), high[b])
                high[b] = jnp.where(
                    lane == k + 40, pltpu.roll(v_high[k, rows, :], k + 41, 1), high[b]
                )
        levels = slice(c * CHUNK, (c + 1) * CHUNK)
        for h in range(2):
            to_west[h, levels, :] = near[levels, 0, lanes_of(h)]
            to_east[h, levels, :] = near[levels, ROWS - 1, lanes_of(h)]
    for b in range(BLOCKS):
        to_south[rows_of(b), :] = low[b]
        to_north[rows_of(b), :] = high[b]
        y_even[rows_of(b), :], y_odd[rows_of(b), :] = sort_out("gy", low[b], high[b])
    last.wait()
    for h in range(2):
        to_east[h, 40:80, :] = u_end[:, 7, lanes_of(h)]
    x_even[...], x_odd[...] = sort_out("gx", to_west[...], to_east[...])


def pack(*args):
    return pl.pallas_call(
        pack_kernel,
        out_shape=(
            shape(LEVELS, ROWS, COLS), shape(ROWS, COLS),
            shape(2, 88, 128), shape(2, 88, 128), shape(ROWS, 128), shape(ROWS, 128),
            shape(ROWS, 128), shape(ROWS, 128), shape(2, 88, 128), shape(2, 88, 128),
        ),
        in_specs=[HBM] * 4,
        out_specs=(VMEM,) * 10,
        scratch_shapes=[
            pltpu.VMEM((LEVELS, ROWS, 128), F32),
            pltpu.VMEM((LEVELS, 8, COLS), F32),
            pltpu.VMEM((ROWS, COLS), jnp.int32),
            pltpu.VMEM((ROWS, COLS), jnp.int32),
            pltpu.SemaphoreType.DMA((3,)),
            pltpu.SemaphoreType.DMA((2, CHUNKS)),
        ],
        compiler_params=params(LIMIT_PACK),
        name="pack",
    )(*args)


UNROLL_IN = 4
UNROLL_FWD = 20
UNROLL_BACK = 20
UNROLL_MOM = 5
UNROLL_OUT = 40


def interior_kernel(
    tb, speeds, mb, count,
    source_out, inverse_out, link_out,
    east_lim, north_lim,
):
    lane, row = lane_id(), row_id()
    first_row, last_row = row == 0, row == 7
    first_lane, last_lane = lane == 0, lane == 127
    zero = jnp.zeros((8, 128), F32)
    pair = range(2)

    counts = tiles_of(count)
    ahead = next_row(counts, [zero, zero], last_row)
    for b, h in TILES:
        east_lim[rows_of(b), lanes_of(h)] = jnp.minimum(counts[b, h], ahead[b, h])
    ahead = next_col(counts, [zero] * BLOCKS, last_lane)
    for b, h in TILES:
        north_lim[rows_of(b), lanes_of(h)] = jnp.minimum(counts[b, h], ahead[b, h])

    def level_step(k, factors, links, opens=None):
        level = k.astype(F32)
        below_at = jnp.minimum(k + 1, LEVELS - 1)
        t_next = [tb[k, rows_of(0), lanes_of(h)] for h in pair]
        turned_next = [pltpu.roll(t_next[h], 7, 0) for h in pair]
        flux_turned = [zero, zero]
        new_factors, new_links, new_opens = [], [], []
        for b in range(BLOCKS):
            rows = rows_of(b)
            t, turned = t_next, turned_next
            if b < BLOCKS - 1:
                t_next = [tb[k, rows_of(b + 1), lanes_of(h)] for h in pair]
                turned_next = [pltpu.roll(t_next[h], 7, 0) for h in pair]
            u = [speeds[0, k, rows, lanes_of(h)] for h in pair]
            v = [speeds[1, k, rows, lanes_of(h)] for h in pair]
            change = []
            for h in pair:
                ahead = jnp.where(last_row, turned_next[h], turned[h])
                flux = jnp.where(level < east_lim[rows, lanes_of(h)], u[h], 0.0) * jnp.where(
                    u[h] > 0.0, t[h], ahead
                )
                flux_before, flux_turned[h] = flux_turned[h], pltpu.roll(flux, 1, 0)
                change.append(flux - jnp.where(first_row, flux_before, flux_turned[h]))
            left = [pltpu.roll(t[h], 127, 1) for h in pair]
            ahead = [jnp.where(last_lane, left[1], left[0]), left[1]]
            flux = [
                jnp.where(level < north_lim[rows, lanes_of(h)], v[h], 0.0)
                * jnp.where(v[h] > 0.0, t[h], ahead[h])
                for h in pair
            ]
            right = [pltpu.roll(flux[h], 1, 1) for h in pair]
            behind = [jnp.where(first_lane, 0.0, right[0]), jnp.where(first_lane, right[0], right[1])]
            for h in pair:
                n = 2 * b + h
                at = (k, rows, lanes_of(h))
                wet = count[rows, lanes_of(h)]
                total = change[h] + (flux[h] - behind[h])
                open_here = level < wet if opens is None else opens[n]
                open_below = level + 1.0 < wet
                source_out[at] = t[h] - jnp.where(open_here, advect_scale * total, 0.0)
                a = links[n]
                below = jnp.where(open_below, mb[below_at, rows, lanes_of(h)], 0.0)
                pivot = (1.0 + below) + (a - a * factors[n])
                inverse = pl.reciprocal(pivot, approx=True)
                inverse = inverse * (2.0 - pivot * inverse)
                inverse_out[at] = inverse
                link_out[at] = a
                new_factors.append(below * inverse)
                new_links.append(below)
                new_opens.append(open_below)
        return tuple(new_factors), tuple(new_links), new_opens

    def step(m, carry):
        for n in range(UNROLL_IN):
            carry = level_step(m * UNROLL_IN + n, *carry)
        return carry[:2]

    blank = tuple(zero for _ in TILES)
    lax.fori_loop(0, LEVELS // UNROLL_IN, step, (blank, blank))


def interior(temp, speeds, mix, count):
    block = shape(LEVELS, ROWS, COLS)
    return pl.pallas_call(
        interior_kernel,
        out_shape=(block,) * 3,
        in_specs=[VMEM] * 4,
        out_specs=(VMEM,) * 3,
        scratch_shapes=[
            pltpu.VMEM((ROWS, COLS), F32), pltpu.VMEM((ROWS, COLS), F32),
        ],
        cost_estimate=pl.CostEstimate(
            flops=COST * LEVELS * ROWS * COLS, bytes_accessed=COST * LEVELS * ROWS * COLS,
            transcendentals=0,
        ),
        compiler_params=params(LIMIT_INTERIOR),
        name="interior",
    )(temp, speeds, mix, count)


OUTER = (0, BLOCKS - 1)
MIDDLE = tuple(range(1, BLOCKS - 1))


def face_limits(
    blocks, count, west, east, south, north, east_lim, north_lim, south_lim, west_lim
):
    lane, row = lane_id(), row_id()
    last_row, last_lane = row == 7, lane == 127
    counts = tiles_of(count)
    pair = range(2)
    for h in pair:
        before = jnp.broadcast_to(west[h, 85:86, :], (8, 128))
        west_lim[:, lanes_of(h)] = jnp.minimum(counts[0, h], before)
        for b in blocks:
            if b == BLOCKS - 1:
                after = jnp.broadcast_to(east[h, 40:41, :], (8, 128))
            else:
                after = pltpu.roll(counts[b + 1, h], 7, 0)
            ahead = jnp.where(last_row, after, pltpu.roll(counts[b, h], 7, 0))
            east_lim[rows_of(b), lanes_of(h)] = jnp.minimum(counts[b, h], ahead)
    for b in blocks:
        rows = rows_of(b)
        left = [pltpu.roll(counts[b, h], 127, 1) for h in pair]
        left.append(pltpu.roll(north[rows, :], 127 - 40, 1))
        for h in pair:
            ahead = jnp.where(last_lane, left[h + 1], left[h])
            north_lim[rows, lanes_of(h)] = jnp.minimum(counts[b, h], ahead)
        south_lim[rows, :] = jnp.minimum(counts[b, 0], pltpu.roll(south[rows, :], 128 - 80, 1))


def column_fluxes(
    blocks, own_north, own_south, south, north, south_lim, north_lim, col_low, col_high
):
    depth = lane_id().astype(F32)
    for b in blocks:
        rows = rows_of(b)
        limit = jnp.broadcast_to(south_lim[rows, 0:1], (8, 128))
        speed = pltpu.roll(south[rows, :], 128 - 40, 1)
        col_low[rows, :] = (
            advect_scale
            * jnp.where(depth < limit, speed, 0.0)
            * jnp.where(speed > 0.0, south[rows, :], own_south[rows, :])
        )
        limit = jnp.broadcast_to(north_lim[rows, COLS - 1 : COLS], (8, 128))
        speed = pltpu.roll(own_north[rows, :], 128 - 40, 1)
        col_high[rows, :] = (
            -advect_scale
            * jnp.where(depth < limit, speed, 0.0)
            * jnp.where(speed > 0.0, own_north[rows, :], north[rows, :])
        )


def row_fluxes(own_east, own_west, west, east, west_lim, east_lim, row_low, row_high):
    depth = lax.broadcasted_iota(jnp.int32, (LEVELS, 128), 0).astype(F32)
    for h in range(2):
        speed = west[h, 40:80, :]
        row_low[h] = (
            advect_scale
            * jnp.where(depth < west_lim[0:1, lanes_of(h)], speed, 0.0)
            * jnp.where(speed > 0.0, west[h, 0:40, :], own_west[h, 0:40, :])
        )
        speed = own_east[h, 40:80, :]
        row_high[h] = (
            -advect_scale
            * jnp.where(depth < east_lim[ROWS - 1 : ROWS, lanes_of(h)], speed, 0.0)
            * jnp.where(speed > 0.0, own_east[h, 0:40, :], east[h, 0:40, :])
        )


def solve(blocks, place, source, inverse, link, col_low, col_high, row_low, row_high, solved):
    lane, row = lane_id(), row_id()
    first_row, last_row = row == 0, row == 7
    first_lane, last_lane = lane == 0, lane == 127
    zero = jnp.zeros((8, 128), F32)
    pair = range(2)

    def forward(k, values):
        out = []
        for n, b in enumerate(blocks):
            rows = rows_of(b)
            add = [
                jnp.where(first_lane, pltpu.roll(col_low[rows, :], 128 - k, 1), 0.0),
                jnp.where(last_lane, pltpu.roll(col_high[rows, :], 127 - k, 1), 0.0),
            ]
            for h in pair:
                at = (k, rows, lanes_of(h))
                total = source[at] + add[h]
                if b == 0:
                    total = total + jnp.where(first_row, spread(row_low, k, h), 0.0)
                if b == BLOCKS - 1:
                    total = total + jnp.where(last_row, spread(row_high, k, h), 0.0)
                turn = inverse[at]
                value = total * turn + (link[at] * turn) * values[2 * n + h]
                solved[k, place(b), lanes_of(h)] = value
                out.append(value)
        return tuple(out)

    blank = (zero,) * (2 * len(blocks))

    def forward_step(m, values):
        for n in range(UNROLL_FWD):
            values = forward(m * UNROLL_FWD + n, values)
        return values

    lax.fori_loop(0, LEVELS // UNROLL_FWD, forward_step, blank)

    def back_step(m, below):
        for n in range(UNROLL_BACK):
            k = LEVELS - 1 - m * UNROLL_BACK - n
            below_at = jnp.minimum(k + 1, LEVELS - 1)
            out = []
            for i, value in zip([(b, h) for b in blocks for h in pair], below):
                at = (rows_of(i[0]), lanes_of(i[1]))
                to = (k, place(i[0]), lanes_of(i[1]))
                value = solved[to] + (inverse[(k, *at)] * link[(below_at, *at)]) * value
                solved[to] = value
                out.append(value)
            below = tuple(out)
        return below

    lax.fori_loop(0, LEVELS // UNROLL_BACK, back_step, blank)


def row_face_sum(west_lim, q_rows):
    depth = lax.broadcasted_iota(jnp.int32, (LEVELS, 128), 0).astype(F32)
    out = []
    for h in range(2):
        part = jnp.where(depth < west_lim[0:1, lanes_of(h)], PRESS * q_rows(h), 0.0)
        out.append(jnp.broadcast_to(jnp.sum(part, axis=0, keepdims=True), (8, 128)))
    return out


def col_face_sum(rows, south_lim, q_col):
    limit = jnp.broadcast_to(south_lim[rows, 0:1], (8, 128))
    part = jnp.where(lane_id().astype(F32) < limit, PRESS * q_col[rows, :], 0.0)
    return jnp.broadcast_to(jnp.sum(part, axis=1, keepdims=True), (8, 128))


def momentum(
    blocks, values, following, speeds, east_lim, north_lim, run, u_sum, v_sum, q_col,
    keep_u, keep_v, keep_row, unroll,
):
    lane, row = lane_id(), row_id()
    last_row, last_lane = row == 7, lane == 127
    zero = jnp.zeros((8, 128), F32)
    pair = range(2)
    many = range(unroll)
    for b in blocks:
        run[rows_of(b), :] = jnp.zeros((8, COLS), F32)
        u_sum[rows_of(b), :] = jnp.zeros((8, COLS), F32)
        v_sum[rows_of(b), :] = jnp.zeros((8, COLS), F32)
        q_col[rows_of(b), :] = zero

    def step(m, _):
        first = m * unroll
        levels = [first + n for n in many]
        depths = [k.astype(F32) for k in levels]

        def running(b):
            out = []
            for h in pair:
                at = (rows_of(b), lanes_of(h))
                total = run[at]
                qs = []
                for k in levels:
                    half = 0.5 * values(k, b, h)
                    qs.append(total + half)
                    total = qs[-1] + half
                run[at] = total
                out.append(qs)
            return out

        q_next = None
        for b in blocks:
            rows = rows_of(b)
            if q_next is None:
                q = running(b)
                turned = [[pltpu.roll(x, 7, 0) for x in q[h]] for h in pair]
            else:
                q, turned = q_next, turned_next
            if b == 0:
                for h in pair:
                    for n in many:
                        keep_row(levels[n], h, q[h][n][0:1])
            if following(b):
                q_next = running(b + 1)
                turned_next = [[pltpu.roll(x, 7, 0) for x in q_next[h]] for h in pair]
            else:
                q_next, turned_next = None, [[zero] * unroll] * 2
            left = [[pltpu.roll(x, 127, 1) for x in q[h]] for h in pair]
            column = q_col[rows, :]
            for n in many:
                column = jnp.where(lane == levels[n], pltpu.roll(q[0][n], levels[n], 1), column)
            q_col[rows, :] = column
            for h in pair:
                at = (rows, lanes_of(h))
                limit = east_lim[at]
                total = u_sum[at]
                for n in many:
                    ahead = jnp.where(last_row, turned_next[h][n], turned[h][n])
                    speed = jnp.where(
                        depths[n] < limit, speeds[(0, levels[n], *at)] - PRESS * (q[h][n] - ahead), 0.0
                    )
                    keep_u(levels[n], b, h, speed)
                    total = total + speed
                u_sum[at] = total
                limit = north_lim[at]
                total = v_sum[at]
                for n in many:
                    ahead = jnp.where(last_lane, left[1][n] if h == 0 else 0.0, left[h][n])
                    speed = jnp.where(
                        depths[n] < limit, speeds[(1, levels[n], *at)] - PRESS * (q[h][n] - ahead), 0.0
                    )
                    keep_v(levels[n], b, h, speed)
                    total = total + speed
                v_sum[at] = total
        return 0

    lax.fori_loop(0, LEVELS // unroll, step, 0)


def forcing(blocks, u_sum, v_sum, row_sum, south_lim, q_col, count, rain, keep):
    lane, row = lane_id(), row_id()
    first_row, first_lane, last_lane = row == 0, lane == 0, lane == 127
    pair = range(2)
    for b in blocks:
        rows = rows_of(b)
        col_sum = col_face_sum(rows, south_lim, q_col)
        u = [u_sum[rows, lanes_of(h)] for h in pair]
        v = [v_sum[rows, lanes_of(h)] for h in pair]
        right = [pltpu.roll(v[h], 1, 1) for h in pair]
        v_before = [
            jnp.where(first_lane, col_sum, right[0]), jnp.where(first_lane, right[0], right[1])
        ]
        tiles = []
        for h in pair:
            at = (rows, lanes_of(h))
            if b == 0:
                before = row_sum[h]
            else:
                before = pltpu.roll(u_sum[rows_of(b - 1), lanes_of(h)], 1, 0)
            u_before = jnp.where(first_row, before, pltpu.roll(u[h], 1, 0))
            divergence = (u[h] - u_before) + (v[h] - v_before[h])
            tiles.append(
                jnp.where(count[at] > 0.0, source_scale * rain[at] - DIVERGE * divergence, 0.0)
            )
        side = jnp.where(first_lane, right[1], jnp.where(last_lane, col_sum, 0.0))
        keep(b, tiles, side)


def outer_kernel(
    source, inverse, link, speeds, count, rain, own_east, own_west, own_north, own_south,
    y_odd_in, y_even_in, x_odd_in, x_even_in,
    solved, to_east, to_west, x_odd, x_even, west, east, south, north,
    row_low, row_high, col_low, col_high, east_lim, north_lim, south_lim, west_lim,
    run, u_sum, v_sum, q_col,
):
    west[...], east[...] = sort_in("gx", x_even_in[...], x_odd_in[...])
    south[...], north[...] = sort_in("gy", y_even_in[...], y_odd_in[...])
    face_limits(
        OUTER, count, west, east, south, north, east_lim, north_lim, south_lim, west_lim
    )
    row_fluxes(own_east, own_west, west, east, west_lim, east_lim, row_low, row_high)
    column_fluxes(
        OUTER, own_north, own_south, south, north, south_lim, north_lim, col_low, col_high
    )

    def place(b):
        return slice(0, 8) if b == 0 else slice(8, 16)

    solve(OUTER, place, source, inverse, link, col_low, col_high, row_low, row_high, solved)

    def keep_row(k, h, value):
        to_west[pl.ds(24 + 40 * h + k, 1), :] = value

    def drop(*args):
        pass

    momentum(
        OUTER, lambda k, b, h: solved[k, place(b), lanes_of(h)], lambda b: False,
        speeds, east_lim, north_lim, run, u_sum, v_sum, q_col, drop, drop, keep_row,
        UNROLL_OUT,
    )
    row_sum = row_face_sum(west_lim, lambda h: to_west[24 + 40 * h : 64 + 40 * h, :])
    u_sum[rows_of(BLOCKS - 2), :] = jnp.zeros((8, COLS), F32)

    def keep(b, tiles, side):
        for h in range(2):
            if b == 0:
                to_west[rows_of(h), :] = tiles[h]
                to_west[8 * h + 5 : 8 * h + 6, :] = row_sum[h][0:1]
            else:
                to_east[rows_of(h), :] = pltpu.roll(tiles[h], 5, 0)
                to_east[8 * h + 5 : 8 * h + 6, :] = u_sum[ROWS - 1 : ROWS, lanes_of(h)]
        if b == 0:
            to_west[16:24, :] = side
        else:
            to_east[16:24, :] = pltpu.roll(side, 5, 0)

    forcing(OUTER, u_sum, v_sum, row_sum, south_lim, q_col, count, rain, keep)
    to_east[24:104, :] = jnp.zeros((80, 128), F32)
    x_even[...], x_odd[...] = sort_out("gx", to_west[...], to_east[...])


def outer(*args):
    plane = pltpu.VMEM((ROWS, COLS), F32)
    strip = pltpu.VMEM((ROWS, 128), F32)
    levels = pltpu.VMEM((2, LEVELS, 128), F32)
    return pl.pallas_call(
        outer_kernel,
        out_shape=(shape(LEVELS, 16, COLS),)
        + (shape(104, 128),) * 4
        + (shape(2, 88, 128),) * 2
        + (shape(ROWS, 128),) * 2,
        in_specs=[VMEM] * 14,
        out_specs=(VMEM,) * 9,
        scratch_shapes=[
            levels, levels, strip, strip, plane, plane, strip, pltpu.VMEM((8, COLS), F32),
            plane, plane, plane, strip,
        ],
        compiler_params=params(LIMIT_COLUMNS),
        name="outer",
    )(*args)


def middle_kernel(
    source, inverse, link, speeds, count, rain, own_north, own_south,
    west, east, south, north, outside, own_west,
    solved, u_new, v_low, v_high, force_out, q_col, sides,
    col_low, col_high, east_lim, north_lim, south_lim, west_lim, run, u_sum, v_sum,
):
    every = tuple(range(BLOCKS))
    face_limits(
        every, count, west, east, south, north, east_lim, north_lim, south_lim, west_lim
    )
    column_fluxes(
        MIDDLE, own_north, own_south, south, north, south_lim, north_lim, col_low, col_high
    )

    def place(b):
        return rows_of(b - 1)

    solve(MIDDLE, place, source, inverse, link, col_low, col_high, None, None, solved)

    def values(k, b, h):
        if b == 0:
            return outside[k, 0:8, lanes_of(h)]
        if b == BLOCKS - 1:
            return outside[k, 8:16, lanes_of(h)]
        return solved[k, place(b), lanes_of(h)]

    def keep_u(k, b, h, speed):
        u_new[k, rows_of(b), lanes_of(h)] = speed

    def keep_v(k, b, h, speed):
        if h == 0:
            v_low[k, rows_of(b), :] = speed
        else:
            v_high[k, rows_of(b), :] = speed

    momentum(
        every, values, lambda b: b < BLOCKS - 1, speeds, east_lim, north_lim,
        run, u_sum, v_sum, q_col, keep_u, keep_v, lambda k, h, value: None,
        UNROLL_MOM,
    )
    row_sum = [
        jnp.broadcast_to(own_west[8 * h + 5 : 8 * h + 6, :], (8, 128)) for h in range(2)
    ]

    def keep(b, tiles, side):
        for h in range(2):
            force_out[rows_of(b), lanes_of(h)] = tiles[h]
        sides[rows_of(b), :] = side

    forcing(every, u_sum, v_sum, row_sum, south_lim, q_col, count, rain, keep)


def middle(*args):
    plane = pltpu.VMEM((ROWS, COLS), F32)
    strip = pltpu.VMEM((ROWS, 128), F32)
    half = shape(LEVELS, ROWS, 128)
    return pl.pallas_call(
        middle_kernel,
        out_shape=(
            shape(LEVELS, ROWS - 16, COLS), shape(LEVELS, ROWS, COLS), half, half,
            shape(ROWS, COLS), shape(ROWS, 128), shape(ROWS, 128),
        ),
        in_specs=[VMEM] * 14,
        out_specs=(VMEM,) * 7,
        scratch_shapes=[
            strip, strip, plane, plane, strip, pltpu.VMEM((8, COLS), F32), plane, plane, plane,
        ],
        cost_estimate=pl.CostEstimate(
            flops=30 * LEVELS * ROWS * COLS, bytes_accessed=16 * LEVELS * ROWS * COLS,
            transcendentals=0,
        ),
        compiler_params=params(LIMIT_COLUMNS),
        name="middle",
    )(*args)


EXT = ROWS + 16


def relax(force, count):
    wide = force.shape[1]
    root = jnp.sqrt(count * (1.0 / LEVELS))

    def total(field):
        sideways = pltpu.roll(field, 1, 1) + pltpu.roll(field, wide - 1, 1)
        mixed = field + 0.5 * sideways
        return sideways + (pltpu.roll(mixed, 1, 0) + pltpu.roll(mixed, EXT - 1, 0))

    inverse = 1.0 / (damping + root * total(root))
    force = force * inverse
    share = root * inverse
    update = force * (1.0 / cheb_gamma)
    iterate = update
    omega = 2.0 / cheb_gamma
    for step in range(1, ITERS):
        residual = (force - iterate) + share * total(root * iterate)
        omega = 1.0 / (cheb_gamma - omega / (4.0 * cheb_alpha * cheb_alpha))
        update = omega * residual + (cheb_gamma * omega - 1.0) * update
        iterate = iterate + update
    return iterate


def writer_kernel(
    outside, solved, u_new, v_low, from_east, count, east, force_ext, count_ext,
    temp_out, speeds_out, inner, u_fix, sems,
):
    copies = [
        (outside.at[:, pl.ds(0, 8), :], temp_out.at[:, pl.ds(0, 8), :]),
        (outside.at[:, pl.ds(8, 8), :], temp_out.at[:, pl.ds(ROWS - 8, 8), :]),
        (solved, temp_out.at[:, pl.ds(8, ROWS - 16), :]),
        (u_new.at[:, pl.ds(0, ROWS - 8), :], speeds_out.at[0, :, pl.ds(0, ROWS - 8), :]),
        (v_low, speeds_out.at[1, :, :, pl.ds(0, 128)]),
        (u_fix, speeds_out.at[0, :, pl.ds(ROWS - 8, 8), :]),
    ]
    copies = [
        pltpu.make_async_copy(origin, target, sems.at[n])
        for n, (origin, target) in enumerate(copies)
    ]
    for copy in copies[:-1]:
        copy.start()
    last_row = row_id() == 7
    for h in range(2):
        limit = jnp.minimum(
            count[ROWS - 8 :, lanes_of(h)], jnp.broadcast_to(east[h, 40:41, :], (8, 128))
        )
        limit = jnp.where(last_row, limit, 0.0)
        for k in range(LEVELS):
            at = 24 + 40 * h + k
            u_fix[k, :, lanes_of(h)] = u_new[k, ROWS - 8 :, lanes_of(h)] + jnp.where(
                float(k) < limit,
                PRESS * jnp.broadcast_to(from_east[at : at + 1, :], (8, 128)),
                0.0,
            )
    copies[-1].start()
    inner[...] = relax(force_ext[...], count_ext[...])[8 : 8 + ROWS]
    for copy in copies:
        copy.wait()


def writer(*args):
    return pl.pallas_call(
        writer_kernel,
        out_shape=(
            shape(LEVELS, ROWS, COLS), shape(2, LEVELS, ROWS, COLS), shape(ROWS, COLS)
        ),
        in_specs=[VMEM] * 9,
        out_specs=(ANY, ANY, VMEM),
        scratch_shapes=[
            pltpu.VMEM((LEVELS, 8, COLS), F32),
            pltpu.SemaphoreType.DMA((6,)),
        ],
        cost_estimate=pl.CostEstimate(
            flops=LEVELS * ROWS * COLS, bytes_accessed=12 * LEVELS * ROWS * COLS,
            transcendentals=0,
        ),
        compiler_params=params(LIMIT_COLUMNS),
        name="writer",
    )(*args)


def edges_kernel(
    force, sides, q_col, count, west, east_in, own_east, own_west, x_odd, x_even,
    force_ext, count_ext, sides_ext, y_odd, y_even, from_east, from_west, to_north, to_south,
):
    from_west[...], from_east[...] = sort_in("gx", x_even[...], x_odd[...])
    zeros8 = jnp.zeros((8, COLS), F32)
    count_ext[0:8, :] = zeros8
    for h in range(2):
        count_ext[2:8, lanes_of(h)] = west[h, 80:86, :]
    count_ext[8 : 8 + ROWS, :] = count[...]
    count_ext[8 + ROWS :, :] = zeros8
    for h in range(2):
        count_ext[8 + ROWS : 14 + ROWS, lanes_of(h)] = east_in[h, 40:46, :]
    sides_ext[0:8, :] = jnp.zeros((8, 128), F32)
    sides_ext[3:8, :] = from_west[16:21, :]
    sides_ext[8 : 8 + ROWS, :] = sides[...]
    sides_ext[8 + ROWS :, :] = jnp.zeros((8, 128), F32)
    sides_ext[8 + ROWS : 13 + ROWS, :] = from_east[16:21, :]
    force_ext[0:8, :] = zeros8
    for h in range(2):
        force_ext[3:8, lanes_of(h)] = from_west[8 * h : 8 * h + 5, :]
    force_ext[8 : 8 + ROWS, :] = force[...]
    force_ext[8 + ROWS :, :] = zeros8
    for h in range(2):
        force_ext[8 + ROWS : 13 + ROWS, lanes_of(h)] = from_east[8 * h : 8 * h + 5, :]

    def add(at, sign, ref):
        for h in range(2):
            place = (slice(at, at + 1), lanes_of(h))
            force_ext[place] = force_ext[place] + jnp.where(
                count_ext[place] > 0.0, sign * DIVERGE * ref[8 * h + 5 : 8 * h + 6, :], 0.0
            )

    add(7, -1.0, own_west)
    add(8, 1.0, from_west)
    add(7 + ROWS, -1.0, from_east)
    add(8 + ROWS, 1.0, own_east)
    lane = lane_id(EXT)
    side = sides_ext[...]
    to_north[...] = jnp.where(
        lane >= 123,
        force_ext[:, 128:],
        jnp.where(lane == 0, side, pltpu.roll(count_ext[:, 128:], 122, 1)),
    )
    to_south[...] = jnp.where(
        lane < 5,
        force_ext[:, :128],
        jnp.where(lane == 127, side, pltpu.roll(count_ext[:, :128], 8, 1)),
    )
    lane = lane_id(ROWS)
    to_south[8 : 8 + ROWS, :] = jnp.where(
        (lane >= 64) & (lane < 64 + LEVELS),
        pltpu.roll(q_col[...], 64, 1),
        to_south[8 : 8 + ROWS, :],
    )
    y_even[...], y_odd[...] = sort_out("gy", to_south[...], to_north[...])


def edges(*args):
    return pl.pallas_call(
        edges_kernel,
        out_shape=(
            shape(EXT, COLS), shape(EXT, COLS), shape(EXT, 128), shape(EXT, 128), shape(EXT, 128),
            shape(104, 128),
        ),
        in_specs=[VMEM] * 10,
        out_specs=(VMEM,) * 6,
        scratch_shapes=[
            pltpu.VMEM((104, 128), F32), pltpu.VMEM((EXT, 128), F32), pltpu.VMEM((EXT, 128), F32)
        ],
        compiler_params=params(LIMIT_COLUMNS),
        name="edges",
    )(*args)


def final_kernel(
    speeds, v_high, count, inner, force_ext, count_ext, sides_ext, y_odd, y_even,
    speeds_out, out, v_fix, south, north, sems,
):
    south[...], north[...] = sort_in("gy", y_even[...], y_odd[...])
    last_lane = lane_id(8) == 127
    limits = []
    for b in range(BLOCKS):
        limit = jnp.minimum(
            count[rows_of(b), 128:], pltpu.roll(north[rows_of(b + 1), :], 127 - 8, 1)
        )
        limits.append(jnp.where(last_lane, limit, 0.0))

    def save(c):
        part = pl.ds(c * FIX_CHUNK, FIX_CHUNK)
        return pltpu.make_async_copy(
            v_fix.at[part], speeds_out.at[1, part, :, pl.ds(128, 128)], sems.at[c]
        )

    for c in range(LEVELS // FIX_CHUNK):
        for k in range(c * FIX_CHUNK, (c + 1) * FIX_CHUNK):
            for b in range(BLOCKS):
                rows = rows_of(b)
                v_fix[k, rows, :] = v_high[k, rows, :] + jnp.where(
                    float(k) < limits[b],
                    PRESS * pltpu.roll(north[rows_of(b + 1), :], 63 - k, 1),
                    0.0,
                )
        save(c).start()

    @pl.when(lax.axis_index("gx") >= 0)
    def _():
        lane = lane_id(EXT)
        count_side = jnp.where(
            lane >= 122,
            pltpu.roll(south[...], 6, 1),
            jnp.where(lane < 6, pltpu.roll(north[...], 120, 1), 0.0),
        )
        force_side = jnp.where(
            lane >= 123, south[...], jnp.where(lane < 5, north[...], 0.0)
        )
        side = sides_ext[...]
        low, high = force_ext[:, :128], force_ext[:, 128:]
        low = low + jnp.where(
            (lane == 0) & (count_ext[:, :128] > 0.0), DIVERGE * south[...], 0.0
        )
        high = high - jnp.where(
            (lane == 127) & (count_ext[:, 128:] > 0.0), DIVERGE * north[...], 0.0
        )
        force_side = force_side + jnp.where(
            (lane == 0) & (count_side > 0.0), DIVERGE * side, 0.0
        )
        force_side = force_side - jnp.where(
            (lane == 127) & (count_side > 0.0), DIVERGE * side, 0.0
        )
        left = (lane < 32) | (lane >= 96)

        def strip(low, high, side):
            return jnp.where(
                left,
                jnp.where(lane < 64, low, side),
                pltpu.roll(jnp.where(lane >= 64, high, side), 64, 1),
            )

        near = relax(
            strip(low, high, force_side), strip(count_ext[:, :128], count_ext[:, 128:], count_side)
        )[8 : 8 + ROWS]
        lane = lane_id(ROWS)
        out[:, :128] = jnp.where(lane < 6, near, inner[:, :128])
        out[:, 128:] = jnp.where(lane >= 122, pltpu.roll(near, 64, 1), inner[:, 128:])
    for c in range(LEVELS // FIX_CHUNK):
        save(c).wait()


def final(*args):
    return pl.pallas_call(
        final_kernel,
        out_shape=(shape(2, LEVELS, ROWS, COLS), shape(ROWS, COLS)),
        in_specs=[ANY] + [VMEM] * 8,
        out_specs=(ANY, VMEM),
        scratch_shapes=[
            pltpu.VMEM((LEVELS, ROWS, 128), F32),
            pltpu.VMEM((EXT, 128), F32), pltpu.VMEM((EXT, 128), F32),
            pltpu.SemaphoreType.DMA((LEVELS // FIX_CHUNK,)),
        ],
        input_output_aliases={0: 0},
        compiler_params=params(LIMIT_COLUMNS),
        name="final",
    )(*args)


def swap(array, axis, first):
    count = lax.axis_size(axis)
    pairs = []
    for low in range(first, count + first, 2):
        low, high = low % count, (low + 1) % count
        pairs += [(low, high), (high, low)]
    return lax.ppermute(array, axis, pairs)


def local(
    thermal_departure,
    current_speeds,
    mixing_coefficient,
    seawater_indicator,
    submerged_layer_tally,
    rainfall_runoff_input,
):
    near, count, to_east, to_west, to_north, to_south, y_odd, y_even, x_odd, x_even = pack(
        *(
            pltpu.with_memory_space_constraint(x, pltpu.HBM)
            for x in (
                thermal_departure, current_speeds, seawater_indicator, submerged_layer_tally
            )
        )
    )
    y_odd = swap(y_odd, "gy", 1)
    y_even = swap(y_even, "gy", 0)
    x_odd = swap(x_odd, "gx", 1)
    x_even = swap(x_even, "gx", 0)
    speeds, mixing = (
        pltpu.with_memory_space_constraint(x, pltpu.VMEM)
        for x in (current_speeds, mixing_coefficient)
    )
    inside = (*interior(near, speeds, mixing, count), speeds)
    outside, own_east, own_west, x_odd, x_even, west, east, south, north = outer(
        *inside, count, rainfall_runoff_input, to_east, to_west, to_north, to_south,
        y_odd, y_even, x_odd, x_even,
    )
    x_odd = swap(x_odd, "gx", 1)
    x_even = swap(x_even, "gx", 0)
    solved, u_new, v_low, v_high, force, q_col, sides = middle(
        *inside, count, rainfall_runoff_input, to_north, to_south,
        west, east, south, north, outside, own_west,
    )
    force_ext, count_ext, sides_ext, y_odd, y_even, from_east = edges(
        force, sides, q_col, count, west, east, own_east, own_west, x_odd, x_even
    )
    y_odd = swap(y_odd, "gy", 1)
    y_even = swap(y_even, "gy", 0)
    temp_next, stored, inner = writer(
        outside, solved, u_new, v_low, from_east, count, east, force_ext, count_ext
    )
    velocity_next, surface = final(
        stored, v_high, count, inner, force_ext, count_ext, sides_ext, y_odd, y_even,
    )
    return (temp_next, velocity_next, surface)


def solution(mesh):
    placed = (
        P(None, "gx", "gy"),
        P(None, None, "gx", "gy"),
        P(None, "gx", "gy"),
        P("gx", "gy"),
        P("gx", "gy"),
        P("gx", "gy"),
    )
    return jax.shard_map(
        local,
        mesh=mesh,
        in_specs=placed,
        out_specs=(P(None, "gx", "gy"), P(None, None, "gx", "gy"), P("gx", "gy")),
        check_vma=False,
    )
```

```python
import jax
import jax.numpy as jnp
from jax import lax
from jax.experimental import pallas as pl
from jax.experimental.pallas import tpu as pltpu
from jax.sharding import PartitionSpec as P

ITERS = 6
FIX_CHUNK = 20
COST = 10000
LIMIT_PACK = 12
LIMIT_INTERIOR = 8
LIMIT_COLUMNS = 12
LEVELS = 40
ROWS = 64
COLS = 256
BLOCKS = ROWS // 8
CHUNK = 20
CHUNKS = LEVELS // CHUNK

damping = 0.05
lower_bound = 0.02
upper_bound = 2.0
cheb_alpha = 2.0 / (upper_bound - lower_bound)
cheb_gamma = (upper_bound + lower_bound) / 2.0
advect_scale = 0.4
force_scale = 4.0
source_scale = 0.5
divergence_scale = 4.0
PRESS = force_scale / LEVELS
DIVERGE = divergence_scale / LEVELS

VMEM = pl.BlockSpec(memory_space=pltpu.VMEM)
ANY = pl.BlockSpec(memory_space=pl.ANY)
HBM = pl.BlockSpec(memory_space=pltpu.HBM)
F32 = jnp.float32
TILES = [(b, h) for b in range(BLOCKS) for h in range(2)]


def shape(*dims):
    return jax.ShapeDtypeStruct(dims, F32)


def params(mebibytes=40):
    return pltpu.CompilerParams(vmem_limit_bytes=int(mebibytes * 1024 * 1024))


def lane_id(rows=8):
    return lax.broadcasted_iota(jnp.int32, (rows, 128), 1)


def row_id():
    return lax.broadcasted_iota(jnp.int32, (8, 128), 0)


def rows_of(b):
    return slice(8 * b, 8 * b + 8)


def lanes_of(h):
    return slice(128 * h, 128 * h + 128)


def odd_place(axis):
    return lax.axis_index(axis) % 2 == 1


def sort_out(axis, lower, upper):
    odd = odd_place(axis)
    return jnp.where(odd, lower, upper), jnp.where(odd, upper, lower)


def sort_in(axis, even_pair, odd_pair):
    odd = odd_place(axis)
    return jnp.where(odd, even_pair, odd_pair), jnp.where(odd, odd_pair, even_pair)


def tiles_of(ref, *lead):
    return {(b, h): ref[(*lead, rows_of(b), lanes_of(h))] for b, h in TILES}


def next_row(x, after, last):
    turned = {t: pltpu.roll(x[t], 7, 0) for t in TILES}
    return {
        (b, h): jnp.where(last, after[h] if b == BLOCKS - 1 else turned[b + 1, h], turned[b, h])
        for b, h in TILES
    }


def prev_row(x, before, first):
    turned = {t: pltpu.roll(x[t], 1, 0) for t in TILES}
    return {
        (b, h): jnp.where(first, before[h] if b == 0 else turned[b - 1, h], turned[b, h])
        for b, h in TILES
    }


def next_col(x, after, last):
    turned = {t: pltpu.roll(x[t], 127, 1) for t in TILES}
    return {
        (b, h): jnp.where(last, after[b] if h == 1 else turned[b, 1], turned[b, h])
        for b, h in TILES
    }


def prev_col(x, before, first):
    turned = {t: pltpu.roll(x[t], 1, 1) for t in TILES}
    return {
        (b, h): jnp.where(first, before[b] if h == 0 else turned[b, 0], turned[b, h])
        for b, h in TILES
    }


def spread(ref, k, h):
    return jnp.broadcast_to(ref[h, pl.ds(k, 1), :], (8, 128))


def pack_kernel(
    temp, speeds, sea_in, tally_in,
    near, count_out, to_east, to_west, to_north, to_south, y_odd, y_even, x_odd, x_even,
    v_high, u_end, sea, tally, sems, part_sems,
):
    first = [
        pltpu.make_async_copy(sea_in, sea, sems.at[0]),
        pltpu.make_async_copy(tally_in, tally, sems.at[1]),
    ]
    parts = []
    for c in range(CHUNKS):
        part = pl.ds(c * CHUNK, CHUNK)
        parts.append(
            (
                pltpu.make_async_copy(temp.at[part], near.at[part], part_sems.at[0, c]),
                pltpu.make_async_copy(
                    speeds.at[1, part, :, pl.ds(128, 128)], v_high.at[part], part_sems.at[1, c]
                ),
            )
        )
    last = pltpu.make_async_copy(speeds.at[0, :, pl.ds(ROWS - 8, 8), :], u_end, sems.at[2])
    for copy in first:
        copy.start()
    for pair in parts:
        for copy in pair:
            copy.start()
    last.start()

    for copy in first:
        copy.wait()
    latitude = lax.axis_index("gy") * COLS + lax.broadcasted_iota(jnp.int32, (ROWS, COLS), 1)
    inner = (latitude > 0) & (latitude < lax.axis_size("gy") * COLS - 1)
    count = jnp.where(inner & (sea[...] == 1), tally[...], 0).astype(F32)
    count_out[...] = count
    for h in range(2):
        to_east[h, 80:86, :] = count[ROWS - 6 :, lanes_of(h)]
        to_east[h, 86:88, :] = jnp.zeros((2, 128), F32)
        to_west[h, 40:46, :] = count[:6, lanes_of(h)]
        to_west[h, 46:88, :] = jnp.zeros((42, 128), F32)
    lane = lane_id()
    low, high = [], []
    for b in range(BLOCKS):
        low.append(pltpu.roll(count[rows_of(b), :128], 40, 1))
        high.append(pltpu.roll(count[rows_of(b), 128:], (80 - 127) % 128, 1))

    for c in range(CHUNKS):
        parts[c][0].wait()
        parts[c][1].wait()
        for k in range(c * CHUNK, (c + 1) * CHUNK):
            for b in range(BLOCKS):
                rows = rows_of(b)
                low[b] = jnp.where(lane == k, pltpu.roll(near[k, rows, :128], k, 1), low[b])
                high[b] = jnp.where(lane == k, pltpu.roll(near[k, rows, 128:], k + 1, 1), high[b])
                high[b] = jnp.where(
                    lane == k + 40, pltpu.roll(v_high[k, rows, :], k + 41, 1), high[b]
                )
        levels = slice(c * CHUNK, (c + 1) * CHUNK)
        for h in range(2):
            to_west[h, levels, :] = near[levels, 0, lanes_of(h)]
            to_east[h, levels, :] = near[levels, ROWS - 1, lanes_of(h)]
    for b in range(BLOCKS):
        to_south[rows_of(b), :] = low[b]
        to_north[rows_of(b), :] = high[b]
        y_even[rows_of(b), :], y_odd[rows_of(b), :] = sort_out("gy", low[b], high[b])
    last.wait()
    for h in range(2):
        to_east[h, 40:80, :] = u_end[:, 7, lanes_of(h)]
    x_even[...], x_odd[...] = sort_out("gx", to_west[...], to_east[...])


def pack(*args):
    return pl.pallas_call(
        pack_kernel,
        out_shape=(
            shape(LEVELS, ROWS, COLS), shape(ROWS, COLS),
            shape(2, 88, 128), shape(2, 88, 128), shape(ROWS, 128), shape(ROWS, 128),
            shape(ROWS, 128), shape(ROWS, 128), shape(2, 88, 128), shape(2, 88, 128),
        ),
        in_specs=[HBM] * 4,
        out_specs=(VMEM,) * 10,
        scratch_shapes=[
            pltpu.VMEM((LEVELS, ROWS, 128), F32),
            pltpu.VMEM((LEVELS, 8, COLS), F32),
            pltpu.VMEM((ROWS, COLS), jnp.int32),
            pltpu.VMEM((ROWS, COLS), jnp.int32),
            pltpu.SemaphoreType.DMA((3,)),
            pltpu.SemaphoreType.DMA((2, CHUNKS)),
        ],
        compiler_params=params(LIMIT_PACK),
        name="pack",
    )(*args)


UNROLL_IN = 4
UNROLL_FWD = 40
UNROLL_BACK = 40
UNROLL_MOM = 5
UNROLL_OUT = 40


def interior_kernel(
    tb, speeds, mb, count,
    source_out, inverse_out, link_out,
    east_lim, north_lim,
):
    lane, row = lane_id(), row_id()
    first_row, last_row = row == 0, row == 7
    first_lane, last_lane = lane == 0, lane == 127
    zero = jnp.zeros((8, 128), F32)
    pair = range(2)

    counts = tiles_of(count)
    ahead = next_row(counts, [zero, zero], last_row)
    for b, h in TILES:
        east_lim[rows_of(b), lanes_of(h)] = jnp.minimum(counts[b, h], ahead[b, h])
    ahead = next_col(counts, [zero] * BLOCKS, last_lane)
    for b, h in TILES:
        north_lim[rows_of(b), lanes_of(h)] = jnp.minimum(counts[b, h], ahead[b, h])

    def level_step(k, factors, links, opens=None):
        level = k.astype(F32)
        below_at = jnp.minimum(k + 1, LEVELS - 1)
        t_next = [tb[k, rows_of(0), lanes_of(h)] for h in pair]
        turned_next = [pltpu.roll(t_next[h], 7, 0) for h in pair]
        flux_turned = [zero, zero]
        new_factors, new_links, new_opens = [], [], []
        for b in range(BLOCKS):
            rows = rows_of(b)
            t, turned = t_next, turned_next
            if b < BLOCKS - 1:
                t_next = [tb[k, rows_of(b + 1), lanes_of(h)] for h in pair]
                turned_next = [pltpu.roll(t_next[h], 7, 0) for h in pair]
            u = [speeds[0, k, rows, lanes_of(h)] for h in pair]
            v = [speeds[1, k, rows, lanes_of(h)] for h in pair]
            change = []
            for h in pair:
                ahead = jnp.where(last_row, turned_next[h], turned[h])
                flux = jnp.where(level < east_lim[rows, lanes_of(h)], u[h], 0.0) * jnp.where(
                    u[h] > 0.0, t[h], ahead
                )
                flux_before, flux_turned[h] = flux_turned[h], pltpu.roll(flux, 1, 0)
                change.append(flux - jnp.where(first_row, flux_before, flux_turned[h]))
            left = [pltpu.roll(t[h], 127, 1) for h in pair]
            ahead = [jnp.where(last_lane, left[1], left[0]), left[1]]
            flux = [
                jnp.where(level < north_lim[rows, lanes_of(h)], v[h], 0.0)
                * jnp.where(v[h] > 0.0, t[h], ahead[h])
                for h in pair
            ]
            right = [pltpu.roll(flux[h], 1, 1) for h in pair]
            behind = [jnp.where(first_lane, 0.0, right[0]), jnp.where(first_lane, right[0], right[1])]
            for h in pair:
                n = 2 * b + h
                at = (k, rows, lanes_of(h))
                wet = count[rows, lanes_of(h)]
                total = change[h] + (flux[h] - behind[h])
                open_here = level < wet if opens is None else opens[n]
                open_below = level + 1.0 < wet
                source_out[at] = t[h] - jnp.where(open_here, advect_scale * total, 0.0)
                a = links[n]
                below = jnp.where(open_below, mb[below_at, rows, lanes_of(h)], 0.0)
                pivot = (1.0 + below) + (a - a * factors[n])
                inverse = pl.reciprocal(pivot, approx=True)
                inverse = inverse * (2.0 - pivot * inverse)
                inverse_out[at] = inverse
                link_out[at] = a
                new_factors.append(below * inverse)
                new_links.append(below)
                new_opens.append(open_below)
        return tuple(new_factors), tuple(new_links), new_opens

    def step(m, carry):
        for n in range(UNROLL_IN):
            carry = level_step(m * UNROLL_IN + n, *carry)
        return carry[:2]

    blank = tuple(zero for _ in TILES)
    lax.fori_loop(0, LEVELS // UNROLL_IN, step, (blank, blank))


def interior(temp, speeds, mix, count):
    block = shape(LEVELS, ROWS, COLS)
    return pl.pallas_call(
        interior_kernel,
        out_shape=(block,) * 3,
        in_specs=[VMEM] * 4,
        out_specs=(VMEM,) * 3,
        scratch_shapes=[
            pltpu.VMEM((ROWS, COLS), F32), pltpu.VMEM((ROWS, COLS), F32),
        ],
        cost_estimate=pl.CostEstimate(
            flops=COST * LEVELS * ROWS * COLS, bytes_accessed=COST * LEVELS * ROWS * COLS,
            transcendentals=0,
        ),
        compiler_params=params(LIMIT_INTERIOR),
        name="interior",
    )(temp, speeds, mix, count)


OUTER = (0, BLOCKS - 1)
MIDDLE = tuple(range(1, BLOCKS - 1))


def face_limits(
    blocks, count, west, east, south, north, east_lim, north_lim, south_lim, west_lim
):
    lane, row = lane_id(), row_id()
    last_row, last_lane = row == 7, lane == 127
    counts = tiles_of(count)
    pair = range(2)
    for h in pair:
        before = jnp.broadcast_to(west[h, 85:86, :], (8, 128))
        west_lim[:, lanes_of(h)] = jnp.minimum(counts[0, h], before)
        for b in blocks:
            if b == BLOCKS - 1:
                after = jnp.broadcast_to(east[h, 40:41, :], (8, 128))
            else:
                after = pltpu.roll(counts[b + 1, h], 7, 0)
            ahead = jnp.where(last_row, after, pltpu.roll(counts[b, h], 7, 0))
            east_lim[rows_of(b), lanes_of(h)] = jnp.minimum(counts[b, h], ahead)
    for b in blocks:
        rows = rows_of(b)
        left = [pltpu.roll(counts[b, h], 127, 1) for h in pair]
        left.append(pltpu.roll(north[rows, :], 127 - 40, 1))
        for h in pair:
            ahead = jnp.where(last_lane, left[h + 1], left[h])
            north_lim[rows, lanes_of(h)] = jnp.minimum(counts[b, h], ahead)
        south_lim[rows, :] = jnp.minimum(counts[b, 0], pltpu.roll(south[rows, :], 128 - 80, 1))


def column_fluxes(
    blocks, own_north, own_south, south, north, south_lim, north_lim, col_low, col_high
):
    depth = lane_id().astype(F32)
    for b in blocks:
        rows = rows_of(b)
        limit = jnp.broadcast_to(south_lim[rows, 0:1], (8, 128))
        speed = pltpu.roll(south[rows, :], 128 - 40, 1)
        col_low[rows, :] = (
            advect_scale
            * jnp.where(depth < limit, speed, 0.0)
            * jnp.where(speed > 0.0, south[rows, :], own_south[rows, :])
        )
        limit = jnp.broadcast_to(north_lim[rows, COLS - 1 : COLS], (8, 128))
        speed = pltpu.roll(own_north[rows, :], 128 - 40, 1)
        col_high[rows, :] = (
            -advect_scale
            * jnp.where(depth < limit, speed, 0.0)
            * jnp.where(speed > 0.0, own_north[rows, :], north[rows, :])
        )


def row_fluxes(own_east, own_west, west, east, west_lim, east_lim, row_low, row_high):
    depth = lax.broadcasted_iota(jnp.int32, (LEVELS, 128), 0).astype(F32)
    for h in range(2):
        speed = west[h, 40:80, :]
        row_low[h] = (
            advect_scale
            * jnp.where(depth < west_lim[0:1, lanes_of(h)], speed, 0.0)
            * jnp.where(speed > 0.0, west[h, 0:40, :], own_west[h, 0:40, :])
        )
        speed = own_east[h, 40:80, :]
        row_high[h] = (
            -advect_scale
            * jnp.where(depth < east_lim[ROWS - 1 : ROWS, lanes_of(h)], speed, 0.0)
            * jnp.where(speed > 0.0, own_east[h, 0:40, :], east[h, 0:40, :])
        )


def solve(blocks, place, source, inverse, link, col_low, col_high, row_low, row_high, solved):
    lane, row = lane_id(), row_id()
    first_row, last_row = row == 0, row == 7
    first_lane, last_lane = lane == 0, lane == 127
    zero = jnp.zeros((8, 128), F32)
    pair = range(2)

    def forward(k, values):
        out = []
        for n, b in enumerate(blocks):
            rows = rows_of(b)
            add = [
                jnp.where(first_lane, pltpu.roll(col_low[rows, :], 128 - k, 1), 0.0),
                jnp.where(last_lane, pltpu.roll(col_high[rows, :], 127 - k, 1), 0.0),
            ]
            for h in pair:
                at = (k, rows, lanes_of(h))
                total = source[at] + add[h]
                if b == 0:
                    total = total + jnp.where(first_row, spread(row_low, k, h), 0.0)
                if b == BLOCKS - 1:
                    total = total + jnp.where(last_row, spread(row_high, k, h), 0.0)
                turn = inverse[at]
                value = total * turn + (link[at] * turn) * values[2 * n + h]
                solved[k, place(b), lanes_of(h)] = value
                out.append(value)
        return tuple(out)

    blank = (zero,) * (2 * len(blocks))

    def forward_step(m, values):
        for n in range(UNROLL_FWD):
            values = forward(m * UNROLL_FWD + n, values)
        return values

    lax.fori_loop(0, LEVELS // UNROLL_FWD, forward_step, blank)

    def back_step(m, below):
        for n in range(UNROLL_BACK):
            k = LEVELS - 1 - m * UNROLL_BACK - n
            below_at = jnp.minimum(k + 1, LEVELS - 1)
            out = []
            for i, value in zip([(b, h) for b in blocks for h in pair], below):
                at = (rows_of(i[0]), lanes_of(i[1]))
                to = (k, place(i[0]), lanes_of(i[1]))
                value = solved[to] + (inverse[(k, *at)] * link[(below_at, *at)]) * value
                solved[to] = value
                out.append(value)
            below = tuple(out)
        return below

    lax.fori_loop(0, LEVELS // UNROLL_BACK, back_step, blank)


def row_face_sum(west_lim, q_rows):
    depth = lax.broadcasted_iota(jnp.int32, (LEVELS, 128), 0).astype(F32)
    out = []
    for h in range(2):
        part = jnp.where(depth < west_lim[0:1, lanes_of(h)], PRESS * q_rows(h), 0.0)
        out.append(jnp.broadcast_to(jnp.sum(part, axis=0, keepdims=True), (8, 128)))
    return out


def col_face_sum(rows, south_lim, q_col):
    limit = jnp.broadcast_to(south_lim[rows, 0:1], (8, 128))
    part = jnp.where(lane_id().astype(F32) < limit, PRESS * q_col[rows, :], 0.0)
    return jnp.broadcast_to(jnp.sum(part, axis=1, keepdims=True), (8, 128))


def momentum(
    blocks, values, following, speeds, east_lim, north_lim, run, u_sum, v_sum, q_col,
    keep_u, keep_v, keep_row, unroll,
):
    lane, row = lane_id(), row_id()
    last_row, last_lane = row == 7, lane == 127
    zero = jnp.zeros((8, 128), F32)
    pair = range(2)
    many = range(unroll)
    for b in blocks:
        run[rows_of(b), :] = jnp.zeros((8, COLS), F32)
        u_sum[rows_of(b), :] = jnp.zeros((8, COLS), F32)
        v_sum[rows_of(b), :] = jnp.zeros((8, COLS), F32)
        q_col[rows_of(b), :] = zero

    def step(m, _):
        first = m * unroll
        levels = [first + n for n in many]
        depths = [k.astype(F32) for k in levels]

        def running(b):
            out = []
            for h in pair:
                at = (rows_of(b), lanes_of(h))
                total = run[at]
                qs = []
                for k in levels:
                    half = 0.5 * values(k, b, h)
                    qs.append(total + half)
                    total = qs[-1] + half
                run[at] = total
                out.append(qs)
            return out

        q_next = None
        for b in blocks:
            rows = rows_of(b)
            if q_next is None:
                q = running(b)
                turned = [[pltpu.roll(x, 7, 0) for x in q[h]] for h in pair]
            else:
                q, turned = q_next, turned_next
            if b == 0:
                for h in pair:
                    for n in many:
                        keep_row(levels[n], h, q[h][n][0:1])
            if following(b):
                q_next = running(b + 1)
                turned_next = [[pltpu.roll(x, 7, 0) for x in q_next[h]] for h in pair]
            else:
                q_next, turned_next = None, [[zero] * unroll] * 2
            left = [[pltpu.roll(x, 127, 1) for x in q[h]] for h in pair]
            column = q_col[rows, :]
            for n in many:
                column = jnp.where(lane == levels[n], pltpu.roll(q[0][n], levels[n], 1), column)
            q_col[rows, :] = column
            for h in pair:
                at = (rows, lanes_of(h))
                limit = east_lim[at]
                total = u_sum[at]
                for n in many:
                    ahead = jnp.where(last_row, turned_next[h][n], turned[h][n])
                    speed = jnp.where(
                        depths[n] < limit, speeds[(0, levels[n], *at)] - PRESS * (q[h][n] - ahead), 0.0
                    )
                    keep_u(levels[n], b, h, speed)
                    total = total + speed
                u_sum[at] = total
                limit = north_lim[at]
                total = v_sum[at]
                for n in many:
                    ahead = jnp.where(last_lane, left[1][n] if h == 0 else 0.0, left[h][n])
                    speed = jnp.where(
                        depths[n] < limit, speeds[(1, levels[n], *at)] - PRESS * (q[h][n] - ahead), 0.0
                    )
                    keep_v(levels[n], b, h, speed)
                    total = total + speed
                v_sum[at] = total
        return 0

    lax.fori_loop(0, LEVELS // unroll, step, 0)


def forcing(blocks, u_sum, v_sum, row_sum, south_lim, q_col, count, rain, keep):
    lane, row = lane_id(), row_id()
    first_row, first_lane, last_lane = row == 0, lane == 0, lane == 127
    pair = range(2)
    for b in blocks:
        rows = rows_of(b)
        col_sum = col_face_sum(rows, south_lim, q_col)
        u = [u_sum[rows, lanes_of(h)] for h in pair]
        v = [v_sum[rows, lanes_of(h)] for h in pair]
        right = [pltpu.roll(v[h], 1, 1) for h in pair]
        v_before = [
            jnp.where(first_lane, col_sum, right[0]), jnp.where(first_lane, right[0], right[1])
        ]
        tiles = []
        for h in pair:
            at = (rows, lanes_of(h))
            if b == 0:
                before = row_sum[h]
            else:
                before = pltpu.roll(u_sum[rows_of(b - 1), lanes_of(h)], 1, 0)
            u_before = jnp.where(first_row, before, pltpu.roll(u[h], 1, 0))
            divergence = (u[h] - u_before) + (v[h] - v_before[h])
            tiles.append(
                jnp.where(count[at] > 0.0, source_scale * rain[at] - DIVERGE * divergence, 0.0)
            )
        side = jnp.where(first_lane, right[1], jnp.where(last_lane, col_sum, 0.0))
        keep(b, tiles, side)


def outer_kernel(
    source, inverse, link, speeds, count, rain, own_east, own_west, own_north, own_south,
    y_odd_in, y_even_in, x_odd_in, x_even_in,
    solved, to_east, to_west, x_odd, x_even, west, east, south, north,
    row_low, row_high, col_low, col_high, east_lim, north_lim, south_lim, west_lim,
    run, u_sum, v_sum, q_col,
):
    west[...], east[...] = sort_in("gx", x_even_in[...], x_odd_in[...])
    south[...], north[...] = sort_in("gy", y_even_in[...], y_odd_in[...])
    face_limits(
        OUTER, count, west, east, south, north, east_lim, north_lim, south_lim, west_lim
    )
    row_fluxes(own_east, own_west, west, east, west_lim, east_lim, row_low, row_high)
    column_fluxes(
        OUTER, own_north, own_south, south, north, south_lim, north_lim, col_low, col_high
    )

    def place(b):
        return slice(0, 8) if b == 0 else slice(8, 16)

    solve(OUTER, place, source, inverse, link, col_low, col_high, row_low, row_high, solved)

    def keep_row(k, h, value):
        to_west[pl.ds(24 + 40 * h + k, 1), :] = value

    def drop(*args):
        pass

    momentum(
        OUTER, lambda k, b, h: solved[k, place(b), lanes_of(h)], lambda b: False,
        speeds, east_lim, north_lim, run, u_sum, v_sum, q_col, drop, drop, keep_row,
        UNROLL_OUT,
    )
    row_sum = row_face_sum(west_lim, lambda h: to_west[24 + 40 * h : 64 + 40 * h, :])
    u_sum[rows_of(BLOCKS - 2), :] = jnp.zeros((8, COLS), F32)

    def keep(b, tiles, side):
        for h in range(2):
            if b == 0:
                to_west[rows_of(h), :] = tiles[h]
                to_west[8 * h + 5 : 8 * h + 6, :] = row_sum[h][0:1]
            else:
                to_east[rows_of(h), :] = pltpu.roll(tiles[h], 5, 0)
                to_east[8 * h + 5 : 8 * h + 6, :] = u_sum[ROWS - 1 : ROWS, lanes_of(h)]
        if b == 0:
            to_west[16:24, :] = side
        else:
            to_east[16:24, :] = pltpu.roll(side, 5, 0)

    forcing(OUTER, u_sum, v_sum, row_sum, south_lim, q_col, count, rain, keep)
    to_east[24:104, :] = jnp.zeros((80, 128), F32)
    x_even[...], x_odd[...] = sort_out("gx", to_west[...], to_east[...])


def outer(*args):
    plane = pltpu.VMEM((ROWS, COLS), F32)
    strip = pltpu.VMEM((ROWS, 128), F32)
    levels = pltpu.VMEM((2, LEVELS, 128), F32)
    return pl.pallas_call(
        outer_kernel,
        out_shape=(shape(LEVELS, 16, COLS),)
        + (shape(104, 128),) * 4
        + (shape(2, 88, 128),) * 2
        + (shape(ROWS, 128),) * 2,
        in_specs=[VMEM] * 14,
        out_specs=(VMEM,) * 9,
        scratch_shapes=[
            levels, levels, strip, strip, plane, plane, strip, pltpu.VMEM((8, COLS), F32),
            plane, plane, plane, strip,
        ],
        compiler_params=params(LIMIT_COLUMNS),
        name="outer",
    )(*args)


def middle_kernel(
    source, inverse, link, speeds, count, rain, own_north, own_south,
    west, east, south, north, outside, own_west,
    solved, u_new, v_low, v_high, force_out, q_col, sides,
    col_low, col_high, east_lim, north_lim, south_lim, west_lim, run, u_sum, v_sum,
):
    every = tuple(range(BLOCKS))
    face_limits(
        every, count, west, east, south, north, east_lim, north_lim, south_lim, west_lim
    )
    column_fluxes(
        MIDDLE, own_north, own_south, south, north, south_lim, north_lim, col_low, col_high
    )

    def place(b):
        return rows_of(b - 1)

    solve(MIDDLE, place, source, inverse, link, col_low, col_high, None, None, solved)

    def values(k, b, h):
        if b == 0:
            return outside[k, 0:8, lanes_of(h)]
        if b == BLOCKS - 1:
            return outside[k, 8:16, lanes_of(h)]
        return solved[k, place(b), lanes_of(h)]

    def keep_u(k, b, h, speed):
        u_new[k, rows_of(b), lanes_of(h)] = speed

    def keep_v(k, b, h, speed):
        if h == 0:
            v_low[k, rows_of(b), :] = speed
        else:
            v_high[k, rows_of(b), :] = speed

    momentum(
        every, values, lambda b: b < BLOCKS - 1, speeds, east_lim, north_lim,
        run, u_sum, v_sum, q_col, keep_u, keep_v, lambda k, h, value: None,
        UNROLL_MOM,
    )
    row_sum = [
        jnp.broadcast_to(own_west[8 * h + 5 : 8 * h + 6, :], (8, 128)) for h in range(2)
    ]

    def keep(b, tiles, side):
        for h in range(2):
            force_out[rows_of(b), lanes_of(h)] = tiles[h]
        sides[rows_of(b), :] = side

    forcing(every, u_sum, v_sum, row_sum, south_lim, q_col, count, rain, keep)


def middle(*args):
    plane = pltpu.VMEM((ROWS, COLS), F32)
    strip = pltpu.VMEM((ROWS, 128), F32)
    half = shape(LEVELS, ROWS, 128)
    return pl.pallas_call(
        middle_kernel,
        out_shape=(
            shape(LEVELS, ROWS - 16, COLS), shape(LEVELS, ROWS, COLS), half, half,
            shape(ROWS, COLS), shape(ROWS, 128), shape(ROWS, 128),
        ),
        in_specs=[VMEM] * 14,
        out_specs=(VMEM,) * 7,
        scratch_shapes=[
            strip, strip, plane, plane, strip, pltpu.VMEM((8, COLS), F32), plane, plane, plane,
        ],
        cost_estimate=pl.CostEstimate(
            flops=30 * LEVELS * ROWS * COLS, bytes_accessed=16 * LEVELS * ROWS * COLS,
            transcendentals=0,
        ),
        compiler_params=params(LIMIT_COLUMNS),
        name="middle",
    )(*args)


EXT = ROWS + 16


def relax(force, count):
    wide = force.shape[1]
    root = jnp.sqrt(count * (1.0 / LEVELS))

    def total(field):
        sideways = pltpu.roll(field, 1, 1) + pltpu.roll(field, wide - 1, 1)
        mixed = field + 0.5 * sideways
        return sideways + (pltpu.roll(mixed, 1, 0) + pltpu.roll(mixed, EXT - 1, 0))

    inverse = 1.0 / (damping + root * total(root))
    force = force * inverse
    share = root * inverse
    update = force * (1.0 / cheb_gamma)
    iterate = update
    omega = 2.0 / cheb_gamma
    for step in range(1, ITERS):
        residual = (force - iterate) + share * total(root * iterate)
        omega = 1.0 / (cheb_gamma - omega / (4.0 * cheb_alpha * cheb_alpha))
        update = omega * residual + (cheb_gamma * omega - 1.0) * update
        iterate = iterate + update
    return iterate


def writer_kernel(
    outside, solved, u_new, v_low, from_east, count, east, force_ext, count_ext,
    temp_out, speeds_out, inner, u_fix, sems,
):
    copies = [
        (outside.at[:, pl.ds(0, 8), :], temp_out.at[:, pl.ds(0, 8), :]),
        (outside.at[:, pl.ds(8, 8), :], temp_out.at[:, pl.ds(ROWS - 8, 8), :]),
        (solved, temp_out.at[:, pl.ds(8, ROWS - 16), :]),
        (u_new.at[:, pl.ds(0, ROWS - 8), :], speeds_out.at[0, :, pl.ds(0, ROWS - 8), :]),
        (v_low, speeds_out.at[1, :, :, pl.ds(0, 128)]),
        (u_fix, speeds_out.at[0, :, pl.ds(ROWS - 8, 8), :]),
    ]
    copies = [
        pltpu.make_async_copy(origin, target, sems.at[n])
        for n, (origin, target) in enumerate(copies)
    ]
    for copy in copies[:-1]:
        copy.start()
    last_row = row_id() == 7
    for h in range(2):
        limit = jnp.minimum(
            count[ROWS - 8 :, lanes_of(h)], jnp.broadcast_to(east[h, 40:41, :], (8, 128))
        )
        limit = jnp.where(last_row, limit, 0.0)
        for k in range(LEVELS):
            at = 24 + 40 * h + k
            u_fix[k, :, lanes_of(h)] = u_new[k, ROWS - 8 :, lanes_of(h)] + jnp.where(
                float(k) < limit,
                PRESS * jnp.broadcast_to(from_east[at : at + 1, :], (8, 128)),
                0.0,
            )
    copies[-1].start()
    inner[...] = relax(force_ext[...], count_ext[...])[8 : 8 + ROWS]
    for copy in copies:
        copy.wait()


def writer(*args):
    return pl.pallas_call(
        writer_kernel,
        out_shape=(
            shape(LEVELS, ROWS, COLS), shape(2, LEVELS, ROWS, COLS), shape(ROWS, COLS)
        ),
        in_specs=[VMEM] * 9,
        out_specs=(ANY, ANY, VMEM),
        scratch_shapes=[
            pltpu.VMEM((LEVELS, 8, COLS), F32),
            pltpu.SemaphoreType.DMA((6,)),
        ],
        cost_estimate=pl.CostEstimate(
            flops=LEVELS * ROWS * COLS, bytes_accessed=12 * LEVELS * ROWS * COLS,
            transcendentals=0,
        ),
        compiler_params=params(LIMIT_COLUMNS),
        name="writer",
    )(*args)


def edges_kernel(
    force, sides, q_col, count, west, east_in, own_east, own_west, x_odd, x_even,
    force_ext, count_ext, sides_ext, y_odd, y_even, from_east, from_west, to_north, to_south,
):
    from_west[...], from_east[...] = sort_in("gx", x_even[...], x_odd[...])
    zeros8 = jnp.zeros((8, COLS), F32)
    count_ext[0:8, :] = zeros8
    for h in range(2):
        count_ext[2:8, lanes_of(h)] = west[h, 80:86, :]
    count_ext[8 : 8 + ROWS, :] = count[...]
    count_ext[8 + ROWS :, :] = zeros8
    for h in range(2):
        count_ext[8 + ROWS : 14 + ROWS, lanes_of(h)] = east_in[h, 40:46, :]
    sides_ext[0:8, :] = jnp.zeros((8, 128), F32)
    sides_ext[3:8, :] = from_west[16:21, :]
    sides_ext[8 : 8 + ROWS, :] = sides[...]
    sides_ext[8 + ROWS :, :] = jnp.zeros((8, 128), F32)
    sides_ext[8 + ROWS : 13 + ROWS, :] = from_east[16:21, :]
    force_ext[0:8, :] = zeros8
    for h in range(2):
        force_ext[3:8, lanes_of(h)] = from_west[8 * h : 8 * h + 5, :]
    force_ext[8 : 8 + ROWS, :] = force[...]
    force_ext[8 + ROWS :, :] = zeros8
    for h in range(2):
        force_ext[8 + ROWS : 13 + ROWS, lanes_of(h)] = from_east[8 * h : 8 * h + 5, :]

    def add(at, sign, ref):
        for h in range(2):
            place = (slice(at, at + 1), lanes_of(h))
            force_ext[place] = force_ext[place] + jnp.where(
                count_ext[place] > 0.0, sign * DIVERGE * ref[8 * h + 5 : 8 * h + 6, :], 0.0
            )

    add(7, -1.0, own_west)
    add(8, 1.0, from_west)
    add(7 + ROWS, -1.0, from_east)
    add(8 + ROWS, 1.0, own_east)
    lane = lane_id(EXT)
    side = sides_ext[...]
    to_north[...] = jnp.where(
        lane >= 123,
        force_ext[:, 128:],
        jnp.where(lane == 0, side, pltpu.roll(count_ext[:, 128:], 122, 1)),
    )
    to_south[...] = jnp.where(
        lane < 5,
        force_ext[:, :128],
        jnp.where(lane == 127, side, pltpu.roll(count_ext[:, :128], 8, 1)),
    )
    lane = lane_id(ROWS)
    to_south[8 : 8 + ROWS, :] = jnp.where(
        (lane >= 64) & (lane < 64 + LEVELS),
        pltpu.roll(q_col[...], 64, 1),
        to_south[8 : 8 + ROWS, :],
    )
    y_even[...], y_odd[...] = sort_out("gy", to_south[...], to_north[...])


def edges(*args):
    return pl.pallas_call(
        edges_kernel,
        out_shape=(
            shape(EXT, COLS), shape(EXT, COLS), shape(EXT, 128), shape(EXT, 128), shape(EXT, 128),
            shape(104, 128),
        ),
        in_specs=[VMEM] * 10,
        out_specs=(VMEM,) * 6,
        scratch_shapes=[
            pltpu.VMEM((104, 128), F32), pltpu.VMEM((EXT, 128), F32), pltpu.VMEM((EXT, 128), F32)
        ],
        compiler_params=params(LIMIT_COLUMNS),
        name="edges",
    )(*args)


def final_kernel(
    speeds, v_high, count, inner, force_ext, count_ext, sides_ext, y_odd, y_even,
    speeds_out, out, v_fix, south, north, sems,
):
    south[...], north[...] = sort_in("gy", y_even[...], y_odd[...])
    last_lane = lane_id(8) == 127
    limits = []
    for b in range(BLOCKS):
        limit = jnp.minimum(
            count[rows_of(b), 128:], pltpu.roll(north[rows_of(b + 1), :], 127 - 8, 1)
        )
        limits.append(jnp.where(last_lane, limit, 0.0))

    def save(c):
        part = pl.ds(c * FIX_CHUNK, FIX_CHUNK)
        return pltpu.make_async_copy(
            v_fix.at[part], speeds_out.at[1, part, :, pl.ds(128, 128)], sems.at[c]
        )

    for c in range(LEVELS // FIX_CHUNK):
        for k in range(c * FIX_CHUNK, (c + 1) * FIX_CHUNK):
            for b in range(BLOCKS):
                rows = rows_of(b)
                v_fix[k, rows, :] = v_high[k, rows, :] + jnp.where(
                    float(k) < limits[b],
                    PRESS * pltpu.roll(north[rows_of(b + 1), :], 63 - k, 1),
                    0.0,
                )
        save(c).start()

    @pl.when(lax.axis_index("gx") >= 0)
    def _():
        lane = lane_id(EXT)
        count_side = jnp.where(
            lane >= 122,
            pltpu.roll(south[...], 6, 1),
            jnp.where(lane < 6, pltpu.roll(north[...], 120, 1), 0.0),
        )
        force_side = jnp.where(
            lane >= 123, south[...], jnp.where(lane < 5, north[...], 0.0)
        )
        side = sides_ext[...]
        low, high = force_ext[:, :128], force_ext[:, 128:]
        low = low + jnp.where(
            (lane == 0) & (count_ext[:, :128] > 0.0), DIVERGE * south[...], 0.0
        )
        high = high - jnp.where(
            (lane == 127) & (count_ext[:, 128:] > 0.0), DIVERGE * north[...], 0.0
        )
        force_side = force_side + jnp.where(
            (lane == 0) & (count_side > 0.0), DIVERGE * side, 0.0
        )
        force_side = force_side - jnp.where(
            (lane == 127) & (count_side > 0.0), DIVERGE * side, 0.0
        )
        left = (lane < 32) | (lane >= 96)

        def strip(low, high, side):
            return jnp.where(
                left,
                jnp.where(lane < 64, low, side),
                pltpu.roll(jnp.where(lane >= 64, high, side), 64, 1),
            )

        near = relax(
            strip(low, high, force_side), strip(count_ext[:, :128], count_ext[:, 128:], count_side)
        )[8 : 8 + ROWS]
        lane = lane_id(ROWS)
        out[:, :128] = jnp.where(lane < 6, near, inner[:, :128])
        out[:, 128:] = jnp.where(lane >= 122, pltpu.roll(near, 64, 1), inner[:, 128:])
    for c in range(LEVELS // FIX_CHUNK):
        save(c).wait()


def final(*args):
    return pl.pallas_call(
        final_kernel,
        out_shape=(shape(2, LEVELS, ROWS, COLS), shape(ROWS, COLS)),
        in_specs=[ANY] + [VMEM] * 8,
        out_specs=(ANY, VMEM),
        scratch_shapes=[
            pltpu.VMEM((LEVELS, ROWS, 128), F32),
            pltpu.VMEM((EXT, 128), F32), pltpu.VMEM((EXT, 128), F32),
            pltpu.SemaphoreType.DMA((LEVELS // FIX_CHUNK,)),
        ],
        input_output_aliases={0: 0},
        compiler_params=params(LIMIT_COLUMNS),
        name="final",
    )(*args)


def swap(array, axis, first):
    count = lax.axis_size(axis)
    pairs = []
    for low in range(first, count + first, 2):
        low, high = low % count, (low + 1) % count
        pairs += [(low, high), (high, low)]
    return lax.ppermute(array, axis, pairs)


def local(
    thermal_departure,
    current_speeds,
    mixing_coefficient,
    seawater_indicator,
    submerged_layer_tally,
    rainfall_runoff_input,
):
    near, count, to_east, to_west, to_north, to_south, y_odd, y_even, x_odd, x_even = pack(
        *(
            pltpu.with_memory_space_constraint(x, pltpu.HBM)
            for x in (
                thermal_departure, current_speeds, seawater_indicator, submerged_layer_tally
            )
        )
    )
    y_odd = swap(y_odd, "gy", 1)
    y_even = swap(y_even, "gy", 0)
    x_odd = swap(x_odd, "gx", 1)
    x_even = swap(x_even, "gx", 0)
    speeds, mixing = (
        pltpu.with_memory_space_constraint(x, pltpu.VMEM)
        for x in (current_speeds, mixing_coefficient)
    )
    inside = (*interior(near, speeds, mixing, count), speeds)
    outside, own_east, own_west, x_odd, x_even, west, east, south, north = outer(
        *inside, count, rainfall_runoff_input, to_east, to_west, to_north, to_south,
        y_odd, y_even, x_odd, x_even,
    )
    x_odd = swap(x_odd, "gx", 1)
    x_even = swap(x_even, "gx", 0)
    solved, u_new, v_low, v_high, force, q_col, sides = middle(
        *inside, count, rainfall_runoff_input, to_north, to_south,
        west, east, south, north, outside, own_west,
    )
    force_ext, count_ext, sides_ext, y_odd, y_even, from_east = edges(
        force, sides, q_col, count, west, east, own_east, own_west, x_odd, x_even
    )
    y_odd = swap(y_odd, "gy", 1)
    y_even = swap(y_even, "gy", 0)
    temp_next, stored, inner = writer(
        outside, solved, u_new, v_low, from_east, count, east, force_ext, count_ext
    )
    velocity_next, surface = final(
        stored, v_high, count, inner, force_ext, count_ext, sides_ext, y_odd, y_even,
    )
    return (temp_next, velocity_next, surface)


def solution(mesh):
    placed = (
        P(None, "gx", "gy"),
        P(None, None, "gx", "gy"),
        P(None, "gx", "gy"),
        P("gx", "gy"),
        P("gx", "gy"),
        P("gx", "gy"),
    )
    return jax.shard_map(
        local,
        mesh=mesh,
        in_specs=placed,
        out_specs=(P(None, "gx", "gy"), P(None, None, "gx", "gy"), P("gx", "gy")),
        check_vma=False,
    )
```

```python
import jax
import jax.numpy as jnp
from jax import lax
from jax.experimental import pallas as pl
from jax.experimental.pallas import tpu as pltpu
from jax.sharding import PartitionSpec as P

ITERS = 6
FIX_CHUNK = 20
COST = 10000
LIMIT_PACK = 12
LIMIT_INTERIOR = 8
LIMIT_COLUMNS = 12
LEVELS = 40
ROWS = 64
COLS = 256
BLOCKS = ROWS // 8
CHUNK = 20
CHUNKS = LEVELS // CHUNK

damping = 0.05
lower_bound = 0.02
upper_bound = 2.0
cheb_alpha = 2.0 / (upper_bound - lower_bound)
cheb_gamma = (upper_bound + lower_bound) / 2.0
advect_scale = 0.4
force_scale = 4.0
source_scale = 0.5
divergence_scale = 4.0
PRESS = force_scale / LEVELS
DIVERGE = divergence_scale / LEVELS

VMEM = pl.BlockSpec(memory_space=pltpu.VMEM)
ANY = pl.BlockSpec(memory_space=pl.ANY)
HBM = pl.BlockSpec(memory_space=pltpu.HBM)
F32 = jnp.float32
TILES = [(b, h) for b in range(BLOCKS) for h in range(2)]


def shape(*dims):
    return jax.ShapeDtypeStruct(dims, F32)


def params(mebibytes=40):
    return pltpu.CompilerParams(vmem_limit_bytes=int(mebibytes * 1024 * 1024))


def lane_id(rows=8):
    return lax.broadcasted_iota(jnp.int32, (rows, 128), 1)


def row_id():
    return lax.broadcasted_iota(jnp.int32, (8, 128), 0)


def rows_of(b):
    return slice(8 * b, 8 * b + 8)


def lanes_of(h):
    return slice(128 * h, 128 * h + 128)


def odd_place(axis):
    return lax.axis_index(axis) % 2 == 1


def sort_out(axis, lower, upper):
    odd = odd_place(axis)
    return jnp.where(odd, lower, upper), jnp.where(odd, upper, lower)


def sort_in(axis, even_pair, odd_pair):
    odd = odd_place(axis)
    return jnp.where(odd, even_pair, odd_pair), jnp.where(odd, odd_pair, even_pair)


def tiles_of(ref, *lead):
    return {(b, h): ref[(*lead, rows_of(b), lanes_of(h))] for b, h in TILES}


def next_row(x, after, last):
    turned = {t: pltpu.roll(x[t], 7, 0) for t in TILES}
    return {
        (b, h): jnp.where(last, after[h] if b == BLOCKS - 1 else turned[b + 1, h], turned[b, h])
        for b, h in TILES
    }


def prev_row(x, before, first):
    turned = {t: pltpu.roll(x[t], 1, 0) for t in TILES}
    return {
        (b, h): jnp.where(first, before[h] if b == 0 else turned[b - 1, h], turned[b, h])
        for b, h in TILES
    }


def next_col(x, after, last):
    turned = {t: pltpu.roll(x[t], 127, 1) for t in TILES}
    return {
        (b, h): jnp.where(last, after[b] if h == 1 else turned[b, 1], turned[b, h])
        for b, h in TILES
    }


def prev_col(x, before, first):
    turned = {t: pltpu.roll(x[t], 1, 1) for t in TILES}
    return {
        (b, h): jnp.where(first, before[b] if h == 0 else turned[b, 0], turned[b, h])
        for b, h in TILES
    }


def spread(ref, k, h):
    return jnp.broadcast_to(ref[h, pl.ds(k, 1), :], (8, 128))


def pack_kernel(
    temp, speeds, sea_in, tally_in,
    near, count_out, to_east, to_west, to_north, to_south, y_odd, y_even, x_odd, x_even,
    v_high, u_end, sea, tally, sems, part_sems,
):
    first = [
        pltpu.make_async_copy(sea_in, sea, sems.at[0]),
        pltpu.make_async_copy(tally_in, tally, sems.at[1]),
    ]
    parts = []
    for c in range(CHUNKS):
        part = pl.ds(c * CHUNK, CHUNK)
        parts.append(
            (
                pltpu.make_async_copy(temp.at[part], near.at[part], part_sems.at[0, c]),
                pltpu.make_async_copy(
                    speeds.at[1, part, :, pl.ds(128, 128)], v_high.at[part], part_sems.at[1, c]
                ),
            )
        )
    last = pltpu.make_async_copy(speeds.at[0, :, pl.ds(ROWS - 8, 8), :], u_end, sems.at[2])
    for copy in first:
        copy.start()
    for pair in parts:
        for copy in pair:
            copy.start()
    last.start()

    for copy in first:
        copy.wait()
    latitude = lax.axis_index("gy") * COLS + lax.broadcasted_iota(jnp.int32, (ROWS, COLS), 1)
    inner = (latitude > 0) & (latitude < lax.axis_size("gy") * COLS - 1)
    count = jnp.where(inner & (sea[...] == 1), tally[...], 0).astype(F32)
    count_out[...] = count
    for h in range(2):
        to_east[h, 80:86, :] = count[ROWS - 6 :, lanes_of(h)]
        to_east[h, 86:88, :] = jnp.zeros((2, 128), F32)
        to_west[h, 40:46, :] = count[:6, lanes_of(h)]
        to_west[h, 46:88, :] = jnp.zeros((42, 128), F32)
    lane = lane_id()
    low, high = [], []
    for b in range(BLOCKS):
        low.append(pltpu.roll(count[rows_of(b), :128], 40, 1))
        high.append(pltpu.roll(count[rows_of(b), 128:], (80 - 127) % 128, 1))

    for c in range(CHUNKS):
        parts[c][0].wait()
        parts[c][1].wait()
        for k in range(c * CHUNK, (c + 1) * CHUNK):
            for b in range(BLOCKS):
                rows = rows_of(b)
                low[b] = jnp.where(lane == k, pltpu.roll(near[k, rows, :128], k, 1), low[b])
                high[b] = jnp.where(lane == k, pltpu.roll(near[k, rows, 128:], k + 1, 1), high[b])
                high[b] = jnp.where(
                    lane == k + 40, pltpu.roll(v_high[k, rows, :], k + 41, 1), high[b]
                )
        levels = slice(c * CHUNK, (c + 1) * CHUNK)
        for h in range(2):
            to_west[h, levels, :] = near[levels, 0, lanes_of(h)]
            to_east[h, levels, :] = near[levels, ROWS - 1, lanes_of(h)]
    for b in range(BLOCKS):
        to_south[rows_of(b), :] = low[b]
        to_north[rows_of(b), :] = high[b]
        y_even[rows_of(b), :], y_odd[rows_of(b), :] = sort_out("gy", low[b], high[b])
    last.wait()
    for h in range(2):
        to_east[h, 40:80, :] = u_end[:, 7, lanes_of(h)]
    x_even[...], x_odd[...] = sort_out("gx", to_west[...], to_east[...])


def pack(*args):
    return pl.pallas_call(
        pack_kernel,
        out_shape=(
            shape(LEVELS, ROWS, COLS), shape(ROWS, COLS),
            shape(2, 88, 128), shape(2, 88, 128), shape(ROWS, 128), shape(ROWS, 128),
            shape(ROWS, 128), shape(ROWS, 128), shape(2, 88, 128), shape(2, 88, 128),
        ),
        in_specs=[HBM] * 4,
        out_specs=(VMEM,) * 10,
        scratch_shapes=[
            pltpu.VMEM((LEVELS, ROWS, 128), F32),
            pltpu.VMEM((LEVELS, 8, COLS), F32),
            pltpu.VMEM((ROWS, COLS), jnp.int32),
            pltpu.VMEM((ROWS, COLS), jnp.int32),
            pltpu.SemaphoreType.DMA((3,)),
            pltpu.SemaphoreType.DMA((2, CHUNKS)),
        ],
        compiler_params=params(LIMIT_PACK),
        name="pack",
    )(*args)


UNROLL_IN = 4
UNROLL_FWD = 20
UNROLL_BACK = 20
UNROLL_MOM = 8
UNROLL_OUT = 40


def interior_kernel(
    tb, speeds, mb, count,
    source_out, inverse_out, link_out,
    east_lim, north_lim,
):
    lane, row = lane_id(), row_id()
    first_row, last_row = row == 0, row == 7
    first_lane, last_lane = lane == 0, lane == 127
    zero = jnp.zeros((8, 128), F32)
    pair = range(2)

    counts = tiles_of(count)
    ahead = next_row(counts, [zero, zero], last_row)
    for b, h in TILES:
        east_lim[rows_of(b), lanes_of(h)] = jnp.minimum(counts[b, h], ahead[b, h])
    ahead = next_col(counts, [zero] * BLOCKS, last_lane)
    for b, h in TILES:
        north_lim[rows_of(b), lanes_of(h)] = jnp.minimum(counts[b, h], ahead[b, h])

    def level_step(k, factors, links, opens=None):
        level = k.astype(F32)
        below_at = jnp.minimum(k + 1, LEVELS - 1)
        t_next = [tb[k, rows_of(0), lanes_of(h)] for h in pair]
        turned_next = [pltpu.roll(t_next[h], 7, 0) for h in pair]
        flux_turned = [zero, zero]
        new_factors, new_links, new_opens = [], [], []
        for b in range(BLOCKS):
            rows = rows_of(b)
            t, turned = t_next, turned_next
            if b < BLOCKS - 1:
                t_next = [tb[k, rows_of(b + 1), lanes_of(h)] for h in pair]
                turned_next = [pltpu.roll(t_next[h], 7, 0) for h in pair]
            u = [speeds[0, k, rows, lanes_of(h)] for h in pair]
            v = [speeds[1, k, rows, lanes_of(h)] for h in pair]
            change = []
            for h in pair:
                ahead = jnp.where(last_row, turned_next[h], turned[h])
                flux = jnp.where(level < east_lim[rows, lanes_of(h)], u[h], 0.0) * jnp.where(
                    u[h] > 0.0, t[h], ahead
                )
                flux_before, flux_turned[h] = flux_turned[h], pltpu.roll(flux, 1, 0)
                change.append(flux - jnp.where(first_row, flux_before, flux_turned[h]))
            left = [pltpu.roll(t[h], 127, 1) for h in pair]
            ahead = [jnp.where(last_lane, left[1], left[0]), left[1]]
            flux = [
                jnp.where(level < north_lim[rows, lanes_of(h)], v[h], 0.0)
                * jnp.where(v[h] > 0.0, t[h], ahead[h])
                for h in pair
            ]
            right = [pltpu.roll(flux[h], 1, 1) for h in pair]
            behind = [jnp.where(first_lane, 0.0, right[0]), jnp.where(first_lane, right[0], right[1])]
            for h in pair:
                n = 2 * b + h
                at = (k, rows, lanes_of(h))
                wet = count[rows, lanes_of(h)]
                total = change[h] + (flux[h] - behind[h])
                open_here = level < wet if opens is None else opens[n]
                open_below = level + 1.0 < wet
                source_out[at] = t[h] - jnp.where(open_here, advect_scale * total, 0.0)
                a = links[n]
                below = jnp.where(open_below, mb[below_at, rows, lanes_of(h)], 0.0)
                pivot = (1.0 + below) + (a - a * factors[n])
                inverse = pl.reciprocal(pivot, approx=True)
                inverse = inverse * (2.0 - pivot * inverse)
                inverse_out[at] = inverse
                link_out[at] = a
                new_factors.append(below * inverse)
                new_links.append(below)
                new_opens.append(open_below)
        return tuple(new_factors), tuple(new_links), new_opens

    def step(m, carry):
        for n in range(UNROLL_IN):
            carry = level_step(m * UNROLL_IN + n, *carry)
        return carry[:2]

    blank = tuple(zero for _ in TILES)
    lax.fori_loop(0, LEVELS // UNROLL_IN, step, (blank, blank))


def interior(temp, speeds, mix, count):
    block = shape(LEVELS, ROWS, COLS)
    return pl.pallas_call(
        interior_kernel,
        out_shape=(block,) * 3,
        in_specs=[VMEM] * 4,
        out_specs=(VMEM,) * 3,
        scratch_shapes=[
            pltpu.VMEM((ROWS, COLS), F32), pltpu.VMEM((ROWS, COLS), F32),
        ],
        cost_estimate=pl.CostEstimate(
            flops=COST * LEVELS * ROWS * COLS, bytes_accessed=COST * LEVELS * ROWS * COLS,
            transcendentals=0,
        ),
        compiler_params=params(LIMIT_INTERIOR),
        name="interior",
    )(temp, speeds, mix, count)


OUTER = (0, BLOCKS - 1)
MIDDLE = tuple(range(1, BLOCKS - 1))


def face_limits(
    blocks, count, west, east, south, north, east_lim, north_lim, south_lim, west_lim
):
    lane, row = lane_id(), row_id()
    last_row, last_lane = row == 7, lane == 127
    counts = tiles_of(count)
    pair = range(2)
    for h in pair:
        before = jnp.broadcast_to(west[h, 85:86, :], (8, 128))
        west_lim[:, lanes_of(h)] = jnp.minimum(counts[0, h], before)
        for b in blocks:
            if b == BLOCKS - 1:
                after = jnp.broadcast_to(east[h, 40:41, :], (8, 128))
            else:
                after = pltpu.roll(counts[b + 1, h], 7, 0)
            ahead = jnp.where(last_row, after, pltpu.roll(counts[b, h], 7, 0))
            east_lim[rows_of(b), lanes_of(h)] = jnp.minimum(counts[b, h], ahead)
    for b in blocks:
        rows = rows_of(b)
        left = [pltpu.roll(counts[b, h], 127, 1) for h in pair]
        left.append(pltpu.roll(north[rows, :], 127 - 40, 1))
        for h in pair:
            ahead = jnp.where(last_lane, left[h + 1], left[h])
            north_lim[rows, lanes_of(h)] = jnp.minimum(counts[b, h], ahead)
        south_lim[rows, :] = jnp.minimum(counts[b, 0], pltpu.roll(south[rows, :], 128 - 80, 1))


def column_fluxes(
    blocks, own_north, own_south, south, north, south_lim, north_lim, col_low, col_high
):
    depth = lane_id().astype(F32)
    for b in blocks:
        rows = rows_of(b)
        limit = jnp.broadcast_to(south_lim[rows, 0:1], (8, 128))
        speed = pltpu.roll(south[rows, :], 128 - 40, 1)
        col_low[rows, :] = (
            advect_scale
            * jnp.where(depth < limit, speed, 0.0)
            * jnp.where(speed > 0.0, south[rows, :], own_south[rows, :])
        )
        limit = jnp.broadcast_to(north_lim[rows, COLS - 1 : COLS], (8, 128))
        speed = pltpu.roll(own_north[rows, :], 128 - 40, 1)
        col_high[rows, :] = (
            -advect_scale
            * jnp.where(depth < limit, speed, 0.0)
            * jnp.where(speed > 0.0, own_north[rows, :], north[rows, :])
        )


def row_fluxes(own_east, own_west, west, east, west_lim, east_lim, row_low, row_high):
    depth = lax.broadcasted_iota(jnp.int32, (LEVELS, 128), 0).astype(F32)
    for h in range(2):
        speed = west[h, 40:80, :]
        row_low[h] = (
            advect_scale
            * jnp.where(depth < west_lim[0:1, lanes_of(h)], speed, 0.0)
            * jnp.where(speed > 0.0, west[h, 0:40, :], own_west[h, 0:40, :])
        )
        speed = own_east[h, 40:80, :]
        row_high[h] = (
            -advect_scale
            * jnp.where(depth < east_lim[ROWS - 1 : ROWS, lanes_of(h)], speed, 0.0)
            * jnp.where(speed > 0.0, own_east[h, 0:40, :], east[h, 0:40, :])
        )


def solve(blocks, place, source, inverse, link, col_low, col_high, row_low, row_high, solved):
    lane, row = lane_id(), row_id()
    first_row, last_row = row == 0, row == 7
    first_lane, last_lane = lane == 0, lane == 127
    zero = jnp.zeros((8, 128), F32)
    pair = range(2)

    def forward(k, values):
        out = []
        for n, b in enumerate(blocks):
            rows = rows_of(b)
            add = [
                jnp.where(first_lane, pltpu.roll(col_low[rows, :], 128 - k, 1), 0.0),
                jnp.where(last_lane, pltpu.roll(col_high[rows, :], 127 - k, 1), 0.0),
            ]
            for h in pair:
                at = (k, rows, lanes_of(h))
                total = source[at] + add[h]
                if b == 0:
                    total = total + jnp.where(first_row, spread(row_low, k, h), 0.0)
                if b == BLOCKS - 1:
                    total = total + jnp.where(last_row, spread(row_high, k, h), 0.0)
                turn = inverse[at]
                value = total * turn + (link[at] * turn) * values[2 * n + h]
                solved[k, place(b), lanes_of(h)] = value
                out.append(value)
        return tuple(out)

    blank = (zero,) * (2 * len(blocks))

    def forward_step(m, values):
        for n in range(UNROLL_FWD):
            values = forward(m * UNROLL_FWD + n, values)
        return values

    lax.fori_loop(0, LEVELS // UNROLL_FWD, forward_step, blank)

    def back_step(m, below):
        for n in range(UNROLL_BACK):
            k = LEVELS - 1 - m * UNROLL_BACK - n
            below_at = jnp.minimum(k + 1, LEVELS - 1)
            out = []
            for i, value in zip([(b, h) for b in blocks for h in pair], below):
                at = (rows_of(i[0]), lanes_of(i[1]))
                to = (k, place(i[0]), lanes_of(i[1]))
                value = solved[to] + (inverse[(k, *at)] * link[(below_at, *at)]) * value
                solved[to] = value
                out.append(value)
            below = tuple(out)
        return below

    lax.fori_loop(0, LEVELS // UNROLL_BACK, back_step, blank)


def row_face_sum(west_lim, q_rows):
    depth = lax.broadcasted_iota(jnp.int32, (LEVELS, 128), 0).astype(F32)
    out = []
    for h in range(2):
        part = jnp.where(depth < west_lim[0:1, lanes_of(h)], PRESS * q_rows(h), 0.0)
        out.append(jnp.broadcast_to(jnp.sum(part, axis=0, keepdims=True), (8, 128)))
    return out


def col_face_sum(rows, south_lim, q_col):
    limit = jnp.broadcast_to(south_lim[rows, 0:1], (8, 128))
    part = jnp.where(lane_id().astype(F32) < limit, PRESS * q_col[rows, :], 0.0)
    return jnp.broadcast_to(jnp.sum(part, axis=1, keepdims=True), (8, 128))


def momentum(
    blocks, values, following, speeds, east_lim, north_lim, run, u_sum, v_sum, q_col,
    keep_u, keep_v, keep_row, unroll,
):
    lane, row = lane_id(), row_id()
    last_row, last_lane = row == 7, lane == 127
    zero = jnp.zeros((8, 128), F32)
    pair = range(2)
    many = range(unroll)
    for b in blocks:
        run[rows_of(b), :] = jnp.zeros((8, COLS), F32)
        u_sum[rows_of(b), :] = jnp.zeros((8, COLS), F32)
        v_sum[rows_of(b), :] = jnp.zeros((8, COLS), F32)
        q_col[rows_of(b), :] = zero

    def step(m, _):
        first = m * unroll
        levels = [first + n for n in many]
        depths = [k.astype(F32) for k in levels]

        def running(b):
            out = []
            for h in pair:
                at = (rows_of(b), lanes_of(h))
                total = run[at]
                qs = []
                for k in levels:
                    half = 0.5 * values(k, b, h)
                    qs.append(total + half)
                    total = qs[-1] + half
                run[at] = total
                out.append(qs)
            return out

        q_next = None
        for b in blocks:
            rows = rows_of(b)
            if q_next is None:
                q = running(b)
                turned = [[pltpu.roll(x, 7, 0) for x in q[h]] for h in pair]
            else:
                q, turned = q_next, turned_next
            if b == 0:
                for h in pair:
                    for n in many:
                        keep_row(levels[n], h, q[h][n][0:1])
            if following(b):
                q_next = running(b + 1)
                turned_next = [[pltpu.roll(x, 7, 0) for x in q_next[h]] for h in pair]
            else:
                q_next, turned_next = None, [[zero] * unroll] * 2
            left = [[pltpu.roll(x, 127, 1) for x in q[h]] for h in pair]
            column = q_col[rows, :]
            for n in many:
                column = jnp.where(lane == levels[n], pltpu.roll(q[0][n], levels[n], 1), column)
            q_col[rows, :] = column
            for h in pair:
                at = (rows, lanes_of(h))
                limit = east_lim[at]
                total = u_sum[at]
                for n in many:
                    ahead = jnp.where(last_row, turned_next[h][n], turned[h][n])
                    speed = jnp.where(
                        depths[n] < limit, speeds[(0, levels[n], *at)] - PRESS * (q[h][n] - ahead), 0.0
                    )
                    keep_u(levels[n], b, h, speed)
                    total = total + speed
                u_sum[at] = total
                limit = north_lim[at]
                total = v_sum[at]
                for n in many:
                    ahead = jnp.where(last_lane, left[1][n] if h == 0 else 0.0, left[h][n])
                    speed = jnp.where(
                        depths[n] < limit, speeds[(1, levels[n], *at)] - PRESS * (q[h][n] - ahead), 0.0
                    )
                    keep_v(levels[n], b, h, speed)
                    total = total + speed
                v_sum[at] = total
        return 0

    lax.fori_loop(0, LEVELS // unroll, step, 0)


def forcing(blocks, u_sum, v_sum, row_sum, south_lim, q_col, count, rain, keep):
    lane, row = lane_id(), row_id()
    first_row, first_lane, last_lane = row == 0, lane == 0, lane == 127
    pair = range(2)
    for b in blocks:
        rows = rows_of(b)
        col_sum = col_face_sum(rows, south_lim, q_col)
        u = [u_sum[rows, lanes_of(h)] for h in pair]
        v = [v_sum[rows, lanes_of(h)] for h in pair]
        right = [pltpu.roll(v[h], 1, 1) for h in pair]
        v_before = [
            jnp.where(first_lane, col_sum, right[0]), jnp.where(first_lane, right[0], right[1])
        ]
        tiles = []
        for h in pair:
            at = (rows, lanes_of(h))
            if b == 0:
                before = row_sum[h]
            else:
                before = pltpu.roll(u_sum[rows_of(b - 1), lanes_of(h)], 1, 0)
            u_before = jnp.where(first_row, before, pltpu.roll(u[h], 1, 0))
            divergence = (u[h] - u_before) + (v[h] - v_before[h])
            tiles.append(
                jnp.where(count[at] > 0.0, source_scale * rain[at] - DIVERGE * divergence, 0.0)
            )
        side = jnp.where(first_lane, right[1], jnp.where(last_lane, col_sum, 0.0))
        keep(b, tiles, side)


def outer_kernel(
    source, inverse, link, speeds, count, rain, own_east, own_west, own_north, own_south,
    y_odd_in, y_even_in, x_odd_in, x_even_in,
    solved, to_east, to_west, x_odd, x_even, west, east, south, north,
    row_low, row_high, col_low, col_high, east_lim, north_lim, south_lim, west_lim,
    run, u_sum, v_sum, q_col,
):
    west[...], east[...] = sort_in("gx", x_even_in[...], x_odd_in[...])
    south[...], north[...] = sort_in("gy", y_even_in[...], y_odd_in[...])
    face_limits(
        OUTER, count, west, east, south, north, east_lim, north_lim, south_lim, west_lim
    )
    row_fluxes(own_east, own_west, west, east, west_lim, east_lim, row_low, row_high)
    column_fluxes(
        OUTER, own_north, own_south, south, north, south_lim, north_lim, col_low, col_high
    )

    def place(b):
        return slice(0, 8) if b == 0 else slice(8, 16)

    solve(OUTER, place, source, inverse, link, col_low, col_high, row_low, row_high, solved)

    def keep_row(k, h, value):
        to_west[pl.ds(24 + 40 * h + k, 1), :] = value

    def drop(*args):
        pass

    momentum(
        OUTER, lambda k, b, h: solved[k, place(b), lanes_of(h)], lambda b: False,
        speeds, east_lim, north_lim, run, u_sum, v_sum, q_col, drop, drop, keep_row,
        UNROLL_OUT,
    )
    row_sum = row_face_sum(west_lim, lambda h: to_west[24 + 40 * h : 64 + 40 * h, :])
    u_sum[rows_of(BLOCKS - 2), :] = jnp.zeros((8, COLS), F32)

    def keep(b, tiles, side):
        for h in range(2):
            if b == 0:
                to_west[rows_of(h), :] = tiles[h]
                to_west[8 * h + 5 : 8 * h + 6, :] = row_sum[h][0:1]
            else:
                to_east[rows_of(h), :] = pltpu.roll(tiles[h], 5, 0)
                to_east[8 * h + 5 : 8 * h + 6, :] = u_sum[ROWS - 1 : ROWS, lanes_of(h)]
        if b == 0:
            to_west[16:24, :] = side
        else:
            to_east[16:24, :] = pltpu.roll(side, 5, 0)

    forcing(OUTER, u_sum, v_sum, row_sum, south_lim, q_col, count, rain, keep)
    to_east[24:104, :] = jnp.zeros((80, 128), F32)
    x_even[...], x_odd[...] = sort_out("gx", to_west[...], to_east[...])


def outer(*args):
    plane = pltpu.VMEM((ROWS, COLS), F32)
    strip = pltpu.VMEM((ROWS, 128), F32)
    levels = pltpu.VMEM((2, LEVELS, 128), F32)
    return pl.pallas_call(
        outer_kernel,
        out_shape=(shape(LEVELS, 16, COLS),)
        + (shape(104, 128),) * 4
        + (shape(2, 88, 128),) * 2
        + (shape(ROWS, 128),) * 2,
        in_specs=[VMEM] * 14,
        out_specs=(VMEM,) * 9,
        scratch_shapes=[
            levels, levels, strip, strip, plane, plane, strip, pltpu.VMEM((8, COLS), F32),
            plane, plane, plane, strip,
        ],
        compiler_params=params(LIMIT_COLUMNS),
        name="outer",
    )(*args)


def middle_kernel(
    source, inverse, link, speeds, count, rain, own_north, own_south,
    west, east, south, north, outside, own_west,
    solved, u_new, v_low, v_high, force_out, q_col, sides,
    col_low, col_high, east_lim, north_lim, south_lim, west_lim, run, u_sum, v_sum,
):
    every = tuple(range(BLOCKS))
    face_limits(
        every, count, west, east, south, north, east_lim, north_lim, south_lim, west_lim
    )
    column_fluxes(
        MIDDLE, own_north, own_south, south, north, south_lim, north_lim, col_low, col_high
    )

    def place(b):
        return rows_of(b - 1)

    solve(MIDDLE, place, source, inverse, link, col_low, col_high, None, None, solved)

    def values(k, b, h):
        if b == 0:
            return outside[k, 0:8, lanes_of(h)]
        if b == BLOCKS - 1:
            return outside[k, 8:16, lanes_of(h)]
        return solved[k, place(b), lanes_of(h)]

    def keep_u(k, b, h, speed):
        u_new[k, rows_of(b), lanes_of(h)] = speed

    def keep_v(k, b, h, speed):
        if h == 0:
            v_low[k, rows_of(b), :] = speed
        else:
            v_high[k, rows_of(b), :] = speed

    momentum(
        every, values, lambda b: b < BLOCKS - 1, speeds, east_lim, north_lim,
        run, u_sum, v_sum, q_col, keep_u, keep_v, lambda k, h, value: None,
        UNROLL_MOM,
    )
    row_sum = [
        jnp.broadcast_to(own_west[8 * h + 5 : 8 * h + 6, :], (8, 128)) for h in range(2)
    ]

    def keep(b, tiles, side):
        for h in range(2):
            force_out[rows_of(b), lanes_of(h)] = tiles[h]
        sides[rows_of(b), :] = side

    forcing(every, u_sum, v_sum, row_sum, south_lim, q_col, count, rain, keep)


def middle(*args):
    plane = pltpu.VMEM((ROWS, COLS), F32)
    strip = pltpu.VMEM((ROWS, 128), F32)
    half = shape(LEVELS, ROWS, 128)
    return pl.pallas_call(
        middle_kernel,
        out_shape=(
            shape(LEVELS, ROWS - 16, COLS), shape(LEVELS, ROWS, COLS), half, half,
            shape(ROWS, COLS), shape(ROWS, 128), shape(ROWS, 128),
        ),
        in_specs=[VMEM] * 14,
        out_specs=(VMEM,) * 7,
        scratch_shapes=[
            strip, strip, plane, plane, strip, pltpu.VMEM((8, COLS), F32), plane, plane, plane,
        ],
        cost_estimate=pl.CostEstimate(
            flops=30 * LEVELS * ROWS * COLS, bytes_accessed=16 * LEVELS * ROWS * COLS,
            transcendentals=0,
        ),
        compiler_params=params(LIMIT_COLUMNS),
        name="middle",
    )(*args)


EXT = ROWS + 16


def relax(force, count):
    wide = force.shape[1]
    root = jnp.sqrt(count * (1.0 / LEVELS))

    def total(field):
        sideways = pltpu.roll(field, 1, 1) + pltpu.roll(field, wide - 1, 1)
        mixed = field + 0.5 * sideways
        return sideways + (pltpu.roll(mixed, 1, 0) + pltpu.roll(mixed, EXT - 1, 0))

    inverse = 1.0 / (damping + root * total(root))
    force = force * inverse
    share = root * inverse
    update = force * (1.0 / cheb_gamma)
    iterate = update
    omega = 2.0 / cheb_gamma
    for step in range(1, ITERS):
        residual = (force - iterate) + share * total(root * iterate)
        omega = 1.0 / (cheb_gamma - omega / (4.0 * cheb_alpha * cheb_alpha))
        update = omega * residual + (cheb_gamma * omega - 1.0) * update
        iterate = iterate + update
    return iterate


def writer_kernel(
    outside, solved, u_new, v_low, from_east, count, east, force_ext, count_ext,
    temp_out, speeds_out, inner, u_fix, sems,
):
    copies = [
        (outside.at[:, pl.ds(0, 8), :], temp_out.at[:, pl.ds(0, 8), :]),
        (outside.at[:, pl.ds(8, 8), :], temp_out.at[:, pl.ds(ROWS - 8, 8), :]),
        (solved, temp_out.at[:, pl.ds(8, ROWS - 16), :]),
        (u_new.at[:, pl.ds(0, ROWS - 8), :], speeds_out.at[0, :, pl.ds(0, ROWS - 8), :]),
        (v_low, speeds_out.at[1, :, :, pl.ds(0, 128)]),
        (u_fix, speeds_out.at[0, :, pl.ds(ROWS - 8, 8), :]),
    ]
    copies = [
        pltpu.make_async_copy(origin, target, sems.at[n])
        for n, (origin, target) in enumerate(copies)
    ]
    for copy in copies[:-1]:
        copy.start()
    last_row = row_id() == 7
    for h in range(2):
        limit = jnp.minimum(
            count[ROWS - 8 :, lanes_of(h)], jnp.broadcast_to(east[h, 40:41, :], (8, 128))
        )
        limit = jnp.where(last_row, limit, 0.0)
        for k in range(LEVELS):
            at = 24 + 40 * h + k
            u_fix[k, :, lanes_of(h)] = u_new[k, ROWS - 8 :, lanes_of(h)] + jnp.where(
                float(k) < limit,
                PRESS * jnp.broadcast_to(from_east[at : at + 1, :], (8, 128)),
                0.0,
            )
    copies[-1].start()
    inner[...] = relax(force_ext[...], count_ext[...])[8 : 8 + ROWS]
    for copy in copies:
        copy.wait()


def writer(*args):
    return pl.pallas_call(
        writer_kernel,
        out_shape=(
            shape(LEVELS, ROWS, COLS), shape(2, LEVELS, ROWS, COLS), shape(ROWS, COLS)
        ),
        in_specs=[VMEM] * 9,
        out_specs=(ANY, ANY, VMEM),
        scratch_shapes=[
            pltpu.VMEM((LEVELS, 8, COLS), F32),
            pltpu.SemaphoreType.DMA((6,)),
        ],
        cost_estimate=pl.CostEstimate(
            flops=LEVELS * ROWS * COLS, bytes_accessed=12 * LEVELS * ROWS * COLS,
            transcendentals=0,
        ),
        compiler_params=params(LIMIT_COLUMNS),
        name="writer",
    )(*args)


def edges_kernel(
    force, sides, q_col, count, west, east_in, own_east, own_west, x_odd, x_even,
    force_ext, count_ext, sides_ext, y_odd, y_even, from_east, from_west, to_north, to_south,
):
    from_west[...], from_east[...] = sort_in("gx", x_even[...], x_odd[...])
    zeros8 = jnp.zeros((8, COLS), F32)
    count_ext[0:8, :] = zeros8
    for h in range(2):
        count_ext[2:8, lanes_of(h)] = west[h, 80:86, :]
    count_ext[8 : 8 + ROWS, :] = count[...]
    count_ext[8 + ROWS :, :] = zeros8
    for h in range(2):
        count_ext[8 + ROWS : 14 + ROWS, lanes_of(h)] = east_in[h, 40:46, :]
    sides_ext[0:8, :] = jnp.zeros((8, 128), F32)
    sides_ext[3:8, :] = from_west[16:21, :]
    sides_ext[8 : 8 + ROWS, :] = sides[...]
    sides_ext[8 + ROWS :, :] = jnp.zeros((8, 128), F32)
    sides_ext[8 + ROWS : 13 + ROWS, :] = from_east[16:21, :]
    force_ext[0:8, :] = zeros8
    for h in range(2):
        force_ext[3:8, lanes_of(h)] = from_west[8 * h : 8 * h + 5, :]
    force_ext[8 : 8 + ROWS, :] = force[...]
    force_ext[8 + ROWS :, :] = zeros8
    for h in range(2):
        force_ext[8 + ROWS : 13 + ROWS, lanes_of(h)] = from_east[8 * h : 8 * h + 5, :]

    def add(at, sign, ref):
        for h in range(2):
            place = (slice(at, at + 1), lanes_of(h))
            force_ext[place] = force_ext[place] + jnp.where(
                count_ext[place] > 0.0, sign * DIVERGE * ref[8 * h + 5 : 8 * h + 6, :], 0.0
            )

    add(7, -1.0, own_west)
    add(8, 1.0, from_west)
    add(7 + ROWS, -1.0, from_east)
    add(8 + ROWS, 1.0, own_east)
    lane = lane_id(EXT)
    side = sides_ext[...]
    to_north[...] = jnp.where(
        lane >= 123,
        force_ext[:, 128:],
        jnp.where(lane == 0, side, pltpu.roll(count_ext[:, 128:], 122, 1)),
    )
    to_south[...] = jnp.where(
        lane < 5,
        force_ext[:, :128],
        jnp.where(lane == 127, side, pltpu.roll(count_ext[:, :128], 8, 1)),
    )
    lane = lane_id(ROWS)
    to_south[8 : 8 + ROWS, :] = jnp.where(
        (lane >= 64) & (lane < 64 + LEVELS),
        pltpu.roll(q_col[...], 64, 1),
        to_south[8 : 8 + ROWS, :],
    )
    y_even[...], y_odd[...] = sort_out("gy", to_south[...], to_north[...])


def edges(*args):
    return pl.pallas_call(
        edges_kernel,
        out_shape=(
            shape(EXT, COLS), shape(EXT, COLS), shape(EXT, 128), shape(EXT, 128), shape(EXT, 128),
            shape(104, 128),
        ),
        in_specs=[VMEM] * 10,
        out_specs=(VMEM,) * 6,
        scratch_shapes=[
            pltpu.VMEM((104, 128), F32), pltpu.VMEM((EXT, 128), F32), pltpu.VMEM((EXT, 128), F32)
        ],
        compiler_params=params(LIMIT_COLUMNS),
        name="edges",
    )(*args)


def final_kernel(
    speeds, v_high, count, inner, force_ext, count_ext, sides_ext, y_odd, y_even,
    speeds_out, out, v_fix, south, north, sems,
):
    south[...], north[...] = sort_in("gy", y_even[...], y_odd[...])
    last_lane = lane_id(8) == 127
    limits = []
    for b in range(BLOCKS):
        limit = jnp.minimum(
            count[rows_of(b), 128:], pltpu.roll(north[rows_of(b + 1), :], 127 - 8, 1)
        )
        limits.append(jnp.where(last_lane, limit, 0.0))

    def save(c):
        part = pl.ds(c * FIX_CHUNK, FIX_CHUNK)
        return pltpu.make_async_copy(
            v_fix.at[part], speeds_out.at[1, part, :, pl.ds(128, 128)], sems.at[c]
        )

    for c in range(LEVELS // FIX_CHUNK):
        for k in range(c * FIX_CHUNK, (c + 1) * FIX_CHUNK):
            for b in range(BLOCKS):
                rows = rows_of(b)
                v_fix[k, rows, :] = v_high[k, rows, :] + jnp.where(
                    float(k) < limits[b],
                    PRESS * pltpu.roll(north[rows_of(b + 1), :], 63 - k, 1),
                    0.0,
                )
        save(c).start()

    @pl.when(lax.axis_index("gx") >= 0)
    def _():
        lane = lane_id(EXT)
        count_side = jnp.where(
            lane >= 122,
            pltpu.roll(south[...], 6, 1),
            jnp.where(lane < 6, pltpu.roll(north[...], 120, 1), 0.0),
        )
        force_side = jnp.where(
            lane >= 123, south[...], jnp.where(lane < 5, north[...], 0.0)
        )
        side = sides_ext[...]
        low, high = force_ext[:, :128], force_ext[:, 128:]
        low = low + jnp.where(
            (lane == 0) & (count_ext[:, :128] > 0.0), DIVERGE * south[...], 0.0
        )
        high = high - jnp.where(
            (lane == 127) & (count_ext[:, 128:] > 0.0), DIVERGE * north[...], 0.0
        )
        force_side = force_side + jnp.where(
            (lane == 0) & (count_side > 0.0), DIVERGE * side, 0.0
        )
        force_side = force_side - jnp.where(
            (lane == 127) & (count_side > 0.0), DIVERGE * side, 0.0
        )
        left = (lane < 32) | (lane >= 96)

        def strip(low, high, side):
            return jnp.where(
                left,
                jnp.where(lane < 64, low, side),
                pltpu.roll(jnp.where(lane >= 64, high, side), 64, 1),
            )

        near = relax(
            strip(low, high, force_side), strip(count_ext[:, :128], count_ext[:, 128:], count_side)
        )[8 : 8 + ROWS]
        lane = lane_id(ROWS)
        out[:, :128] = jnp.where(lane < 6, near, inner[:, :128])
        out[:, 128:] = jnp.where(lane >= 122, pltpu.roll(near, 64, 1), inner[:, 128:])
    for c in range(LEVELS // FIX_CHUNK):
        save(c).wait()


def final(*args):
    return pl.pallas_call(
        final_kernel,
        out_shape=(shape(2, LEVELS, ROWS, COLS), shape(ROWS, COLS)),
        in_specs=[ANY] + [VMEM] * 8,
        out_specs=(ANY, VMEM),
        scratch_shapes=[
            pltpu.VMEM((LEVELS, ROWS, 128), F32),
            pltpu.VMEM((EXT, 128), F32), pltpu.VMEM((EXT, 128), F32),
            pltpu.SemaphoreType.DMA((LEVELS // FIX_CHUNK,)),
        ],
        input_output_aliases={0: 0},
        compiler_params=params(LIMIT_COLUMNS),
        name="final",
    )(*args)


def swap(array, axis, first):
    count = lax.axis_size(axis)
    pairs = []
    for low in range(first, count + first, 2):
        low, high = low % count, (low + 1) % count
        pairs += [(low, high), (high, low)]
    return lax.ppermute(array, axis, pairs)


def local(
    thermal_departure,
    current_speeds,
    mixing_coefficient,
    seawater_indicator,
    submerged_layer_tally,
    rainfall_runoff_input,
):
    near, count, to_east, to_west, to_north, to_south, y_odd, y_even, x_odd, x_even = pack(
        *(
            pltpu.with_memory_space_constraint(x, pltpu.HBM)
            for x in (
                thermal_departure, current_speeds, seawater_indicator, submerged_layer_tally
            )
        )
    )
    y_odd = swap(y_odd, "gy", 1)
    y_even = swap(y_even, "gy", 0)
    x_odd = swap(x_odd, "gx", 1)
    x_even = swap(x_even, "gx", 0)
    speeds, mixing = (
        pltpu.with_memory_space_constraint(x, pltpu.VMEM)
        for x in (current_speeds, mixing_coefficient)
    )
    inside = (*interior(near, speeds, mixing, count), speeds)
    outside, own_east, own_west, x_odd, x_even, west, east, south, north = outer(
        *inside, count, rainfall_runoff_input, to_east, to_west, to_north, to_south,
        y_odd, y_even, x_odd, x_even,
    )
    x_odd = swap(x_odd, "gx", 1)
    x_even = swap(x_even, "gx", 0)
    solved, u_new, v_low, v_high, force, q_col, sides = middle(
        *inside, count, rainfall_runoff_input, to_north, to_south,
        west, east, south, north, outside, own_west,
    )
    force_ext, count_ext, sides_ext, y_odd, y_even, from_east = edges(
        force, sides, q_col, count, west, east, own_east, own_west, x_odd, x_even
    )
    y_odd = swap(y_odd, "gy", 1)
    y_even = swap(y_even, "gy", 0)
    temp_next, stored, inner = writer(
        outside, solved, u_new, v_low, from_east, count, east, force_ext, count_ext
    )
    velocity_next, surface = final(
        stored, v_high, count, inner, force_ext, count_ext, sides_ext, y_odd, y_even,
    )
    return (temp_next, velocity_next, surface)


def solution(mesh):
    placed = (
        P(None, "gx", "gy"),
        P(None, None, "gx", "gy"),
        P(None, "gx", "gy"),
        P("gx", "gy"),
        P("gx", "gy"),
        P("gx", "gy"),
    )
    return jax.shard_map(
        local,
        mesh=mesh,
        in_specs=placed,
        out_specs=(P(None, "gx", "gy"), P(None, None, "gx", "gy"), P("gx", "gy")),
        check_vma=False,
    )
```
